256 devices in a mesh: rows: 32 (over x, z), cols: 8 (over y, core).
Axes of the slice: x: 4, y: 4, z: 8, core: 2. Of those that a mesh axis runs over, the one named last changes fastest.
Arguments:
- vectors: bfloat16 [65536, 768], P('rows'), may hold values from -24 to 24
- centroids: bfloat16 [8192, 768], P('cols'), may hold values from -0.2 to 0.2
Outputs:
- new_centroids: float32 [8192, 768], P('cols')
- row_potential: float32 [65536], P('rows')
- col_potential: float32 [8192], P('cols')
The draws below stay inside these ranges and needn't reach their ends.
All inputs are finite; a program needn't handle non-finite values.
Results may differ from the reference program's by a relative error of at most 0.0023.
Values sent between devices are 32-bit elements; how exact they have to be, the bound alone decides.
No kernel may reach another device: no remote copies, remote signals or barrier semaphores. Data moves between devices by JAX's collectives and lax.ppermute only.
A program may use at most 64 MiB of HBM per device.

```python
import math
import jax
import jax.numpy as jnp
from jax import lax

D = 768
K = 8192
ROWS_DEV = 2048
ITERS = 3
NV = 65536


def shared_pattern(key):
    pattern_key = jax.random.fold_in(key, 5)
    second = jax.random.fold_in(pattern_key, 1)
    block = K // 32
    offsets = jax.random.randint(second, (32,), 0, block, dtype=jnp.int32)
    picked = jnp.arange(32, dtype=jnp.int32) * block + offsets
    return picked


def centroid_table(key):
    base = jax.random.normal(key, (K, D), jnp.float32) * D ** (-0.5)
    base = jnp.clip(base, -0.19921875, 0.19921875)
    picked = shared_pattern(key)
    replaced = base[picked]
    return base.at[picked].set(replaced)


def draw_centroids(key, part):
    cent = centroid_table(key)
    return cent.astype(jnp.bfloat16)


def draw_vectors(key, part):
    key = jax.random.fold_in(key, 23)
    second = jax.random.fold_in(key, 1)
    base = jax.random.normal(second, (NV, D), jnp.float32)
    return jnp.clip(base, -24.0, 24.0).astype(jnp.bfloat16)


def setup_inputs(seed: int = 0) -> dict:
    key_of = jax.random.split(jax.random.key(seed), 3)
    return {
        "vectors": draw_vectors(jax.random.fold_in(key_of[2], 71), 0),
        "centroids": draw_centroids(jax.random.fold_in(key_of[2], 71), 0),
    }


def row_lse(z):
    top = jnp.max(z, axis=1)
    return top + jnp.log(jnp.sum(jnp.exp(z - top[:, None]), axis=1))


def reference(vectors, centroids):
    blocks = vectors.reshape(NV // ROWS_DEV, ROWS_DEV, D)
    cent = centroids.astype(jnp.float32)
    log_target = math.log(NV / K)

    def logits_of(block):
        return 4.0 * jnp.dot(block.astype(jnp.float32), cent.T, precision=lax.Precision.HIGHEST)

    def sweep(col_pot):
        def step(carry, block):
            col_top, col_sum = carry
            logits = logits_of(block)
            row_pot = -row_lse(logits + col_pot[None, :])
            shifted = logits + row_pot[:, None]
            new_top = jnp.maximum(col_top, jnp.max(shifted, axis=0))
            col_sum = col_sum * jnp.exp(col_top - new_top) + jnp.sum(jnp.exp(shifted - new_top[None, :]), axis=0)
            return (new_top, col_sum), row_pot
        init = (jnp.full((K,), -1e30, jnp.float32), jnp.zeros((K,), jnp.float32))
        (col_top, col_sum), row_pot = lax.scan(step, init, blocks)
        return row_pot, log_target - (col_top + jnp.log(col_sum))

    col_pot = jnp.zeros((K,), jnp.float32)
    for it in range(ITERS):
        row_pot, col_pot = sweep(col_pot)

    def final(carry, block):
        weighted, mass = carry
        logits = logits_of(block)
        row_pot = -row_lse(logits + col_pot[None, :])
        plan = jnp.exp(logits + row_pot[:, None] + col_pot[None, :])
        mass = mass + jnp.sum(plan, axis=0)
        plan_b = plan.astype(jnp.bfloat16)
        weighted = weighted + jnp.dot(plan_b.T, block, preferred_element_type=jnp.float32)
        return (weighted, mass), row_pot

    init = (jnp.zeros((K, D), jnp.float32), jnp.zeros((K,), jnp.float32))
    (weighted, mass), row_pot = lax.scan(final, init, blocks)
    new_centroids = weighted / mass[:, None]
    return new_centroids, row_pot.reshape(NV), col_pot
```

```python
import functools
import math

import jax
import jax.numpy as jnp
from jax import lax
from jax.experimental import pallas as pl
from jax.experimental.pallas import tpu as pltpu
from jax.sharding import PartitionSpec as P

ITERS = 3
LANES = 128
LIM = 40.0
VMEM_LIMIT = 48 * 1024 * 1024
F32 = jnp.float32


def combine_lse(parts):
    top = jnp.max(parts, axis=0)
    return top + jnp.log(jnp.sum(jnp.exp(parts - top[None]), axis=0))


def lane_to_sublane(row):
    return jnp.transpose(jnp.broadcast_to(row, (LANES, LANES)))


def fold(x):
    return jnp.sum(x.reshape(x.shape[0] // 8, 8, x.shape[1]), axis=0)


def lane_group(g):
    return slice(g * LANES, (g + 1) * LANES)


def row_tile(t):
    return pl.ds(pl.multiple_of(t * LANES, LANES), LANES)


def put_copies(out_ref, value):
    for k in range(out_ref.shape[0]):
        out_ref[k] = value


def logit_block(k_ref, ok, t, g):
    block = k_ref[row_tile(t), lane_group(g)]
    return jnp.where(ok != 0, jnp.log(block), block)


def row_lse_exact(k_ref, ok, pot_ref, out_ref):
    tiles, groups = k_ref.shape[0] // LANES, k_ref.shape[1] // LANES

    def shifted(t, g):
        z = logit_block(k_ref, ok, t, g)
        return z if pot_ref is None else z + lane_to_sublane(pot_ref[pl.ds(t, 1), :])

    for g in range(groups):
        def top_of(t, top, g=g):
            return jnp.maximum(top, jnp.max(shifted(t, g), axis=0, keepdims=True))

        top = lax.fori_loop(0, tiles, top_of, jnp.full((1, LANES), -3.0e38, F32))

        def sum_of(t, total, g=g, top=top):
            return total + jnp.sum(jnp.exp(shifted(t, g) - top), axis=0, keepdims=True)

        total = lax.fori_loop(0, tiles, sum_of, jnp.zeros((1, LANES), F32))
        out_ref[g : g + 1, :] = top + jnp.log(total)


def col_lse_exact(k_ref, ok, pot, out_ref):
    tiles, groups = k_ref.shape[0] // LANES, k_ref.shape[1] // LANES

    def tile(t, carry):
        top = jnp.full((LANES, LANES), -3.0e38, F32)
        for g in range(groups):
            top = jnp.maximum(top, logit_block(k_ref, ok, t, g) + pot[g : g + 1, :])
        top = jnp.broadcast_to(jnp.max(top, axis=1, keepdims=True), (LANES, LANES))
        total = jnp.zeros((LANES, LANES), F32)
        for g in range(groups):
            total = total + jnp.exp(logit_block(k_ref, ok, t, g) + pot[g : g + 1, :] - top)
        total = jnp.sum(jnp.transpose(total), axis=0, keepdims=True)
        out_ref[pl.ds(t, 1), :] = jnp.transpose(top)[0:1, :] + jnp.log(total)
        return carry

    lax.fori_loop(0, tiles, tile, 0)


def logits_kernel(cent_ref, vec_ref, k_ref, ok_ref, out_ref, lse_ref):
    cents, rows = k_ref.shape
    groups = rows // LANES
    step = 256

    def logits(t):
        return 4.0 * lax.dot_general(
            cent_ref[t * step : (t + 1) * step, :], vec_ref[...],
            (((1,), (1,)), ((), ())), preferred_element_type=F32,
        )

    sums = [jnp.zeros((8, LANES), F32)] * groups
    peak = jnp.zeros((8, LANES), F32)
    for t in range(cents // step):
        block = logits(t)
        for g in range(groups):
            part = block[:, lane_group(g)]
            size = jnp.abs(part)
            peak = jnp.maximum(peak, jnp.max(size.reshape(step // 8, 8, LANES), axis=0))
            part = jnp.exp(part)
            k_ref[t * step : (t + 1) * step, lane_group(g)] = part
            sums[g] = sums[g] + fold(part)
    for g in range(groups):
        lse_ref[g : g + 1, :] = jnp.log(jnp.sum(sums[g], axis=0, keepdims=True))
    ok = jnp.max(peak) <= LIM
    ok_ref[0, 0] = ok.astype(jnp.int32)

    @pl.when(jnp.logical_not(ok))
    def _():
        def tile(t, carry):
            at = pl.ds(pl.multiple_of(t * LANES, LANES), LANES)
            for g in range(groups):
                k_ref[at, lane_group(g)] = 4.0 * lax.dot_general(
                    cent_ref[at, :], vec_ref[lane_group(g), :],
                    (((1,), (1,)), ((), ())), preferred_element_type=F32,
                )
            return carry

        lax.fori_loop(0, cents // LANES, tile, 0)
        row_lse_exact(k_ref, 0, None, lse_ref)

    put_copies(out_ref, lse_ref[...])


def row_kernel(log_target, got_ref, ok_ref, k_ref, out_ref, pot_ref, lse_ref):
    tiles, groups = k_ref.shape[0] // LANES, k_ref.shape[1] // LANES
    pot = log_target - combine_lse(got_ref[...])
    ok = ok_ref[0, 0]
    fast = jnp.logical_and(ok != 0, jnp.max(jnp.abs(pot)) <= LIM)

    @pl.when(fast)
    def _():
        pot_ref[...] = jnp.exp(pot)

        def tile(t, sums):
            scale = lane_to_sublane(pot_ref[pl.ds(t, 1), :])
            return tuple(
                sums[g] + fold(k_ref[row_tile(t), lane_group(g)] * scale) for g in range(groups)
            )

        sums = lax.fori_loop(0, tiles, tile, (jnp.zeros((8, LANES), F32),) * groups)
        for g in range(groups):
            lse_ref[g : g + 1, :] = jnp.sum(sums[g], axis=0, keepdims=True)
        lse_ref[...] = jnp.log(lse_ref[...])

    @pl.when(jnp.logical_not(fast))
    def _():
        pot_ref[...] = pot
        row_lse_exact(k_ref, ok, pot_ref, lse_ref)

    put_copies(out_ref, lse_ref[...])


def col_kernel(got_ref, ok_ref, k_ref, out_ref, lse_ref):
    tiles, groups = k_ref.shape[0] // LANES, k_ref.shape[1] // LANES
    pot = -combine_lse(got_ref[...])
    ok = ok_ref[0, 0]
    fast = jnp.logical_and(ok != 0, jnp.max(jnp.abs(pot)) <= LIM)

    @pl.when(fast)
    def _():
        scale = jnp.exp(pot)

        def tile(t, carry):
            total = jnp.zeros((LANES, LANES), F32)
            for g in range(groups):
                total = total + k_ref[row_tile(t), lane_group(g)] * scale[g : g + 1, :]
            lse_ref[pl.ds(t, 1), :] = jnp.sum(jnp.transpose(total), axis=0, keepdims=True)
            return carry

        lax.fori_loop(0, tiles, tile, 0)
        lse_ref[...] = jnp.log(lse_ref[...])

    @pl.when(jnp.logical_not(fast))
    def _():
        col_lse_exact(k_ref, ok, pot, lse_ref)

    put_copies(out_ref, lse_ref[...])


def final_kernel(
    log_target, cols_ref, rows_ref, ok_ref, k_ref, vec_ref,
    weighted_ref, mass_ref, row_pot_ref, col_pot_ref, scale_ref, plan_ref,
):
    tiles, groups = k_ref.shape[0] // LANES, k_ref.shape[1] // LANES
    col_pot = log_target - combine_lse(cols_ref[...])
    row_pot = -combine_lse(rows_ref[...])
    col_pot_ref[...] = col_pot
    row_pot_ref[...] = row_pot
    ok = ok_ref[0, 0]
    fast = jnp.logical_and(
        ok != 0, jnp.maximum(jnp.max(jnp.abs(col_pot)), jnp.max(jnp.abs(row_pot))) <= LIM
    )

    def plan_tile(t, block):
        total = jnp.zeros((LANES, LANES), F32)
        for g in range(groups):
            plan = block(g)
            total = total + plan
            plan_ref[row_tile(t), lane_group(g)] = plan.astype(jnp.bfloat16)
        mass_ref[pl.ds(t, 1), :] = jnp.sum(jnp.transpose(total), axis=0, keepdims=True)

    @pl.when(fast)
    def _():
        scale_ref[...] = jnp.exp(col_pot)
        row_scale = jnp.exp(row_pot)

        def tile(t, carry):
            scale = lane_to_sublane(scale_ref[pl.ds(t, 1), :])
            plan_tile(
                t, lambda g: k_ref[row_tile(t), lane_group(g)] * row_scale[g : g + 1, :] * scale
            )
            return carry

        lax.fori_loop(0, tiles, tile, 0)

    @pl.when(jnp.logical_not(fast))
    def _():
        scale_ref[...] = col_pot

        def tile(t, carry):
            shift = lane_to_sublane(scale_ref[pl.ds(t, 1), :])
            plan_tile(
                t, lambda g: jnp.exp(logit_block(k_ref, ok, t, g) + row_pot[g : g + 1, :] + shift)
            )
            return carry

        lax.fori_loop(0, tiles, tile, 0)

    step = 256
    for t in range(k_ref.shape[0] // step):
        at = slice(t * step, (t + 1) * step)
        weighted_ref[at, :] = jnp.dot(plan_ref[at, :], vec_ref[...], preferred_element_type=F32)


def vmem():
    return pl.BlockSpec(memory_space=pltpu.VMEM)


def smem():
    return pl.BlockSpec(memory_space=pltpu.SMEM)


def params():
    return pltpu.CompilerParams(vmem_limit_bytes=VMEM_LIMIT)


def per_device(vectors, centroids):
    n_rows, n_cols = lax.axis_size("rows"), lax.axis_size("cols")
    rows, width = vectors.shape
    cents = centroids.shape[0]
    log_target = math.log(rows * n_rows / (cents * n_cols))
    groups, tiles = rows // LANES, cents // LANES
    kept = jax.ShapeDtypeStruct((cents, rows), F32)
    ok_type = jax.ShapeDtypeStruct((1, 1), jnp.int32)
    row_parts = jax.ShapeDtypeStruct((n_cols, groups, LANES), F32)
    col_parts = jax.ShapeDtypeStruct((n_rows, tiles, LANES), F32)
    row_scratch = pltpu.VMEM((groups, LANES), F32)
    col_scratch = pltpu.VMEM((tiles, LANES), F32)

    kernel, ok, part = pl.pallas_call(
        logits_kernel,
        out_shape=(kept, ok_type, row_parts),
        in_specs=[vmem(), vmem()],
        out_specs=(vmem(), smem(), vmem()),
        scratch_shapes=[row_scratch],
        compiler_params=params(),
        name="logits",
    )(centroids, vectors)

    for step in range(ITERS):
        row_got = lax.all_to_all(part, "cols", 0, 0, tiled=True)
        part = pl.pallas_call(
            col_kernel,
            out_shape=col_parts,
            in_specs=[vmem(), smem(), vmem()],
            out_specs=vmem(),
            scratch_shapes=[col_scratch],
            compiler_params=params(),
            name="col_step",
        )(row_got, ok, kernel)
        col_got = lax.all_to_all(part, "rows", 0, 0, tiled=True)
        part = pl.pallas_call(
            functools.partial(row_kernel, log_target),
            out_shape=row_parts,
            in_specs=[vmem(), smem(), vmem()],
            out_specs=vmem(),
            scratch_shapes=[col_scratch, row_scratch],
            compiler_params=params(),
            name="row_step",
        )(col_got, ok, kernel)
    row_got = lax.all_to_all(part, "cols", 0, 0, tiled=True)

    weighted, mass, row_pot, col_pot = pl.pallas_call(
        functools.partial(final_kernel, log_target),
        out_shape=(
            jax.ShapeDtypeStruct((cents, width), F32),
            jax.ShapeDtypeStruct((tiles, LANES), F32),
            jax.ShapeDtypeStruct((groups, LANES), F32),
            jax.ShapeDtypeStruct((tiles, LANES), F32),
        ),
        in_specs=[vmem(), vmem(), smem(), vmem(), vmem()],
        out_specs=(vmem(), vmem(), vmem(), vmem()),
        scratch_shapes=[col_scratch, pltpu.VMEM((cents, rows), jnp.bfloat16)],
        compiler_params=params(),
        name="weighted_sums",
    )(col_got, row_got, ok, kernel, vectors)

    masses = lax.all_to_all(
        jnp.broadcast_to(mass[None], (n_rows, tiles, LANES)), "rows", 0, 0, tiled=True
    )
    full_mass = jnp.sum(masses, axis=0).reshape(cents)
    full_sum = lax.psum(weighted, "rows")
    new_centroids = full_sum / full_mass[:, None]
    return (new_centroids, row_pot.reshape(rows), col_pot.reshape(cents))


def solution(mesh):
    return jax.shard_map(
        per_device,
        mesh=mesh,
        in_specs=(P("rows", None), P("cols", None)),
        out_specs=(P("cols", None), P("rows"), P("cols")),
        check_vma=False,
    )
```

```python
import functools
import math

import jax
import jax.numpy as jnp
from jax import lax
from jax.experimental import pallas as pl
from jax.experimental.pallas import tpu as pltpu
from jax.sharding import PartitionSpec as P

ITERS = 3
LANES = 128
LIM = 40.0
VMEM_LIMIT = 32 * 1024 * 1024
F32 = jnp.float32
XS, ZS = 4, 8
BLOCK = 32
PARTS = BLOCK // 8
XB1, XB2, ZB1, ZB2 = range(4)


def combine_lse(parts):
    top = jnp.max(parts, axis=0)
    return top + jnp.log(jnp.sum(jnp.exp(parts - top[None]), axis=0))


def lane_to_sublane(row):
    return jnp.transpose(jnp.broadcast_to(row, (LANES, LANES)))


def fold(x):
    return jnp.sum(x.reshape(x.shape[0] // 8, 8, x.shape[1]), axis=0)


def lane_group(g):
    return slice(g * LANES, (g + 1) * LANES)


def row_tile(t):
    return pl.ds(pl.multiple_of(t * LANES, LANES), LANES)


def put_copies(out_ref, value):
    for k in range(out_ref.shape[0]):
        out_ref[k] = value


def logit_block(k_ref, ok, t, g):
    block = k_ref[row_tile(t), lane_group(g)]
    return jnp.where(ok != 0, jnp.log(block), block)


def row_lse_exact(k_ref, ok, pot_ref, out_ref):
    tiles, groups = k_ref.shape[0] // LANES, k_ref.shape[1] // LANES

    def shifted(t, g):
        z = logit_block(k_ref, ok, t, g)
        return z if pot_ref is None else z + lane_to_sublane(pot_ref[pl.ds(t, 1), :])

    for g in range(groups):
        def top_of(t, top, g=g):
            return jnp.maximum(top, jnp.max(shifted(t, g), axis=0, keepdims=True))

        top = lax.fori_loop(0, tiles, top_of, jnp.full((1, LANES), -3.0e38, F32))

        def sum_of(t, total, g=g, top=top):
            return total + jnp.sum(jnp.exp(shifted(t, g) - top), axis=0, keepdims=True)

        total = lax.fori_loop(0, tiles, sum_of, jnp.zeros((1, LANES), F32))
        out_ref[g : g + 1, :] = top + jnp.log(total)


def col_lse_exact(k_ref, ok, pot, out_ref):
    tiles, groups = k_ref.shape[0] // LANES, k_ref.shape[1] // LANES

    def tile(t, carry):
        top = jnp.full((LANES, LANES), -3.0e38, F32)
        for g in range(groups):
            top = jnp.maximum(top, logit_block(k_ref, ok, t, g) + pot[g : g + 1, :])
        top = jnp.broadcast_to(jnp.max(top, axis=1, keepdims=True), (LANES, LANES))
        total = jnp.zeros((LANES, LANES), F32)
        for g in range(groups):
            total = total + jnp.exp(logit_block(k_ref, ok, t, g) + pot[g : g + 1, :] - top)
        total = jnp.sum(jnp.transpose(total), axis=0, keepdims=True)
        out_ref[pl.ds(t, 1), :] = jnp.transpose(top)[0:1, :] + jnp.log(total)
        return carry

    lax.fori_loop(0, tiles, tile, 0)


def logits_kernel(cent_ref, vec_ref, k_ref, ok_ref, out_ref, lse_ref):
    cents, rows = k_ref.shape
    groups = rows // LANES
    step = 256

    def logits(t):
        return 4.0 * lax.dot_general(
            cent_ref[t * step : (t + 1) * step, :], vec_ref[...],
            (((1,), (1,)), ((), ())), preferred_element_type=F32,
        )

    sums = [jnp.zeros((8, LANES), F32)] * groups
    peak = jnp.zeros((8, LANES), F32)
    for t in range(cents // step):
        block = logits(t)
        for g in range(groups):
            part = block[:, lane_group(g)]
            size = jnp.abs(part)
            peak = jnp.maximum(peak, jnp.max(size.reshape(step // 8, 8, LANES), axis=0))
            part = jnp.exp(part)
            k_ref[t * step : (t + 1) * step, lane_group(g)] = part
            sums[g] = sums[g] + fold(part)
    for g in range(groups):
        lse_ref[g : g + 1, :] = jnp.log(jnp.sum(sums[g], axis=0, keepdims=True))
    ok = jnp.max(peak) <= LIM
    ok_ref[0, 0] = ok.astype(jnp.int32)

    @pl.when(jnp.logical_not(ok))
    def _():
        def tile(t, carry):
            at = pl.ds(pl.multiple_of(t * LANES, LANES), LANES)
            for g in range(groups):
                k_ref[at, lane_group(g)] = 4.0 * lax.dot_general(
                    cent_ref[at, :], vec_ref[lane_group(g), :],
                    (((1,), (1,)), ((), ())), preferred_element_type=F32,
                )
            return carry

        lax.fori_loop(0, cents // LANES, tile, 0)
        row_lse_exact(k_ref, 0, None, lse_ref)

    put_copies(out_ref, lse_ref[...])


def row_kernel(log_target, got_ref, ok_ref, k_ref, out_ref, pot_ref, lse_ref):
    tiles, groups = k_ref.shape[0] // LANES, k_ref.shape[1] // LANES
    pot = log_target - combine_lse(got_ref[...])
    ok = ok_ref[0, 0]
    fast = jnp.logical_and(ok != 0, jnp.max(jnp.abs(pot)) <= LIM)

    @pl.when(fast)
    def _():
        pot_ref[...] = jnp.exp(pot)

        def tile(t, sums):
            scale = lane_to_sublane(pot_ref[pl.ds(t, 1), :])
            return tuple(
                sums[g] + fold(k_ref[row_tile(t), lane_group(g)] * scale) for g in range(groups)
            )

        sums = lax.fori_loop(0, tiles, tile, (jnp.zeros((8, LANES), F32),) * groups)
        for g in range(groups):
            lse_ref[g : g + 1, :] = jnp.sum(sums[g], axis=0, keepdims=True)
        lse_ref[...] = jnp.log(lse_ref[...])

    @pl.when(jnp.logical_not(fast))
    def _():
        pot_ref[...] = pot
        row_lse_exact(k_ref, ok, pot_ref, lse_ref)

    put_copies(out_ref, lse_ref[...])


def col_kernel(got_ref, ok_ref, k_ref, out_ref, lse_ref):
    tiles, groups = k_ref.shape[0] // LANES, k_ref.shape[1] // LANES
    pot = -combine_lse(got_ref[...])
    ok = ok_ref[0, 0]
    fast = jnp.logical_and(ok != 0, jnp.max(jnp.abs(pot)) <= LIM)

    @pl.when(fast)
    def _():
        scale = jnp.exp(pot)

        def tile(t, carry):
            total = jnp.zeros((LANES, LANES), F32)
            for g in range(groups):
                total = total + k_ref[row_tile(t), lane_group(g)] * scale[g : g + 1, :]
            lse_ref[pl.ds(t, 1), :] = jnp.sum(jnp.transpose(total), axis=0, keepdims=True)
            return carry

        lax.fori_loop(0, tiles, tile, 0)
        lse_ref[...] = jnp.log(lse_ref[...])

    @pl.when(jnp.logical_not(fast))
    def _():
        col_lse_exact(k_ref, ok, pot, lse_ref)

    put_copies(out_ref, lse_ref[...])


def plan_kernel(
    log_target, bits_ref, cols_ref, rows_ref, ok_ref, k_ref, vec_ref,
    send_a_ref, send_b_ref, plan_ref, mass_ref, row_pot_ref, col_pot_ref, scale_ref,
):
    tiles, groups = k_ref.shape[0] // LANES, k_ref.shape[1] // LANES
    col_pot = log_target - combine_lse(cols_ref[...])
    row_pot = -combine_lse(rows_ref[...])
    col_pot_ref[...] = col_pot
    row_pot_ref[...] = row_pot
    ok = ok_ref[0, 0]
    fast = jnp.logical_and(
        ok != 0, jnp.maximum(jnp.max(jnp.abs(col_pot)), jnp.max(jnp.abs(row_pot))) <= LIM
    )

    def plan_tile(t, block):
        total = jnp.zeros((LANES, LANES), F32)
        for g in range(groups):
            plan = block(g)
            total = total + plan
            plan_ref[row_tile(t), lane_group(g)] = plan.astype(jnp.bfloat16)
        mass = jnp.broadcast_to(jnp.sum(total, axis=1, keepdims=True), (LANES, LANES))
        spot = lax.broadcasted_iota(jnp.int32, (8, LANES), 1) // (LANES // PARTS)
        for b in range(LANES // BLOCK):
            unit = mass[b * BLOCK : b * BLOCK + 8, :]
            for k in range(1, PARTS):
                at = b * BLOCK + 8 * k
                unit = jnp.where(spot == k, mass[at : at + 8, :], unit)
            mass_ref[t * (LANES // BLOCK) + b] = unit

    @pl.when(fast)
    def _():
        scale_ref[...] = jnp.exp(col_pot)
        row_scale = jnp.exp(row_pot)

        def tile(t, carry):
            scale = lane_to_sublane(scale_ref[pl.ds(t, 1), :])
            plan_tile(
                t, lambda g: k_ref[row_tile(t), lane_group(g)] * row_scale[g : g + 1, :] * scale
            )
            return carry

        lax.fori_loop(0, tiles, tile, 0)

    @pl.when(jnp.logical_not(fast))
    def _():
        scale_ref[...] = col_pot

        def tile(t, carry):
            shift = lane_to_sublane(scale_ref[pl.ds(t, 1), :])
            plan_tile(
                t, lambda g: jnp.exp(logit_block(k_ref, ok, t, g) + row_pot[g : g + 1, :] + shift)
            )
            return carry

        lax.fori_loop(0, tiles, tile, 0)

    half_sums(1 - bits_ref[XB1], 1 - bits_ref[ZB1], plan_ref, mass_ref, vec_ref, send_a_ref, send_b_ref)


def keep_kernel(bits_ref, plan_ref, mass_ref, vec_ref, keep_a_ref, keep_b_ref):
    half_sums(bits_ref[XB1], bits_ref[ZB1], plan_ref, mass_ref, vec_ref, keep_a_ref, keep_b_ref)


def half_sums(half_a, half_b, plan_ref, mass_ref, vec_ref, a_ref, b_ref):
    blocks = a_ref.shape[0]
    size = blocks * BLOCK
    for chain, (half, out_ref) in enumerate(((half_a, a_ref), (half_b, b_ref))):
        first = chain * 2 * blocks + half * blocks
        at = pl.ds(pl.multiple_of(first * BLOCK, size), size)
        sums = jnp.dot(plan_ref[at, :], vec_ref[...], preferred_element_type=F32)
        for b in range(blocks):
            for k in range(PARTS):
                row = b * BLOCK + 8 * k
                for g in range(sums.shape[1] // LANES):
                    out_ref[b, k * (sums.shape[1] // LANES) + g] = sums[row : row + 8, lane_group(g)]
            out_ref[b, out_ref.shape[1] - 1] = mass_ref[first + b]


def fold_kernel(which, bits_ref, keep_ref, got_ref, send_ref, kept_ref):
    half = send_ref.shape[0]
    mine = bits_ref[which] * half
    other = (1 - bits_ref[which]) * half
    for b in range(half):
        send_ref[b] = keep_ref[other + b] + got_ref[other + b]
        kept_ref[b] = keep_ref[mine + b] + got_ref[mine + b]


def pair_kernel(keep_a_ref, got_a_ref, keep_b_ref, got_b_ref, out_ref):
    out_ref[0] = keep_a_ref[0] + got_a_ref[0]
    out_ref[1] = keep_b_ref[0] + got_b_ref[0]


def mean_kernel(sum_ref, got_ref, a_ref, b_ref):
    units = a_ref.shape[1]
    width = LANES // PARTS
    for chain, out_ref in enumerate((a_ref, b_ref)):
        mass = sum_ref[chain, units] + got_ref[chain, units]
        for k in range(PARTS):
            part = jnp.broadcast_to(mass[:, k * width : k * width + 1], (8, LANES))
            for g in range(units // PARTS):
                u = k * (units // PARTS) + g
                out_ref[0, u] = (sum_ref[chain, u] + got_ref[chain, u]) / part


def join_kernel(which, bits_ref, mine_ref, got_ref, out_ref):
    half = mine_ref.shape[0]
    mine = bits_ref[which] * half
    other = (1 - bits_ref[which]) * half
    for b in range(half):
        out_ref[mine + b] = mine_ref[b]
        out_ref[other + b] = got_ref[b]


def output_kernel(bits_ref, mine_a_ref, got_a_ref, mine_b_ref, got_b_ref, out_ref):
    half, units = mine_a_ref.shape[:2]
    across = units // PARTS
    for chain, (mine_ref, got_ref, bit) in enumerate(
        ((mine_a_ref, got_a_ref, bits_ref[XB1]), (mine_b_ref, got_b_ref, bits_ref[ZB1]))
    ):
        for side, part_ref in ((bit, mine_ref), (1 - bit, got_ref)):
            for b in range(half):
                first = (chain * 2 * half + side * half + b) * BLOCK
                for k in range(PARTS):
                    at = pl.ds(pl.multiple_of(first + 8 * k, 8), 8)
                    for g in range(across):
                        out_ref[at, lane_group(g)] = part_ref[b, k * across + g]


def place(row, core):
    return (row // ZS + (XS - 1) * core) % XS, (row % ZS + (ZS - 1) * core) % ZS


def pairs(partner, n_cols):
    out = []
    for row in range(XS * ZS):
        for col in range(n_cols):
            core = col % 2
            x, z = partner(*place(row, core))
            to = (x + core) % XS * ZS + (z + core) % ZS
            out.append((row * n_cols + col, to * n_cols + col))
    return out


def exchange(x, partner):
    return lax.ppermute(x, ("rows", "cols"), pairs(partner, lax.axis_size("cols")))


def x_first(x, z):
    return x ^ 1, z


def x_second(x, z):
    return XS - 1 - x, z


def z_first(x, z):
    return x, z ^ 1


def z_second(x, z):
    return x, (z - 1 + 2 * (z % 2)) % ZS


def z_third(x, z):
    return x, {0: 3, 3: 0, 1: 6, 6: 1, 2: 5, 5: 2, 4: 7, 7: 4}[z]


def position_bits():
    x, z = place(lax.axis_index("rows"), lax.axis_index("cols") % 2)
    return jnp.stack([(x ^ (x >> 1)) & 1, x >> 1, ((z + 1) >> 1) & 1, (0xB4 >> z) & 1]).astype(jnp.int32)


def halve(which, bits, keep, got):
    half = jax.ShapeDtypeStruct((keep.shape[0] // 2, *keep.shape[1:]), F32)
    return pl.pallas_call(
        functools.partial(fold_kernel, which),
        out_shape=(half, half),
        in_specs=[smem(), vmem(), vmem()],
        out_specs=(vmem(), vmem()),
        compiler_params=params(),
        name="fold",
    )(bits, keep, got)


def join(which, bits, mine, got):
    return pl.pallas_call(
        functools.partial(join_kernel, which),
        out_shape=jax.ShapeDtypeStruct((2 * mine.shape[0], *mine.shape[1:]), F32),
        in_specs=[smem(), vmem(), vmem()],
        out_specs=vmem(),
        compiler_params=params(),
        name="join",
    )(bits, mine, got)


def mean_over_rows(bits, send_a, keep_a, send_b, keep_b, cents, width):
    got_a, got_b = exchange(send_a, x_first), exchange(send_b, z_first)
    send_a, keep_a = halve(XB2, bits, keep_a, got_a)
    send_b, keep_b = halve(ZB2, bits, keep_b, got_b)
    got_a, got_b = exchange(send_a, x_second), exchange(send_b, z_second)
    send_a, keep_a = halve(ZB1, bits, keep_a, got_a)
    send_b, keep_b = halve(XB1, bits, keep_b, got_b)
    got_a, got_b = exchange(send_a, z_first), exchange(send_b, x_first)
    send_a, keep_a = halve(ZB2, bits, keep_a, got_a)
    send_b, keep_b = halve(XB2, bits, keep_b, got_b)
    got_a, got_b = exchange(send_a, z_second), exchange(send_b, x_second)
    block = keep_a.shape[1:]
    sums = pl.pallas_call(
        pair_kernel,
        out_shape=jax.ShapeDtypeStruct((2, *block), F32),
        in_specs=[vmem()] * 4,
        out_specs=vmem(),
        compiler_params=params(),
        name="pair",
    )(keep_a, got_a, keep_b, got_b)
    got = exchange(sums, z_third)
    one = jax.ShapeDtypeStruct((1, block[0] - 1, *block[1:]), F32)
    mine_a, mine_b = pl.pallas_call(
        mean_kernel,
        out_shape=(one, one),
        in_specs=[vmem()] * 2,
        out_specs=(vmem(), vmem()),
        compiler_params=params(),
        name="mean",
    )(sums, got)
    got_a, got_b = exchange(mine_a, z_second), exchange(mine_b, x_second)
    mine_a = join(ZB2, bits, mine_a, got_a)
    mine_b = join(XB2, bits, mine_b, got_b)
    got_a, got_b = exchange(mine_a, z_first), exchange(mine_b, x_first)
    mine_a = join(ZB1, bits, mine_a, got_a)
    mine_b = join(XB1, bits, mine_b, got_b)
    got_a, got_b = exchange(mine_a, x_second), exchange(mine_b, z_second)
    mine_a = join(XB2, bits, mine_a, got_a)
    mine_b = join(ZB2, bits, mine_b, got_b)
    got_a, got_b = exchange(mine_a, x_first), exchange(mine_b, z_first)
    return pl.pallas_call(
        output_kernel,
        out_shape=jax.ShapeDtypeStruct((cents, width), F32),
        in_specs=[smem()] + [vmem()] * 4,
        out_specs=vmem(),
        compiler_params=params(),
        name="output",
    )(bits, mine_a, got_a, mine_b, got_b)


def vmem():
    return pl.BlockSpec(memory_space=pltpu.VMEM)


def smem():
    return pl.BlockSpec(memory_space=pltpu.SMEM)


def params():
    return pltpu.CompilerParams(vmem_limit_bytes=VMEM_LIMIT)


def per_device(vectors, centroids):
    n_rows, n_cols = lax.axis_size("rows"), lax.axis_size("cols")
    rows, width = vectors.shape
    cents = centroids.shape[0]
    log_target = math.log(rows * n_rows / (cents * n_cols))
    groups, tiles = rows // LANES, cents // LANES
    kept = jax.ShapeDtypeStruct((cents, rows), F32)
    ok_type = jax.ShapeDtypeStruct((1, 1), jnp.int32)
    row_parts = jax.ShapeDtypeStruct((n_cols, groups, LANES), F32)
    col_parts = jax.ShapeDtypeStruct((n_rows, tiles, LANES), F32)
    row_scratch = pltpu.VMEM((groups, LANES), F32)
    col_scratch = pltpu.VMEM((tiles, LANES), F32)

    bits = position_bits()

    kernel, ok, part = pl.pallas_call(
        logits_kernel,
        out_shape=(kept, ok_type, row_parts),
        in_specs=[vmem(), vmem()],
        out_specs=(vmem(), smem(), vmem()),
        scratch_shapes=[row_scratch],
        compiler_params=params(),
        name="logits",
    )(centroids, vectors)

    for step in range(ITERS):
        row_got = lax.all_to_all(part, "cols", 0, 0, tiled=True)
        part = pl.pallas_call(
            col_kernel,
            out_shape=col_parts,
            in_specs=[vmem(), smem(), vmem()],
            out_specs=vmem(),
            scratch_shapes=[col_scratch],
            compiler_params=params(),
            name="col_step",
        )(row_got, ok, kernel)
        col_got = lax.all_to_all(part, "rows", 0, 0, tiled=True)
        part = pl.pallas_call(
            functools.partial(row_kernel, log_target),
            out_shape=row_parts,
            in_specs=[vmem(), smem(), vmem()],
            out_specs=vmem(),
            scratch_shapes=[col_scratch, row_scratch],
            compiler_params=params(),
            name="row_step",
        )(col_got, ok, kernel)
    row_got = lax.all_to_all(part, "cols", 0, 0, tiled=True)

    part_units = PARTS * (width // LANES) + 1
    halves = jax.ShapeDtypeStruct((cents // BLOCK // 4, part_units, 8, LANES), F32)
    send_a, send_b, plan, mass, row_pot, col_pot = pl.pallas_call(
        functools.partial(plan_kernel, log_target),
        out_shape=(
            halves,
            halves,
            jax.ShapeDtypeStruct((cents, rows), jnp.bfloat16),
            jax.ShapeDtypeStruct((cents // BLOCK, 8, LANES), F32),
            jax.ShapeDtypeStruct((groups, LANES), F32),
            jax.ShapeDtypeStruct((tiles, LANES), F32),
        ),
        in_specs=[smem(), vmem(), vmem(), smem(), vmem(), vmem()],
        out_specs=(vmem(),) * 6,
        scratch_shapes=[col_scratch],
        compiler_params=params(),
        name="plan",
    )(bits, col_got, row_got, ok, kernel, vectors)
    keep_a, keep_b = pl.pallas_call(
        keep_kernel,
        out_shape=(halves, halves),
        in_specs=[smem(), vmem(), vmem(), vmem()],
        out_specs=(vmem(), vmem()),
        compiler_params=params(),
        cost_estimate=pl.CostEstimate(flops=rows * cents * width, bytes_accessed=8 << 20, transcendentals=0),
        name="keep",
    )(bits, plan, mass, vectors)
    new_centroids = mean_over_rows(bits, send_a, keep_a, send_b, keep_b, cents, width)
    return (new_centroids, row_pot.reshape(rows), col_pot.reshape(cents))


def solution(mesh):
    return jax.shard_map(
        per_device,
        mesh=mesh,
        in_specs=(P("rows", None), P("cols", None)),
        out_specs=(P("cols", None), P("rows"), P("cols")),
        check_vma=False,
    )
```

```python
import functools
import math

import jax
import jax.numpy as jnp
from jax import lax
from jax.experimental import pallas as pl
from jax.experimental.pallas import tpu as pltpu
from jax.sharding import PartitionSpec as P

ITERS = 3
LANES = 128
LIM = 40.0
MIB = 1024 * 1024
F32 = jnp.float32
XS, ZS = 4, 8
BLOCK = 32
PARTS = BLOCK // 8
CHUNKS = 4
XB1, XB2, ZB1, ZB2 = range(4)


def combine_lse(parts):
    top = jnp.max(parts, axis=0)
    return top + jnp.log(jnp.sum(jnp.exp(parts - top[None]), axis=0))


def lane_to_sublane(row):
    return jnp.transpose(jnp.broadcast_to(row, (LANES, LANES)))


def fold(x):
    return jnp.sum(x.reshape(x.shape[0] // 8, 8, x.shape[1]), axis=0)


def lane_group(g):
    return slice(g * LANES, (g + 1) * LANES)


def row_tile(t):
    return pl.ds(pl.multiple_of(t * LANES, LANES), LANES)


def put_copies(out_ref, value):
    for k in range(out_ref.shape[0]):
        out_ref[k] = value


def logit_block(k_ref, ok, t, g):
    block = k_ref[row_tile(t), lane_group(g)]
    return jnp.where(ok != 0, jnp.log(block), block)


def row_lse_exact(k_ref, ok, pot_ref, out_ref):
    tiles, groups = k_ref.shape[0] // LANES, k_ref.shape[1] // LANES

    def shifted(t, g):
        z = logit_block(k_ref, ok, t, g)
        return z if pot_ref is None else z + lane_to_sublane(pot_ref[pl.ds(t, 1), :])

    for g in range(groups):
        def top_of(t, top, g=g):
            return jnp.maximum(top, jnp.max(shifted(t, g), axis=0, keepdims=True))

        top = lax.fori_loop(0, tiles, top_of, jnp.full((1, LANES), -3.0e38, F32))

        def sum_of(t, total, g=g, top=top):
            return total + jnp.sum(jnp.exp(shifted(t, g) - top), axis=0, keepdims=True)

        total = lax.fori_loop(0, tiles, sum_of, jnp.zeros((1, LANES), F32))
        out_ref[g : g + 1, :] = top + jnp.log(total)


def col_lse_exact(k_ref, ok, pot, out_ref):
    tiles, groups = k_ref.shape[0] // LANES, k_ref.shape[1] // LANES

    def tile(t, carry):
        top = jnp.full((LANES, LANES), -3.0e38, F32)
        for g in range(groups):
            top = jnp.maximum(top, logit_block(k_ref, ok, t, g) + pot[g : g + 1, :])
        top = jnp.broadcast_to(jnp.max(top, axis=1, keepdims=True), (LANES, LANES))
        total = jnp.zeros((LANES, LANES), F32)
        for g in range(groups):
            total = total + jnp.exp(logit_block(k_ref, ok, t, g) + pot[g : g + 1, :] - top)
        total = jnp.sum(jnp.transpose(total), axis=0, keepdims=True)
        out_ref[pl.ds(t, 1), :] = jnp.transpose(top)[0:1, :] + jnp.log(total)
        return carry

    lax.fori_loop(0, tiles, tile, 0)


def logits_kernel(_, cent_hbm, vec_hbm, k_ref, ok_ref, out_ref, lse_ref, cent_ref, vec_ref, sems):
    cents, rows = k_ref.shape
    groups = rows // LANES
    step, chunk = cents // CHUNKS, rows // CHUNKS

    def pieces(hbm_ref, vmem_ref, first, size):
        return [
            pltpu.make_async_copy(
                hbm_ref.at[pl.ds(c * size, size), :], vmem_ref.at[pl.ds(c * size, size), :], sems.at[first + c]
            )
            for c in range(CHUNKS)
        ]

    vec_copies = pieces(vec_hbm, vec_ref, 0, chunk)
    cent_copies = pieces(cent_hbm, cent_ref, CHUNKS, step)
    for copy in vec_copies[:1] + cent_copies + vec_copies[1:]:
        copy.start()

    peak = jnp.zeros((8, LANES), F32)
    for c in range(CHUNKS):
        vec_copies[c].wait()
        if c == 0:
            for copy in cent_copies:
                copy.wait()
        block = lax.dot_general(
            cent_ref[...], vec_ref[c * chunk : (c + 1) * chunk, :],
            (((1,), (1,)), ((), ())), preferred_element_type=F32,
        )
        for g in range(chunk // LANES):
            group = c * (chunk // LANES) + g
            total = jnp.zeros((8, LANES), F32)
            for t in range(cents // LANES):
                part = 4.0 * block[t * LANES : (t + 1) * LANES, lane_group(g)]
                peak = jnp.maximum(peak, jnp.max(jnp.abs(part).reshape(LANES // 8, 8, LANES), axis=0))
                part = jnp.exp(part)
                k_ref[t * LANES : (t + 1) * LANES, lane_group(group)] = part
                total = total + fold(part)
            lse_ref[group : group + 1, :] = jnp.sum(total, axis=0, keepdims=True)
    lse_ref[...] = jnp.log(lse_ref[...])
    ok = jnp.max(peak) <= LIM
    ok_ref[0, 0] = ok.astype(jnp.int32)

    @pl.when(jnp.logical_not(ok))
    def _():
        def tile(t, carry):
            at = row_tile(t)
            for g in range(groups):
                k_ref[at, lane_group(g)] = 4.0 * lax.dot_general(
                    cent_ref[at, :], vec_ref[lane_group(g), :],
                    (((1,), (1,)), ((), ())), preferred_element_type=F32,
                )
            return carry

        lax.fori_loop(0, cents // LANES, tile, 0)
        row_lse_exact(k_ref, 0, None, lse_ref)

    put_copies(out_ref, lse_ref[...])


def row_kernel(log_target, got_ref, ok_ref, k_ref, out_ref, pot_ref, lse_ref):
    tiles, groups = k_ref.shape[0] // LANES, k_ref.shape[1] // LANES
    pot = log_target - combine_lse(got_ref[...])
    ok = ok_ref[0, 0]
    fast = jnp.logical_and(ok != 0, jnp.max(jnp.abs(pot)) <= LIM)

    @pl.when(fast)
    def _():
        scales = jnp.exp(pot)
        sums = [jnp.zeros((8, LANES), F32)] * groups
        for t in range(tiles):
            scale = lane_to_sublane(scales[t : t + 1, :])
            for g in range(groups):
                sums[g] = sums[g] + fold(k_ref[t * LANES : (t + 1) * LANES, lane_group(g)] * scale)
        for g in range(groups):
            lse_ref[g : g + 1, :] = jnp.sum(sums[g], axis=0, keepdims=True)
        lse_ref[...] = jnp.log(lse_ref[...])

    @pl.when(jnp.logical_not(fast))
    def _():
        pot_ref[...] = pot
        row_lse_exact(k_ref, ok, pot_ref, lse_ref)

    put_copies(out_ref, lse_ref[...])


def col_kernel(got_ref, ok_ref, k_ref, out_ref, lse_ref):
    tiles, groups = k_ref.shape[0] // LANES, k_ref.shape[1] // LANES
    pot = -combine_lse(got_ref[...])
    ok = ok_ref[0, 0]
    fast = jnp.logical_and(ok != 0, jnp.max(jnp.abs(pot)) <= LIM)

    @pl.when(fast)
    def _():
        scale = jnp.exp(pot)

        for t in range(tiles):
            total = jnp.zeros((LANES, LANES), F32)
            for g in range(groups):
                total = total + k_ref[t * LANES : (t + 1) * LANES, lane_group(g)] * scale[g : g + 1, :]
            lse_ref[t : t + 1, :] = jnp.sum(jnp.transpose(total), axis=0, keepdims=True)
        lse_ref[...] = jnp.log(lse_ref[...])

    @pl.when(jnp.logical_not(fast))
    def _():
        col_lse_exact(k_ref, ok, pot, lse_ref)

    put_copies(out_ref, lse_ref[...])


def half_kernel(
    log_target, keep, bits_ref, cols_ref, rows_ref, ok_ref, k_ref, vec_ref,
    a_ref, b_ref, *rest,
):
    scale_ref, plan_ref, mass_ref = rest[-3:]
    groups = k_ref.shape[1] // LANES
    col_pot = log_target - combine_lse(cols_ref[...])
    row_pot = -combine_lse(rows_ref[...])
    if not keep:
        rest[0][...] = row_pot
        rest[1][...] = col_pot
    ok = ok_ref[0, 0]
    fast = jnp.logical_and(
        ok != 0, jnp.maximum(jnp.max(jnp.abs(col_pot)), jnp.max(jnp.abs(row_pot))) <= LIM
    )
    scale_ref[...] = jnp.where(fast, jnp.exp(col_pot), col_pot)
    row_scale = jnp.exp(row_pot)
    blocks = a_ref.shape[0]
    tiles = blocks * BLOCK // LANES

    def plan_tile(spot, block):
        total = jnp.zeros((LANES, LANES), F32)
        for g in range(groups):
            plan = block(g)
            total = total + plan
            plan_ref[row_tile(spot), lane_group(g)] = plan.astype(jnp.bfloat16)
        mass = jnp.broadcast_to(jnp.sum(total, axis=1, keepdims=True), (LANES, LANES))
        lane = lax.broadcasted_iota(jnp.int32, (8, LANES), 1) // (LANES // PARTS)
        for b in range(LANES // BLOCK):
            unit = mass[b * BLOCK : b * BLOCK + 8, :]
            for k in range(1, PARTS):
                at = b * BLOCK + 8 * k
                unit = jnp.where(lane == k, mass[at : at + 8, :], unit)
            mass_ref[spot * (LANES // BLOCK) + b] = unit

    firsts = []
    for chain, which in enumerate((XB1, ZB1)):
        bit = bits_ref[which] if keep else 1 - bits_ref[which]
        firsts.append((chain * 2 + bit) * tiles)

    def sums():
        size = blocks * BLOCK
        for chain, out_ref in enumerate((a_ref, b_ref)):
            block = jnp.dot(
                plan_ref[chain * size : (chain + 1) * size, :], vec_ref[...], preferred_element_type=F32
            )
            across = block.shape[1] // LANES
            for b in range(blocks):
                for k in range(PARTS):
                    row = b * BLOCK + 8 * k
                    for g in range(across):
                        out_ref[b, k * across + g] = block[row : row + 8, lane_group(g)]
                out_ref[b, out_ref.shape[1] - 1] = mass_ref[chain * blocks + b]

    @pl.when(fast)
    def _():
        for chain, first in enumerate(firsts):
            for t in range(tiles):
                scale = lane_to_sublane(scale_ref[pl.ds(first + t, 1), :])
                plan_tile(
                    chain * tiles + t,
                    lambda g: k_ref[row_tile(first + t), lane_group(g)] * row_scale[g : g + 1, :] * scale,
                )
        sums()

    @pl.when(jnp.logical_not(fast))
    def _():
        for chain, first in enumerate(firsts):
            def tile(t, carry):
                shift = lane_to_sublane(scale_ref[pl.ds(first + t, 1), :])
                plan_tile(
                    chain * tiles + t,
                    lambda g: jnp.exp(
                        logit_block(k_ref, ok, first + t, g) + row_pot[g : g + 1, :] + shift
                    ),
                )
                return carry

            lax.fori_loop(0, tiles, tile, 0)
        sums()


def fold_kernel(which, bits_ref, keep_ref, got_ref, send_ref, kept_ref):
    half = send_ref.shape[0]
    mine = bits_ref[which] * half
    other = (1 - bits_ref[which]) * half
    for b in range(half):
        send_ref[b] = keep_ref[other + b] + got_ref[other + b]
        kept_ref[b] = keep_ref[mine + b] + got_ref[mine + b]


def quarter_kernel(keep_a_ref, got_a_ref, keep_b_ref, got_b_ref, out_ref):
    for p in range(out_ref.shape[0]):
        out_ref[p, 0] = keep_a_ref[p] + got_a_ref[p]
        out_ref[p, 1] = keep_b_ref[p] + got_b_ref[p]


def four_kernel(got_ref, out_ref):
    out_ref[...] = (got_ref[0] + got_ref[1]) + (got_ref[2] + got_ref[3])


def mean_kernel(sum_ref, got_ref, out_ref):
    copies, chains, _, width = out_ref.shape
    units = sum_ref.shape[1] - 1
    across = width // LANES
    lanes = LANES // PARTS
    for chain in range(chains):
        mass = sum_ref[chain, units] + got_ref[chain, units]
        for k in range(PARTS):
            part = jnp.broadcast_to(mass[:, k * lanes : k * lanes + 1], (8, LANES))
            for g in range(across):
                u = k * across + g
                mean = (sum_ref[chain, u] + got_ref[chain, u]) / part
                for copy in range(copies):
                    out_ref[copy, chain, 8 * k : 8 * k + 8, lane_group(g)] = mean


def part_kernel(got_ref, a_ref, b_ref):
    for p in range(got_ref.shape[0]):
        at = slice(p * BLOCK, (p + 1) * BLOCK)
        a_ref[at, :] = got_ref[p, 0]
        b_ref[at, :] = got_ref[p, 1]


def join_kernel(which, bits_ref, mine_ref, got_ref, out_ref):
    size = mine_ref.shape[0]
    bit = bits_ref[which]
    out_ref[pl.ds(pl.multiple_of(bit * size, size), size), :] = mine_ref[...]
    out_ref[pl.ds(pl.multiple_of((1 - bit) * size, size), size), :] = got_ref[...]


def place_kernel(own, bits_ref, a_ref, b_ref, *rest):
    out_ref, sems = rest[-2:]
    size = a_ref.shape[0]
    copies = []
    for chain, (which, part_ref) in enumerate(((XB1, a_ref), (ZB1, b_ref))):
        side = bits_ref[which] if own else 1 - bits_ref[which]
        at = pl.ds(pl.multiple_of((2 * chain + side) * size, size), size)
        copies.append(pltpu.make_async_copy(part_ref, out_ref.at[at, :], sems.at[chain]))
    for copy in copies:
        copy.start()
    for copy in copies:
        copy.wait()


def place(row, core):
    return (row // ZS + (XS - 1) * core) % XS, (row % ZS + (ZS - 1) * core) % ZS


def pairs(partner, n_cols):
    out = []
    for row in range(XS * ZS):
        for col in range(n_cols):
            core = col % 2
            x, z = partner(*place(row, core))
            to = (x + core) % XS * ZS + (z + core) % ZS
            out.append((row * n_cols + col, to * n_cols + col))
    return out


def exchange(x, partner):
    return lax.ppermute(x, ("rows", "cols"), pairs(partner, lax.axis_size("cols")))


def x_first(x, z):
    return x ^ 1, z


def x_second(x, z):
    return XS - 1 - x, z


def z_first(x, z):
    return x, z ^ 1


def z_second(x, z):
    return x, (z - 1 + 2 * (z % 2)) % ZS


def z_third(x, z):
    return x, {0: 3, 3: 0, 1: 6, 6: 1, 2: 5, 5: 2, 4: 7, 7: 4}[z]


def position_bits():
    x, z = place(lax.axis_index("rows"), lax.axis_index("cols") % 2)
    return jnp.stack([(x ^ (x >> 1)) & 1, x >> 1, ((z + 1) >> 1) & 1, (0xB4 >> z) & 1]).astype(jnp.int32)


def quads(n_cols):
    groups = {}
    for row in range(XS * ZS):
        for col in range(n_cols):
            x, z = place(row, col % 2)
            key = (col, min(x, x_second(x, z)[0]), min(z, z_second(x, z)[1]))
            groups.setdefault(key, []).append(((x >> 1) * 2 + ((0xB4 >> z) & 1), row * n_cols + col))
    return [[device for _, device in sorted(groups[key])] for key in sorted(groups)]


def trade(x):
    return lax.all_to_all(
        x, ("rows", "cols"), 0, 0, tiled=True, axis_index_groups=quads(lax.axis_size("cols"))
    )


def halve(which, bits, keep, got):
    half = jax.ShapeDtypeStruct((keep.shape[0] // 2, *keep.shape[1:]), F32)
    return pl.pallas_call(
        functools.partial(fold_kernel, which),
        out_shape=(half, half),
        in_specs=[smem(), vmem(), vmem()],
        out_specs=(vmem(), vmem()),
        compiler_params=params(4),
        name="fold",
    )(bits, keep, got)


def join(which, bits, mine, got):
    return pl.pallas_call(
        functools.partial(join_kernel, which),
        out_shape=jax.ShapeDtypeStruct((2 * mine.shape[0], *mine.shape[1:]), F32),
        in_specs=[smem(), vmem(), vmem()],
        out_specs=vmem(),
        compiler_params=params(4),
        name="join",
    )(bits, mine, got)


def put(own, bits, a, b, cents, *before):
    return pl.pallas_call(
        functools.partial(place_kernel, own),
        out_shape=jax.ShapeDtypeStruct((cents, a.shape[1]), F32),
        in_specs=[smem(), vmem(), vmem()] + [hbm()] * len(before),
        out_specs=hbm(),
        scratch_shapes=[pltpu.SemaphoreType.DMA((2,))],
        input_output_aliases={3: 0} if before else {},
        compiler_params=params(4),
        name="place",
    )(bits, a, b, *before)


def mean_over_rows(bits, send_a, keep_a, send_b, keep_b, cents, width):
    got_a, got_b = exchange(send_a, x_first), exchange(send_b, z_first)
    send_a, keep_a = halve(ZB1, bits, keep_a, got_a)
    send_b, keep_b = halve(XB1, bits, keep_b, got_b)
    got_a, got_b = exchange(send_a, z_first), exchange(send_b, x_first)
    block = keep_a.shape[1:]
    quarter = pl.pallas_call(
        quarter_kernel,
        out_shape=jax.ShapeDtypeStruct((4, 2, *block), F32),
        in_specs=[vmem()] * 4,
        out_specs=vmem(),
        compiler_params=params(4),
        name="quarter",
    )(keep_a, got_a, keep_b, got_b)
    sums = pl.pallas_call(
        four_kernel,
        out_shape=jax.ShapeDtypeStruct((2, *block), F32),
        in_specs=[vmem()],
        out_specs=vmem(),
        compiler_params=params(4),
        name="four",
    )(trade(quarter))
    mean = pl.pallas_call(
        mean_kernel,
        out_shape=jax.ShapeDtypeStruct((4, 2, BLOCK, width), F32),
        in_specs=[vmem()] * 2,
        out_specs=vmem(),
        compiler_params=params(4),
        name="mean",
    )(sums, exchange(sums, z_third))
    part = jax.ShapeDtypeStruct((4 * BLOCK, width), F32)
    mine_a, mine_b = pl.pallas_call(
        part_kernel,
        out_shape=(part, part),
        in_specs=[vmem()],
        out_specs=(vmem(), vmem()),
        compiler_params=params(4),
        name="part",
    )(trade(mean))
    got_a, got_b = exchange(mine_a, z_first), exchange(mine_b, x_first)
    mine_a = join(ZB1, bits, mine_a, got_a)
    mine_b = join(XB1, bits, mine_b, got_b)
    got_a, got_b = exchange(mine_a, x_first), exchange(mine_b, z_first)
    return put(False, bits, got_a, got_b, cents, put(True, bits, mine_a, mine_b, cents))


def vmem():
    return pl.BlockSpec(memory_space=pltpu.VMEM)


def hbm():
    return pl.BlockSpec(memory_space=pltpu.HBM)


def smem():
    return pl.BlockSpec(memory_space=pltpu.SMEM)


def pinned(x):
    return pltpu.with_memory_space_constraint(x, pltpu.VMEM)


def params(mib):
    return pltpu.CompilerParams(vmem_limit_bytes=mib * MIB)


def per_device(vectors, centroids):
    n_rows, n_cols = lax.axis_size("rows"), lax.axis_size("cols")
    rows, width = vectors.shape
    cents = centroids.shape[0]
    log_target = math.log(rows * n_rows / (cents * n_cols))
    groups, tiles = rows // LANES, cents // LANES
    kept = pltpu.VMEM((cents, rows), F32)
    ok_type = jax.ShapeDtypeStruct((1, 1), jnp.int32)
    row_parts = jax.ShapeDtypeStruct((n_cols, groups, LANES), F32)
    col_parts = jax.ShapeDtypeStruct((n_rows, tiles, LANES), F32)
    row_scratch = pltpu.VMEM((groups, LANES), F32)
    col_scratch = pltpu.VMEM((tiles, LANES), F32)

    bits = position_bits()

    kernel, ok, part = pl.pallas_call(
        logits_kernel,
        out_shape=(kept, ok_type, row_parts),
        in_specs=[smem(), hbm(), hbm()],
        out_specs=(vmem(), smem(), vmem()),
        scratch_shapes=[
            row_scratch,
            pltpu.VMEM((cents, width), jnp.bfloat16),
            pltpu.VMEM((rows, width), jnp.bfloat16),
            pltpu.SemaphoreType.DMA((2 * CHUNKS,)),
        ],
        compiler_params=params(24),
        name="logits",
    )(bits, *(pltpu.with_memory_space_constraint(x, pltpu.HBM) for x in (centroids, vectors)))

    for step in range(ITERS):
        row_got = lax.all_to_all(part, "cols", 0, 0, tiled=True)
        part = pl.pallas_call(
            col_kernel,
            out_shape=col_parts,
            in_specs=[vmem(), smem(), vmem()],
            out_specs=vmem(),
            scratch_shapes=[col_scratch],
            compiler_params=params(4),
            name="col_step",
        )(row_got, ok, pinned(kernel))
        col_got = lax.all_to_all(part, "rows", 0, 0, tiled=True)
        part = pl.pallas_call(
            functools.partial(row_kernel, log_target),
            out_shape=row_parts,
            in_specs=[vmem(), smem(), vmem()],
            out_specs=vmem(),
            scratch_shapes=[col_scratch, row_scratch],
            compiler_params=params(4),
            name="row_step",
        )(col_got, ok, pinned(kernel))
    row_got = lax.all_to_all(part, "cols", 0, 0, tiled=True)

    part_units = PARTS * (width // LANES) + 1
    halves = jax.ShapeDtypeStruct((cents // BLOCK // 4, part_units, 8, LANES), F32)

    def half(keep):
        pots = (jax.ShapeDtypeStruct((groups, LANES), F32), jax.ShapeDtypeStruct((tiles, LANES), F32))
        return pl.pallas_call(
            functools.partial(half_kernel, log_target, keep),
            out_shape=(halves, halves) + (() if keep else pots),
            in_specs=[smem(), vmem(), vmem(), smem(), vmem(), vmem()],
            out_specs=(vmem(),) * (2 if keep else 4),
            scratch_shapes=[
                col_scratch,
                pltpu.VMEM((cents // 2, rows), jnp.bfloat16),
                pltpu.VMEM((cents // BLOCK // 2, 8, LANES), F32),
            ],
            compiler_params=params(12),
            cost_estimate=pl.CostEstimate(
                flops=rows * cents * width, bytes_accessed=8 * MIB, transcendentals=0
            ),
            name="keep" if keep else "send",
        )(bits, col_got, row_got, ok, pinned(kernel), vectors)

    send_a, send_b, row_pot, col_pot = half(False)
    keep_a, keep_b = half(True)
    new_centroids = mean_over_rows(bits, send_a, keep_a, send_b, keep_b, cents, width)
    return (new_centroids, row_pot.reshape(rows), col_pot.reshape(cents))


def solution(mesh):
    return jax.shard_map(
        per_device,
        mesh=mesh,
        in_specs=(P("rows", None), P("cols", None)),
        out_specs=(P("cols", None), P("rows"), P("cols")),
        check_vma=False,
    )
```

```python
import functools
import math

import jax
import jax.numpy as jnp
from jax import lax
from jax.experimental import pallas as pl
from jax.experimental.pallas import tpu as pltpu
from jax.sharding import PartitionSpec as P

ITERS = 3
LANES = 128
LIM = 40.0
MIB = 1024 * 1024
F32 = jnp.float32
XS, ZS = 4, 8
BLOCK = 32
PARTS = BLOCK // 8
CHUNKS = 4
XB1, XB2, ZB1, ZB2 = range(4)


def combine_lse(parts):
    top = jnp.max(parts, axis=0)
    return top + jnp.log(jnp.sum(jnp.exp(parts - top[None]), axis=0))


def lane_to_sublane(row):
    return jnp.transpose(jnp.broadcast_to(row, (LANES, LANES)))


def fold(x):
    return jnp.sum(x.reshape(x.shape[0] // 8, 8, x.shape[1]), axis=0)


def lane_group(g):
    return slice(g * LANES, (g + 1) * LANES)


def row_tile(t):
    return pl.ds(pl.multiple_of(t * LANES, LANES), LANES)


def put_copies(out_ref, value):
    for k in range(out_ref.shape[0]):
        out_ref[k] = value


def logit_block(k_ref, ok, t, g):
    block = k_ref[row_tile(t), lane_group(g)]
    return jnp.where(ok, jnp.log(block), block)


def within(peak, *pots):
    for pot in pots:
        pot = jnp.abs(pot)
        for k in range(pot.shape[0] // 8):
            peak = jnp.maximum(peak, pot[8 * k : 8 * k + 8, :])
    return jnp.max(peak) <= LIM


def row_lse_exact(k_ref, ok, pot_ref, out_ref):
    tiles, groups = k_ref.shape[0] // LANES, k_ref.shape[1] // LANES

    def shifted(t, g):
        z = logit_block(k_ref, ok, t, g)
        return z if pot_ref is None else z + lane_to_sublane(pot_ref[pl.ds(t, 1), :])

    for g in range(groups):
        def top_of(t, top, g=g):
            return jnp.maximum(top, jnp.max(shifted(t, g), axis=0, keepdims=True))

        top = lax.fori_loop(0, tiles, top_of, jnp.full((1, LANES), -3.0e38, F32))

        def sum_of(t, total, g=g, top=top):
            return total + jnp.sum(jnp.exp(shifted(t, g) - top), axis=0, keepdims=True)

        total = lax.fori_loop(0, tiles, sum_of, jnp.zeros((1, LANES), F32))
        out_ref[g : g + 1, :] = top + jnp.log(total)


def col_lse_exact(k_ref, ok, pot, out_ref):
    tiles, groups = k_ref.shape[0] // LANES, k_ref.shape[1] // LANES

    def tile(t, carry):
        top = jnp.full((LANES, LANES), -3.0e38, F32)
        for g in range(groups):
            top = jnp.maximum(top, logit_block(k_ref, ok, t, g) + pot[g : g + 1, :])
        top = jnp.broadcast_to(jnp.max(top, axis=1, keepdims=True), (LANES, LANES))
        total = jnp.zeros((LANES, LANES), F32)
        for g in range(groups):
            total = total + jnp.exp(logit_block(k_ref, ok, t, g) + pot[g : g + 1, :] - top)
        total = jnp.sum(jnp.transpose(total), axis=0, keepdims=True)
        out_ref[pl.ds(t, 1), :] = jnp.transpose(top)[0:1, :] + jnp.log(total)
        return carry

    lax.fori_loop(0, tiles, tile, 0)


def logits_kernel(cent_hbm, vec_hbm, k_ref, peak_ref, out_ref, lse_ref, cent_ref, vec_ref, sems):
    cents, rows = k_ref.shape
    groups = rows // LANES
    step, chunk = cents // CHUNKS, rows // CHUNKS

    def pieces(hbm_ref, vmem_ref, first, size):
        return [
            pltpu.make_async_copy(
                hbm_ref.at[pl.ds(c * size, size), :], vmem_ref.at[pl.ds(c * size, size), :], sems.at[first + c]
            )
            for c in range(CHUNKS)
        ]

    vec_copies = pieces(vec_hbm, vec_ref, 0, chunk)
    cent_copies = pieces(cent_hbm, cent_ref, CHUNKS, step)
    for copy in vec_copies[:1] + cent_copies + vec_copies[1:]:
        copy.start()

    peak = jnp.zeros((8, LANES), F32)
    for c in range(CHUNKS):
        vec_copies[c].wait()
        if c == 0:
            for copy in cent_copies:
                copy.wait()
        block = lax.dot_general(
            cent_ref[...], vec_ref[c * chunk : (c + 1) * chunk, :],
            (((1,), (1,)), ((), ())), preferred_element_type=F32,
        )
        for g in range(chunk // LANES):
            group = c * (chunk // LANES) + g
            total = jnp.zeros((8, LANES), F32)
            for t in range(cents // LANES):
                part = 4.0 * block[t * LANES : (t + 1) * LANES, lane_group(g)]
                peak = jnp.maximum(peak, jnp.max(jnp.abs(part).reshape(LANES // 8, 8, LANES), axis=0))
                part = jnp.exp(part)
                k_ref[t * LANES : (t + 1) * LANES, lane_group(group)] = part
                total = total + fold(part)
            lse_ref[group : group + 1, :] = jnp.sum(total, axis=0, keepdims=True)
    lse_ref[...] = jnp.log(lse_ref[...])
    peak_ref[...] = peak

    @pl.when(jnp.logical_not(within(peak)))
    def _():
        def tile(t, carry):
            at = row_tile(t)
            for g in range(groups):
                k_ref[at, lane_group(g)] = 4.0 * lax.dot_general(
                    cent_ref[at, :], vec_ref[lane_group(g), :],
                    (((1,), (1,)), ((), ())), preferred_element_type=F32,
                )
            return carry

        lax.fori_loop(0, cents // LANES, tile, 0)
        row_lse_exact(k_ref, False, None, lse_ref)

    put_copies(out_ref, lse_ref[...])


def row_kernel(log_target, got_ref, peak_ref, k_ref, out_ref, pot_ref, lse_ref):
    tiles, groups = k_ref.shape[0] // LANES, k_ref.shape[1] // LANES
    pot = log_target - combine_lse(got_ref[...])
    fast = within(peak_ref[...], pot)

    @pl.when(fast)
    def _():
        scales = jnp.exp(pot)
        sums = [jnp.zeros((8, LANES), F32)] * groups
        for t in range(tiles):
            scale = lane_to_sublane(scales[t : t + 1, :])
            for g in range(groups):
                sums[g] = sums[g] + fold(k_ref[t * LANES : (t + 1) * LANES, lane_group(g)] * scale)
        for g in range(groups):
            lse_ref[g : g + 1, :] = jnp.sum(sums[g], axis=0, keepdims=True)
        lse_ref[...] = jnp.log(lse_ref[...])

    @pl.when(jnp.logical_not(fast))
    def _():
        pot_ref[...] = pot
        row_lse_exact(k_ref, within(peak_ref[...]), pot_ref, lse_ref)

    put_copies(out_ref, lse_ref[...])


def col_kernel(got_ref, peak_ref, k_ref, out_ref, lse_ref):
    tiles, groups = k_ref.shape[0] // LANES, k_ref.shape[1] // LANES
    pot = -combine_lse(got_ref[...])
    fast = within(peak_ref[...], pot)

    @pl.when(fast)
    def _():
        scale = jnp.exp(pot)

        for t in range(tiles):
            total = jnp.zeros((LANES, LANES), F32)
            for g in range(groups):
                total = total + k_ref[t * LANES : (t + 1) * LANES, lane_group(g)] * scale[g : g + 1, :]
            lse_ref[t : t + 1, :] = jnp.sum(jnp.transpose(total), axis=0, keepdims=True)
        lse_ref[...] = jnp.log(lse_ref[...])

    @pl.when(jnp.logical_not(fast))
    def _():
        col_lse_exact(k_ref, within(peak_ref[...]), pot, lse_ref)

    put_copies(out_ref, lse_ref[...])


def half_kernel(
    log_target, keep, cols_ref, rows_ref, peak_ref, k_ref, vec_ref,
    a_ref, b_ref, *rest,
):
    scale_ref, plan_ref, mass_ref = rest[-3:]
    groups = k_ref.shape[1] // LANES
    col_pot = log_target - combine_lse(cols_ref[...])
    row_pot = -combine_lse(rows_ref[...])
    if not keep:
        rest[0][...] = row_pot
        rest[1][...] = col_pot
    fast = within(peak_ref[...], col_pot, row_pot)
    scale_ref[...] = jnp.where(fast, jnp.exp(col_pot), col_pot)
    row_scale = jnp.exp(row_pot)
    blocks = a_ref.shape[0]
    tiles = blocks * BLOCK // LANES

    def plan_tile(spot, block):
        total = jnp.zeros((LANES, LANES), F32)
        for g in range(groups):
            plan = block(g)
            total = total + plan
            plan_ref[row_tile(spot), lane_group(g)] = plan.astype(jnp.bfloat16)
        mass = jnp.broadcast_to(jnp.sum(total, axis=1, keepdims=True), (LANES, LANES))
        lane = lax.broadcasted_iota(jnp.int32, (8, LANES), 1) // (LANES // PARTS)
        for b in range(LANES // BLOCK):
            unit = mass[b * BLOCK : b * BLOCK + 8, :]
            for k in range(1, PARTS):
                at = b * BLOCK + 8 * k
                unit = jnp.where(lane == k, mass[at : at + 8, :], unit)
            mass_ref[spot * (LANES // BLOCK) + b] = unit

    bits = position_bits()
    firsts = []
    for chain, which in enumerate((XB1, ZB1)):
        bit = bits[which] if keep else 1 - bits[which]
        firsts.append((chain * 2 + bit) * tiles)

    def sums():
        size = blocks * BLOCK
        for chain, out_ref in enumerate((a_ref, b_ref)):
            block = jnp.dot(
                plan_ref[chain * size : (chain + 1) * size, :], vec_ref[...], preferred_element_type=F32
            )
            across = block.shape[1] // LANES
            for b in range(blocks):
                for k in range(PARTS):
                    row = b * BLOCK + 8 * k
                    for g in range(across):
                        out_ref[b, k * across + g] = block[row : row + 8, lane_group(g)]
                out_ref[b, out_ref.shape[1] - 1] = mass_ref[chain * blocks + b]

    @pl.when(fast)
    def _():
        for chain, first in enumerate(firsts):
            for t in range(tiles):
                scale = lane_to_sublane(scale_ref[pl.ds(first + t, 1), :])
                plan_tile(
                    chain * tiles + t,
                    lambda g: k_ref[row_tile(first + t), lane_group(g)] * row_scale[g : g + 1, :] * scale,
                )
        sums()

    @pl.when(jnp.logical_not(fast))
    def _():
        ok = within(peak_ref[...])
        for chain, first in enumerate(firsts):
            def tile(t, carry):
                shift = lane_to_sublane(scale_ref[pl.ds(first + t, 1), :])
                plan_tile(
                    chain * tiles + t,
                    lambda g: jnp.exp(
                        logit_block(k_ref, ok, first + t, g) + row_pot[g : g + 1, :] + shift
                    ),
                )
                return carry

            lax.fori_loop(0, tiles, tile, 0)
        sums()


def fold_kernel(which, keep_ref, got_ref, send_ref, kept_ref):
    half = send_ref.shape[0]
    bit = position_bits()[which]
    mine, other = bit * half, (1 - bit) * half
    for b in range(half):
        send_ref[b] = keep_ref[other + b] + got_ref[other + b]
        kept_ref[b] = keep_ref[mine + b] + got_ref[mine + b]


def quarter_kernel(keep_a_ref, got_a_ref, keep_b_ref, got_b_ref, out_ref):
    for p in range(out_ref.shape[0]):
        out_ref[p, 0] = keep_a_ref[p] + got_a_ref[p]
        out_ref[p, 1] = keep_b_ref[p] + got_b_ref[p]


def four_kernel(got_ref, out_ref):
    out_ref[...] = (got_ref[0] + got_ref[1]) + (got_ref[2] + got_ref[3])


def mean_kernel(sum_ref, got_ref, out_ref):
    copies, chains, _, width = out_ref.shape
    units = sum_ref.shape[1] - 1
    across = width // LANES
    lanes = LANES // PARTS
    for chain in range(chains):
        mass = sum_ref[chain, units] + got_ref[chain, units]
        for k in range(PARTS):
            part = jnp.broadcast_to(mass[:, k * lanes : k * lanes + 1], (8, LANES))
            for g in range(across):
                u = k * across + g
                mean = (sum_ref[chain, u] + got_ref[chain, u]) / part
                for copy in range(copies):
                    out_ref[copy, chain, 8 * k : 8 * k + 8, lane_group(g)] = mean


def part_kernel(got_ref, a_ref, b_ref):
    for p in range(got_ref.shape[0]):
        at = slice(p * BLOCK, (p + 1) * BLOCK)
        a_ref[at, :] = got_ref[p, 0]
        b_ref[at, :] = got_ref[p, 1]


def join_kernel(which, mine_ref, got_ref, out_ref):
    size = mine_ref.shape[0]
    bit = position_bits()[which]
    out_ref[pl.ds(pl.multiple_of(bit * size, size), size), :] = mine_ref[...]
    out_ref[pl.ds(pl.multiple_of((1 - bit) * size, size), size), :] = got_ref[...]


def place_kernel(own, a_ref, b_ref, *rest):
    out_ref, sems = rest[-2:]
    size = a_ref.shape[0]
    bits = position_bits()
    copies = []
    for chain, (which, part_ref) in enumerate(((XB1, a_ref), (ZB1, b_ref))):
        side = bits[which] if own else 1 - bits[which]
        at = pl.ds(pl.multiple_of((2 * chain + side) * size, size), size)
        copies.append(pltpu.make_async_copy(part_ref, out_ref.at[at, :], sems.at[chain]))
    for copy in copies:
        copy.start()
    for copy in copies:
        copy.wait()


def place(row, core):
    return (row // ZS + (XS - 1) * core) % XS, (row % ZS + (ZS - 1) * core) % ZS


def pairs(partner, n_cols):
    out = []
    for row in range(XS * ZS):
        for col in range(n_cols):
            core = col % 2
            x, z = partner(*place(row, core))
            to = (x + core) % XS * ZS + (z + core) % ZS
            out.append((row * n_cols + col, to * n_cols + col))
    return out


def exchange(x, partner):
    return lax.ppermute(x, ("rows", "cols"), pairs(partner, lax.axis_size("cols")))


def x_first(x, z):
    return x ^ 1, z


def x_second(x, z):
    return XS - 1 - x, z


def z_first(x, z):
    return x, z ^ 1


def z_second(x, z):
    return x, (z - 1 + 2 * (z % 2)) % ZS


def z_third(x, z):
    return x, {0: 3, 3: 0, 1: 6, 6: 1, 2: 5, 5: 2, 4: 7, 7: 4}[z]


def position_bits():
    core = lax.axis_index("cols") & 1
    row = lax.axis_index("rows")
    x = ((row >> 3) + (XS - 1) * core) & (XS - 1)
    z = (row + (ZS - 1) * core) & (ZS - 1)
    return (x ^ (x >> 1)) & 1, x >> 1, ((z + 1) >> 1) & 1, (0xB4 >> z) & 1


def quads(n_cols):
    groups = {}
    for row in range(XS * ZS):
        for col in range(n_cols):
            x, z = place(row, col % 2)
            key = (col, min(x, x_second(x, z)[0]), min(z, z_second(x, z)[1]))
            groups.setdefault(key, []).append(((x >> 1) * 2 + ((0xB4 >> z) & 1), row * n_cols + col))
    return [[device for _, device in sorted(groups[key])] for key in sorted(groups)]


def trade(x):
    return lax.all_to_all(
        x, ("rows", "cols"), 0, 0, tiled=True, axis_index_groups=quads(lax.axis_size("cols"))
    )


def halve(which, keep, got):
    half = jax.ShapeDtypeStruct((keep.shape[0] // 2, *keep.shape[1:]), F32)
    return pl.pallas_call(
        functools.partial(fold_kernel, which),
        out_shape=(half, half),
        in_specs=[vmem(), vmem()],
        out_specs=(vmem(), vmem()),
        compiler_params=params(4),
        name="fold",
    )(keep, got)


def join(which, mine, got):
    return pl.pallas_call(
        functools.partial(join_kernel, which),
        out_shape=jax.ShapeDtypeStruct((2 * mine.shape[0], *mine.shape[1:]), F32),
        in_specs=[vmem(), vmem()],
        out_specs=vmem(),
        compiler_params=params(4),
        name="join",
    )(mine, got)


def put(own, a, b, cents, *before):
    return pl.pallas_call(
        functools.partial(place_kernel, own),
        out_shape=jax.ShapeDtypeStruct((cents, a.shape[1]), F32),
        in_specs=[vmem(), vmem()] + [hbm()] * len(before),
        out_specs=hbm(),
        scratch_shapes=[pltpu.SemaphoreType.DMA((2,))],
        input_output_aliases={2: 0} if before else {},
        compiler_params=params(4),
        name="place",
    )(a, b, *before)


def mean_over_rows(send_a, keep_a, send_b, keep_b, cents, width):
    got_a, got_b = exchange(send_a, x_first), exchange(send_b, z_first)
    send_a, keep_a = halve(ZB1, keep_a, got_a)
    send_b, keep_b = halve(XB1, keep_b, got_b)
    got_a, got_b = exchange(send_a, z_first), exchange(send_b, x_first)
    block = keep_a.shape[1:]
    quarter = pl.pallas_call(
        quarter_kernel,
        out_shape=jax.ShapeDtypeStruct((4, 2, *block), F32),
        in_specs=[vmem()] * 4,
        out_specs=vmem(),
        compiler_params=params(4),
        name="quarter",
    )(keep_a, got_a, keep_b, got_b)
    sums = pl.pallas_call(
        four_kernel,
        out_shape=jax.ShapeDtypeStruct((2, *block), F32),
        in_specs=[vmem()],
        out_specs=vmem(),
        compiler_params=params(4),
        name="four",
    )(trade(quarter))
    mean = pl.pallas_call(
        mean_kernel,
        out_shape=jax.ShapeDtypeStruct((4, 2, BLOCK, width), F32),
        in_specs=[vmem()] * 2,
        out_specs=vmem(),
        compiler_params=params(4),
        name="mean",
    )(sums, exchange(sums, z_third))
    part = jax.ShapeDtypeStruct((4 * BLOCK, width), F32)
    mine_a, mine_b = pl.pallas_call(
        part_kernel,
        out_shape=(part, part),
        in_specs=[vmem()],
        out_specs=(vmem(), vmem()),
        compiler_params=params(4),
        name="part",
    )(trade(mean))
    got_a, got_b = exchange(mine_a, z_first), exchange(mine_b, x_first)
    mine_a = join(ZB1, mine_a, got_a)
    mine_b = join(XB1, mine_b, got_b)
    got_a, got_b = exchange(mine_a, x_first), exchange(mine_b, z_first)
    return put(False, got_a, got_b, cents, put(True, mine_a, mine_b, cents))


def vmem():
    return pl.BlockSpec(memory_space=pltpu.VMEM)


def hbm():
    return pl.BlockSpec(memory_space=pltpu.HBM)


def pinned(x):
    return pltpu.with_memory_space_constraint(x, pltpu.VMEM)


def params(mib):
    return pltpu.CompilerParams(vmem_limit_bytes=mib * MIB)


def per_device(vectors, centroids):
    n_rows, n_cols = lax.axis_size("rows"), lax.axis_size("cols")
    rows, width = vectors.shape
    cents = centroids.shape[0]
    log_target = math.log(rows * n_rows / (cents * n_cols))
    groups, tiles = rows // LANES, cents // LANES
    kept = pltpu.VMEM((cents, rows), F32)
    peak_type = jax.ShapeDtypeStruct((8, LANES), F32)
    row_parts = jax.ShapeDtypeStruct((n_cols, groups, LANES), F32)
    col_parts = jax.ShapeDtypeStruct((n_rows, tiles, LANES), F32)
    row_scratch = pltpu.VMEM((groups, LANES), F32)
    col_scratch = pltpu.VMEM((tiles, LANES), F32)

    kernel, peak, part = pl.pallas_call(
        logits_kernel,
        out_shape=(kept, peak_type, row_parts),
        in_specs=[hbm(), hbm()],
        out_specs=(vmem(), vmem(), vmem()),
        scratch_shapes=[
            row_scratch,
            pltpu.VMEM((cents, width), jnp.bfloat16),
            pltpu.VMEM((rows, width), jnp.bfloat16),
            pltpu.SemaphoreType.DMA((2 * CHUNKS,)),
        ],
        compiler_params=params(24),
        name="logits",
    )(*(pltpu.with_memory_space_constraint(x, pltpu.HBM) for x in (centroids, vectors)))

    for step in range(ITERS):
        row_got = lax.all_to_all(part, "cols", 0, 0, tiled=True)
        part = pl.pallas_call(
            col_kernel,
            out_shape=col_parts,
            in_specs=[vmem(), vmem(), vmem()],
            out_specs=vmem(),
            scratch_shapes=[col_scratch],
            compiler_params=params(4),
            name="col_step",
        )(row_got, peak, pinned(kernel))
        col_got = lax.all_to_all(part, "rows", 0, 0, tiled=True)
        part = pl.pallas_call(
            functools.partial(row_kernel, log_target),
            out_shape=row_parts,
            in_specs=[vmem(), vmem(), vmem()],
            out_specs=vmem(),
            scratch_shapes=[col_scratch, row_scratch],
            compiler_params=params(4),
            name="row_step",
        )(col_got, peak, pinned(kernel))
    row_got = lax.all_to_all(part, "cols", 0, 0, tiled=True)

    part_units = PARTS * (width // LANES) + 1
    halves = jax.ShapeDtypeStruct((cents // BLOCK // 4, part_units, 8, LANES), F32)

    def half(keep):
        pots = (jax.ShapeDtypeStruct((groups, LANES), F32), jax.ShapeDtypeStruct((tiles, LANES), F32))
        return pl.pallas_call(
            functools.partial(half_kernel, log_target, keep),
            out_shape=(halves, halves) + (() if keep else pots),
            in_specs=[vmem()] * 5,
            out_specs=(vmem(),) * (2 if keep else 4),
            scratch_shapes=[
                col_scratch,
                pltpu.VMEM((cents // 2, rows), jnp.bfloat16),
                pltpu.VMEM((cents // BLOCK // 2, 8, LANES), F32),
            ],
            compiler_params=params(12),
            cost_estimate=pl.CostEstimate(
                flops=rows * cents * width, bytes_accessed=8 * MIB, transcendentals=0
            ),
            name="keep" if keep else "send",
        )(col_got, row_got, peak, pinned(kernel), vectors)

    send_a, send_b, row_pot, col_pot = half(False)
    keep_a, keep_b = half(True)
    new_centroids = mean_over_rows(send_a, keep_a, send_b, keep_b, cents, width)
    return (new_centroids, row_pot.reshape(rows), col_pot.reshape(cents))


def solution(mesh):
    return jax.shard_map(
        per_device,
        mesh=mesh,
        in_specs=(P("rows", None), P("cols", None)),
        out_specs=(P("cols", None), P("rows"), P("cols")),
        check_vma=False,
    )
```

```python
import functools
import math

import jax
import jax.numpy as jnp
from jax import lax
from jax.experimental import pallas as pl
from jax.experimental.pallas import tpu as pltpu
from jax.sharding import PartitionSpec as P

ITERS = 3
LANES = 128
LIM = 40.0
MIB = 1024 * 1024
F32 = jnp.float32
LOG2E = math.log2(math.e)
XS, ZS = 4, 8
BLOCK = 32
PARTS = BLOCK // 8
CHUNKS = 4
XB1, XB2, ZB1, ZB2 = range(4)


def combine_lse(parts):
    top = jnp.max(parts, axis=0)
    return top + jnp.log(jnp.sum(jnp.exp(parts - top[None]), axis=0))


def lane_to_sublane(row):
    return jnp.transpose(jnp.broadcast_to(row, (LANES, LANES)))


def fold(x):
    return jnp.sum(x.reshape(x.shape[0] // 8, 8, x.shape[1]), axis=0)


def lane_group(g):
    return slice(g * LANES, (g + 1) * LANES)


def row_tile(t):
    return pl.ds(pl.multiple_of(t * LANES, LANES), LANES)


def put_copies(out_ref, value):
    for k in range(out_ref.shape[0]):
        out_ref[k] = value


def logit_block(k_ref, ok, t, g):
    block = k_ref[row_tile(t), lane_group(g)]
    return jnp.where(ok, jnp.log(block), block)


def within(peak, *pots):
    for pot in pots:
        pot = jnp.abs(pot)
        for k in range(pot.shape[0] // 8):
            peak = jnp.maximum(peak, pot[8 * k : 8 * k + 8, :])
    return jnp.max(peak) <= LIM


def row_lse_exact(k_ref, ok, pot_ref, out_ref):
    tiles, groups = k_ref.shape[0] // LANES, k_ref.shape[1] // LANES

    def shifted(t, g):
        z = logit_block(k_ref, ok, t, g)
        return z if pot_ref is None else z + lane_to_sublane(pot_ref[pl.ds(t, 1), :])

    for g in range(groups):
        def top_of(t, top, g=g):
            return jnp.maximum(top, jnp.max(shifted(t, g), axis=0, keepdims=True))

        top = lax.fori_loop(0, tiles, top_of, jnp.full((1, LANES), -3.0e38, F32))

        def sum_of(t, total, g=g, top=top):
            return total + jnp.sum(jnp.exp(shifted(t, g) - top), axis=0, keepdims=True)

        total = lax.fori_loop(0, tiles, sum_of, jnp.zeros((1, LANES), F32))
        out_ref[g : g + 1, :] = top + jnp.log(total)


def col_lse_exact(k_ref, ok, pot, out_ref):
    tiles, groups = k_ref.shape[0] // LANES, k_ref.shape[1] // LANES

    def tile(t, carry):
        top = jnp.full((LANES, LANES), -3.0e38, F32)
        for g in range(groups):
            top = jnp.maximum(top, logit_block(k_ref, ok, t, g) + pot[g : g + 1, :])
        top = jnp.broadcast_to(jnp.max(top, axis=1, keepdims=True), (LANES, LANES))
        total = jnp.zeros((LANES, LANES), F32)
        for g in range(groups):
            total = total + jnp.exp(logit_block(k_ref, ok, t, g) + pot[g : g + 1, :] - top)
        total = jnp.sum(jnp.transpose(total), axis=0, keepdims=True)
        out_ref[pl.ds(t, 1), :] = jnp.transpose(top)[0:1, :] + jnp.log(total)
        return carry

    lax.fori_loop(0, tiles, tile, 0)


def logits_kernel(cent_hbm, vec_hbm, k_ref, peak_ref, out_ref, lse_ref, cent_ref, vec_ref, sems):
    cents, rows = k_ref.shape
    groups = rows // LANES
    step, chunk = cents // CHUNKS, rows // CHUNKS

    def pieces(hbm_ref, vmem_ref, first, size):
        return [
            pltpu.make_async_copy(
                hbm_ref.at[pl.ds(c * size, size), :], vmem_ref.at[pl.ds(c * size, size), :], sems.at[first + c]
            )
            for c in range(CHUNKS)
        ]

    vec_copies = pieces(vec_hbm, vec_ref, 0, chunk)
    cent_copies = pieces(cent_hbm, cent_ref, CHUNKS, step)
    for copy in vec_copies[:1] + cent_copies + vec_copies[1:]:
        copy.start()

    def dots(c):
        vec_copies[c].wait()
        if c == 0:
            for copy in cent_copies:
                copy.wait()
        return lax.dot_general(
            cent_ref[...], vec_ref[c * chunk : (c + 1) * chunk, :],
            (((1,), (1,)), ((), ())), preferred_element_type=F32,
        )

    peak = jnp.zeros((8, LANES), F32)
    ahead = dots(0)
    for c in range(CHUNKS):
        block = ahead
        if c + 1 < CHUNKS:
            ahead = dots(c + 1)
        for g in range(chunk // LANES):
            group = c * (chunk // LANES) + g
            total = jnp.zeros((8, LANES), F32)
            for t in range(cents // LANES):
                part = block[t * LANES : (t + 1) * LANES, lane_group(g)]
                peak = jnp.maximum(peak, jnp.max(jnp.abs(part).reshape(LANES // 8, 8, LANES), axis=0))
                part = jnp.exp2(part * (4.0 * LOG2E))
                k_ref[t * LANES : (t + 1) * LANES, lane_group(group)] = part
                total = total + fold(part)
            lse_ref[group : group + 1, :] = jnp.sum(total, axis=0, keepdims=True)
    peak = 4.0 * peak
    lse_ref[...] = jnp.log(lse_ref[...])
    peak_ref[...] = peak

    @pl.when(jnp.logical_not(within(peak)))
    def _():
        def tile(t, carry):
            at = row_tile(t)
            for g in range(groups):
                k_ref[at, lane_group(g)] = 4.0 * lax.dot_general(
                    cent_ref[at, :], vec_ref[lane_group(g), :],
                    (((1,), (1,)), ((), ())), preferred_element_type=F32,
                )
            return carry

        lax.fori_loop(0, cents // LANES, tile, 0)
        row_lse_exact(k_ref, False, None, lse_ref)

    put_copies(out_ref, lse_ref[...])


def row_kernel(log_target, got_ref, peak_ref, k_ref, out_ref, pot_ref, lse_ref):
    tiles, groups = k_ref.shape[0] // LANES, k_ref.shape[1] // LANES
    pot = log_target - combine_lse(got_ref[...])
    fast = within(peak_ref[...], pot)

    @pl.when(fast)
    def _():
        scales = jnp.exp(pot)
        sums = [jnp.zeros((8, LANES), F32)] * groups
        for t in range(tiles):
            scale = lane_to_sublane(scales[t : t + 1, :])
            for g in range(groups):
                sums[g] = sums[g] + fold(k_ref[t * LANES : (t + 1) * LANES, lane_group(g)] * scale)
        for g in range(groups):
            lse_ref[g : g + 1, :] = jnp.sum(sums[g], axis=0, keepdims=True)
        lse_ref[...] = jnp.log(lse_ref[...])

    @pl.when(jnp.logical_not(fast))
    def _():
        pot_ref[...] = pot
        row_lse_exact(k_ref, within(peak_ref[...]), pot_ref, lse_ref)

    put_copies(out_ref, lse_ref[...])


def col_kernel(got_ref, peak_ref, k_ref, out_ref, lse_ref):
    tiles, groups = k_ref.shape[0] // LANES, k_ref.shape[1] // LANES
    pot = -combine_lse(got_ref[...])
    fast = within(peak_ref[...], pot)

    @pl.when(fast)
    def _():
        scale = jnp.exp(pot)

        for t in range(tiles):
            total = jnp.zeros((LANES, LANES), F32)
            for g in range(groups):
                total = total + k_ref[t * LANES : (t + 1) * LANES, lane_group(g)] * scale[g : g + 1, :]
            lse_ref[t : t + 1, :] = jnp.sum(jnp.transpose(total), axis=0, keepdims=True)
        lse_ref[...] = jnp.log(lse_ref[...])

    @pl.when(jnp.logical_not(fast))
    def _():
        col_lse_exact(k_ref, within(peak_ref[...]), pot, lse_ref)

    put_copies(out_ref, lse_ref[...])


def sums_kernel(log_target, flips, *refs):
    first_call = log_target is not None
    cols_ref, rows_ref, peak_ref, k_ref, vec_ref, a_ref, b_ref = refs[:7]
    plan_ref, scale_ref = refs[-2:]
    groups = k_ref.shape[1] // LANES
    if first_call:
        col_pot = log_target - combine_lse(cols_ref[...])
        row_pot = -combine_lse(rows_ref[...])
        for pot_ref in refs[7:9]:
            pot_ref[...] = col_pot
        for pot_ref in refs[9:11]:
            pot_ref[...] = row_pot
    else:
        col_pot, row_pot = cols_ref[...], rows_ref[...]
    fast = within(peak_ref[...], col_pot, row_pot)
    scale_ref[...] = jnp.where(fast, jnp.exp(col_pot), col_pot)
    row_scale = jnp.exp(row_pot)
    bits = position_bits()
    x1, z1 = bits[XB1], bits[ZB1]
    tiles = []
    for chain, (first, second) in enumerate(((x1, z1), (z1, x1))):
        first = 1 - first if flips[0] else first
        second = 1 - second if flips[1] else second
        tiles.append(chain * 4 + first * 2 + second)

    def plan_tile(chain, out_ref, block):
        total = jnp.zeros((LANES, LANES), F32)
        for g in range(groups):
            plan = block(g)
            total = total + plan
            plan_ref[chain * LANES : (chain + 1) * LANES, lane_group(g)] = plan.astype(jnp.bfloat16)
        mass = jnp.broadcast_to(jnp.sum(total, axis=1, keepdims=True), (LANES, LANES))
        lane = lax.broadcasted_iota(jnp.int32, (8, LANES), 1) // (LANES // PARTS)
        for b in range(LANES // BLOCK):
            unit = mass[b * BLOCK : b * BLOCK + 8, :]
            for k in range(1, PARTS):
                at = b * BLOCK + 8 * k
                unit = jnp.where(lane == k, mass[at : at + 8, :], unit)
            out_ref[b, out_ref.shape[1] - 1] = unit

    def sums():
        block = jnp.dot(plan_ref[...], vec_ref[...], preferred_element_type=F32)
        across = block.shape[1] // LANES
        for chain, out_ref in enumerate((a_ref, b_ref)):
            for b in range(LANES // BLOCK):
                for k in range(PARTS):
                    row = chain * LANES + b * BLOCK + 8 * k
                    for g in range(across):
                        out_ref[b, k * across + g] = block[row : row + 8, lane_group(g)]

    @pl.when(fast)
    def _():
        for chain, (tile, out_ref) in enumerate(zip(tiles, (a_ref, b_ref))):
            scale = lane_to_sublane(scale_ref[pl.ds(tile, 1), :])
            plan_tile(
                chain,
                out_ref,
                lambda g: k_ref[row_tile(tile), lane_group(g)] * row_scale[g : g + 1, :] * scale,
            )
        sums()

    @pl.when(jnp.logical_not(fast))
    def _():
        ok = within(peak_ref[...])
        for chain, (tile, out_ref) in enumerate(zip(tiles, (a_ref, b_ref))):
            shift = lane_to_sublane(scale_ref[pl.ds(tile, 1), :])
            plan_tile(
                chain,
                out_ref,
                lambda g: jnp.exp(logit_block(k_ref, ok, tile, g) + row_pot[g : g + 1, :] + shift),
            )
        sums()


def add_kernel(mine_ref, got_ref, out_ref):
    out_ref[...] = mine_ref[...] + got_ref[...]


def quarter_kernel(mine_a_ref, first_a_ref, second_a_ref, mine_b_ref, first_b_ref, second_b_ref, out_ref):
    for p in range(out_ref.shape[0]):
        out_ref[p, 0] = mine_a_ref[p] + first_a_ref[p] + second_a_ref[p]
        out_ref[p, 1] = mine_b_ref[p] + first_b_ref[p] + second_b_ref[p]


def four_kernel(got_ref, out_ref):
    out_ref[...] = (got_ref[0] + got_ref[1]) + (got_ref[2] + got_ref[3])


def mean_kernel(sum_ref, got_ref, out_ref):
    copies, chains, _, width = out_ref.shape
    units = sum_ref.shape[1] - 1
    across = width // LANES
    lanes = LANES // PARTS
    for chain in range(chains):
        mass = sum_ref[chain, units] + got_ref[chain, units]
        for k in range(PARTS):
            part = jnp.broadcast_to(mass[:, k * lanes : k * lanes + 1], (8, LANES))
            for g in range(across):
                u = k * across + g
                mean = (sum_ref[chain, u] + got_ref[chain, u]) / part
                for copy in range(copies):
                    out_ref[copy, chain, 8 * k : 8 * k + 8, lane_group(g)] = mean


def part_kernel(got_ref, a_ref, b_ref):
    for p in range(got_ref.shape[0]):
        at = slice(p * BLOCK, (p + 1) * BLOCK)
        a_ref[at, :] = got_ref[p, 0]
        b_ref[at, :] = got_ref[p, 1]


def place_kernel(spots, *refs):
    out_ref, sems = refs[-2:]
    bits = position_bits()
    x1, z1 = bits[XB1], bits[ZB1]
    copies = []
    for n, ((chain, flips), part_ref) in enumerate(zip(spots, refs)):
        size = part_ref.shape[0]
        first, second = (z1, x1) if chain else (x1, z1)
        first = 1 - first if flips[0] else first
        second = 1 - second if flips[1] else second
        at = pl.ds(pl.multiple_of((chain * 4 + first * 2 + second) * size, size), size)
        copies.append(pltpu.make_async_copy(part_ref, out_ref.at[at, :], sems.at[n]))
    for copy in copies:
        copy.start()
    for copy in copies:
        copy.wait()


def place(row, core):
    return (row // ZS + (XS - 1) * core) % XS, (row % ZS + (ZS - 1) * core) % ZS


def pairs(partner, n_cols):
    out = []
    for row in range(XS * ZS):
        for col in range(n_cols):
            core = col % 2
            x, z = partner(*place(row, core))
            to = (x + core) % XS * ZS + (z + core) % ZS
            out.append((row * n_cols + col, to * n_cols + col))
    return out


def exchange(x, partner):
    return lax.ppermute(x, ("rows", "cols"), pairs(partner, lax.axis_size("cols")))


def x_first(x, z):
    return x ^ 1, z


def x_second(x, z):
    return XS - 1 - x, z


def z_first(x, z):
    return x, z ^ 1


def z_second(x, z):
    return x, (z - 1 + 2 * (z % 2)) % ZS


def z_third(x, z):
    return x, {0: 3, 3: 0, 1: 6, 6: 1, 2: 5, 5: 2, 4: 7, 7: 4}[z]


def position_bits():
    core = lax.axis_index("cols") & 1
    row = lax.axis_index("rows")
    x = ((row >> 3) + (XS - 1) * core) & (XS - 1)
    z = (row + (ZS - 1) * core) & (ZS - 1)
    return (x ^ (x >> 1)) & 1, x >> 1, ((z + 1) >> 1) & 1, (0xB4 >> z) & 1


def quads(n_cols):
    groups = {}
    for row in range(XS * ZS):
        for col in range(n_cols):
            x, z = place(row, col % 2)
            key = (col, min(x, x_second(x, z)[0]), min(z, z_second(x, z)[1]))
            groups.setdefault(key, []).append(((x >> 1) * 2 + ((0xB4 >> z) & 1), row * n_cols + col))
    return [[device for _, device in sorted(groups[key])] for key in sorted(groups)]


def trade(x):
    return lax.all_to_all(
        x, ("rows", "cols"), 0, 0, tiled=True, axis_index_groups=quads(lax.axis_size("cols"))
    )


def add(mine, got):
    return pl.pallas_call(
        add_kernel,
        out_shape=jax.ShapeDtypeStruct(mine.shape, F32),
        in_specs=[vmem(), vmem()],
        out_specs=vmem(),
        compiler_params=params(4),
        name="add",
    )(mine, got)


def put(spots, parts, cents, *before):
    return pl.pallas_call(
        functools.partial(place_kernel, spots),
        out_shape=jax.ShapeDtypeStruct((cents, parts[0].shape[1]), F32),
        in_specs=[vmem()] * len(parts) + [hbm()] * len(before),
        out_specs=hbm(),
        scratch_shapes=[pltpu.SemaphoreType.DMA((len(parts),))],
        input_output_aliases={len(parts): 0} if before else {},
        compiler_params=params(4),
        name="place",
    )(*parts, *before)


def mean_over_rows(quarter_sums, cents, width):
    pass_a, pass_b = quarter_sums((True, True))
    pass_a, pass_b = exchange(pass_a, x_first), exchange(pass_b, z_first)
    stay_a, stay_b = quarter_sums((True, False))
    stay_a, stay_b = exchange(stay_a, x_first), exchange(stay_b, z_first)
    mine_a, mine_b = quarter_sums((False, True))
    next_a = exchange(add(mine_a, pass_a), z_first)
    next_b = exchange(add(mine_b, pass_b), x_first)
    mine_a, mine_b = quarter_sums((False, False))
    block = mine_a.shape[1:]
    quarter = pl.pallas_call(
        quarter_kernel,
        out_shape=jax.ShapeDtypeStruct((4, 2, *block), F32),
        in_specs=[vmem()] * 6,
        out_specs=vmem(),
        compiler_params=params(4),
        name="quarter",
    )(mine_a, stay_a, next_a, mine_b, stay_b, next_b)
    sums = pl.pallas_call(
        four_kernel,
        out_shape=jax.ShapeDtypeStruct((2, *block), F32),
        in_specs=[vmem()],
        out_specs=vmem(),
        compiler_params=params(4),
        name="four",
    )(trade(quarter))
    mean = pl.pallas_call(
        mean_kernel,
        out_shape=jax.ShapeDtypeStruct((4, 2, BLOCK, width), F32),
        in_specs=[vmem()] * 2,
        out_specs=vmem(),
        compiler_params=params(4),
        name="mean",
    )(sums, exchange(sums, z_third))
    part = jax.ShapeDtypeStruct((4 * BLOCK, width), F32)
    mine_a, mine_b = pl.pallas_call(
        part_kernel,
        out_shape=(part, part),
        in_specs=[vmem()],
        out_specs=(vmem(), vmem()),
        compiler_params=params(4),
        name="part",
    )(trade(mean))
    next_a, next_b = exchange(mine_a, z_first), exchange(mine_b, x_first)
    stay_a, stay_b = exchange(mine_a, x_first), exchange(mine_b, z_first)
    pass_a, pass_b = exchange(next_a, x_first), exchange(next_b, z_first)
    out = put(((0, (False, False)), (1, (False, False))), (mine_a, mine_b), cents)
    out = put(((0, (False, True)), (1, (False, True))), (next_a, next_b), cents, out)
    out = put(((0, (True, False)), (1, (True, False))), (stay_a, stay_b), cents, out)
    return put(((0, (True, True)), (1, (True, True))), (pass_a, pass_b), cents, out)


def vmem():
    return pl.BlockSpec(memory_space=pltpu.VMEM)


def hbm():
    return pl.BlockSpec(memory_space=pltpu.HBM)


def pinned(x):
    return pltpu.with_memory_space_constraint(x, pltpu.VMEM)


def params(mib):
    return pltpu.CompilerParams(vmem_limit_bytes=mib * MIB)


def per_device(vectors, centroids):
    n_rows, n_cols = lax.axis_size("rows"), lax.axis_size("cols")
    rows, width = vectors.shape
    cents = centroids.shape[0]
    log_target = math.log(rows * n_rows / (cents * n_cols))
    groups, tiles = rows // LANES, cents // LANES
    kept = pltpu.VMEM((cents, rows), F32)
    peak_type = jax.ShapeDtypeStruct((8, LANES), F32)
    row_parts = jax.ShapeDtypeStruct((n_cols, groups, LANES), F32)
    col_parts = jax.ShapeDtypeStruct((n_rows, tiles, LANES), F32)
    row_scratch = pltpu.VMEM((groups, LANES), F32)
    col_scratch = pltpu.VMEM((tiles, LANES), F32)

    kernel, peak, part = pl.pallas_call(
        logits_kernel,
        out_shape=(kept, peak_type, row_parts),
        in_specs=[hbm(), hbm()],
        out_specs=(vmem(), vmem(), vmem()),
        scratch_shapes=[
            row_scratch,
            pltpu.VMEM((cents, width), jnp.bfloat16),
            pltpu.VMEM((rows, width), jnp.bfloat16),
            pltpu.SemaphoreType.DMA((2 * CHUNKS,)),
        ],
        compiler_params=params(24),
        name="logits",
    )(*(pltpu.with_memory_space_constraint(x, pltpu.HBM) for x in (centroids, vectors)))

    for step in range(ITERS):
        row_got = lax.all_to_all(part, "cols", 0, 0, tiled=True)
        part = pl.pallas_call(
            col_kernel,
            out_shape=col_parts,
            in_specs=[vmem(), vmem(), vmem()],
            out_specs=vmem(),
            scratch_shapes=[col_scratch],
            compiler_params=params(4),
            name="col_step",
        )(row_got, peak, pinned(kernel))
        col_got = lax.all_to_all(part, "rows", 0, 0, tiled=True)
        part = pl.pallas_call(
            functools.partial(row_kernel, log_target),
            out_shape=row_parts,
            in_specs=[vmem(), vmem(), vmem()],
            out_specs=vmem(),
            scratch_shapes=[col_scratch, row_scratch],
            compiler_params=params(4),
            name="row_step",
        )(col_got, peak, pinned(kernel))
    row_got = lax.all_to_all(part, "cols", 0, 0, tiled=True)

    quarter = jax.ShapeDtypeStruct((LANES // BLOCK, PARTS * (width // LANES) + 1, 8, LANES), F32)
    pots = []

    def quarter_sums(flips):
        first = not pots
        pot_types = tuple(jax.ShapeDtypeStruct((n, LANES), F32) for n in (tiles, tiles, groups, groups))
        a, b, *new = pl.pallas_call(
            functools.partial(sums_kernel, log_target if first else None, flips),
            out_shape=(quarter, quarter) + (pot_types if first else ()),
            in_specs=[vmem()] * 5,
            out_specs=(vmem(),) * (6 if first else 2),
            scratch_shapes=[pltpu.VMEM((2 * LANES, rows), jnp.bfloat16), col_scratch],
            compiler_params=params(8),
            cost_estimate=pl.CostEstimate(
                flops=rows * cents * width // 2, bytes_accessed=4 * MIB, transcendentals=0
            ),
            name="sums",
        )(*(pots[1::2] or (col_got, row_got)), peak, pinned(kernel), vectors)
        pots.extend(new)
        return a, b

    new_centroids = mean_over_rows(quarter_sums, cents, width)
    col_pot, row_pot = pots[0::2]
    return (new_centroids, row_pot.reshape(rows), col_pot.reshape(cents))


def solution(mesh):
    return jax.shard_map(
        per_device,
        mesh=mesh,
        in_specs=(P("rows", None), P("cols", None)),
        out_specs=(P("cols", None), P("rows"), P("cols")),
        check_vma=False,
    )
```

```python
import functools
import math

import jax
import jax.numpy as jnp
from jax import lax
from jax.experimental import pallas as pl
from jax.experimental.pallas import tpu as pltpu
from jax.sharding import PartitionSpec as P

ITERS = 3
LANES = 128
LIM = 40.0
MIB = 1024 * 1024
F32 = jnp.float32
LOG2E = math.log2(math.e)
XS, ZS = 4, 8
BLOCK = 32
PARTS = BLOCK // 8
CHUNKS = 4
XB1, XB2, ZB1, ZB2 = range(4)


def combine_lse(parts):
    top = jnp.max(parts, axis=0)
    return top + jnp.log(jnp.sum(jnp.exp(parts - top[None]), axis=0))


def lane_to_sublane(row):
    return jnp.transpose(jnp.broadcast_to(row, (LANES, LANES)))


def fold(x):
    return jnp.sum(x.reshape(x.shape[0] // 8, 8, x.shape[1]), axis=0)


def lane_group(g):
    return slice(g * LANES, (g + 1) * LANES)


def row_tile(t):
    return pl.ds(pl.multiple_of(t * LANES, LANES), LANES)


def put_copies(out_ref, value):
    for k in range(out_ref.shape[0]):
        out_ref[k] = value


def logit_block(k_ref, ok, t, g):
    block = k_ref[row_tile(t), lane_group(g)]
    return jnp.where(ok, jnp.log(block), block)


def within(peak, *pots):
    for pot in pots:
        pot = jnp.abs(pot)
        for k in range(pot.shape[0] // 8):
            peak = jnp.maximum(peak, pot[8 * k : 8 * k + 8, :])
    return jnp.max(peak) <= LIM


def row_lse_exact(k_ref, ok, pot_ref, out_ref):
    tiles, groups = k_ref.shape[0] // LANES, k_ref.shape[1] // LANES

    def shifted(t, g):
        z = logit_block(k_ref, ok, t, g)
        return z if pot_ref is None else z + lane_to_sublane(pot_ref[pl.ds(t, 1), :])

    for g in range(groups):
        def top_of(t, top, g=g):
            return jnp.maximum(top, jnp.max(shifted(t, g), axis=0, keepdims=True))

        top = lax.fori_loop(0, tiles, top_of, jnp.full((1, LANES), -3.0e38, F32))

        def sum_of(t, total, g=g, top=top):
            return total + jnp.sum(jnp.exp(shifted(t, g) - top), axis=0, keepdims=True)

        total = lax.fori_loop(0, tiles, sum_of, jnp.zeros((1, LANES), F32))
        out_ref[g : g + 1, :] = top + jnp.log(total)


def col_lse_exact(k_ref, ok, pot, out_ref):
    tiles, groups = k_ref.shape[0] // LANES, k_ref.shape[1] // LANES

    def tile(t, carry):
        top = jnp.full((LANES, LANES), -3.0e38, F32)
        for g in range(groups):
            top = jnp.maximum(top, logit_block(k_ref, ok, t, g) + pot[g : g + 1, :])
        top = jnp.broadcast_to(jnp.max(top, axis=1, keepdims=True), (LANES, LANES))
        total = jnp.zeros((LANES, LANES), F32)
        for g in range(groups):
            total = total + jnp.exp(logit_block(k_ref, ok, t, g) + pot[g : g + 1, :] - top)
        total = jnp.sum(jnp.transpose(total), axis=0, keepdims=True)
        out_ref[pl.ds(t, 1), :] = jnp.transpose(top)[0:1, :] + jnp.log(total)
        return carry

    lax.fori_loop(0, tiles, tile, 0)


def logits_kernel(cent_hbm, vec_hbm, k_ref, peak_ref, out_ref, lse_ref, cent_ref, vec_ref, sems):
    cents, rows = k_ref.shape
    groups = rows // LANES
    step, chunk = cents // CHUNKS, rows // CHUNKS

    def pieces(hbm_ref, vmem_ref, first, size):
        return [
            pltpu.make_async_copy(
                hbm_ref.at[pl.ds(c * size, size), :], vmem_ref.at[pl.ds(c * size, size), :], sems.at[first + c]
            )
            for c in range(CHUNKS)
        ]

    vec_copies = pieces(vec_hbm, vec_ref, 0, chunk)
    cent_copies = pieces(cent_hbm, cent_ref, CHUNKS, step)
    for copy in vec_copies[:1] + cent_copies + vec_copies[1:]:
        copy.start()

    def dots(c):
        vec_copies[c].wait()
        if c == 0:
            for copy in cent_copies:
                copy.wait()
        return lax.dot_general(
            cent_ref[...], vec_ref[c * chunk : (c + 1) * chunk, :],
            (((1,), (1,)), ((), ())), preferred_element_type=F32,
        )

    peak = jnp.zeros((8, LANES), F32)
    ahead = dots(0)
    for c in range(CHUNKS):
        block = ahead
        if c + 1 < CHUNKS:
            ahead = dots(c + 1)
        for g in range(chunk // LANES):
            group = c * (chunk // LANES) + g
            total = jnp.zeros((8, LANES), F32)
            for t in range(cents // LANES):
                part = block[t * LANES : (t + 1) * LANES, lane_group(g)]
                peak = jnp.maximum(peak, jnp.max(jnp.abs(part).reshape(LANES // 8, 8, LANES), axis=0))
                part = jnp.exp2(part * (4.0 * LOG2E))
                k_ref[t * LANES : (t + 1) * LANES, lane_group(group)] = part
                total = total + fold(part)
            lse_ref[group : group + 1, :] = jnp.sum(total, axis=0, keepdims=True)
    peak = 4.0 * peak
    lse_ref[...] = jnp.log(lse_ref[...])
    peak_ref[...] = peak

    @pl.when(jnp.logical_not(within(peak)))
    def _():
        def tile(t, carry):
            at = row_tile(t)
            for g in range(groups):
                k_ref[at, lane_group(g)] = 4.0 * lax.dot_general(
                    cent_ref[at, :], vec_ref[lane_group(g), :],
                    (((1,), (1,)), ((), ())), preferred_element_type=F32,
                )
            return carry

        lax.fori_loop(0, cents // LANES, tile, 0)
        row_lse_exact(k_ref, False, None, lse_ref)

    put_copies(out_ref, lse_ref[...])


def row_kernel(log_target, got_ref, peak_ref, k_ref, out_ref, pot_ref, lse_ref):
    tiles, groups = k_ref.shape[0] // LANES, k_ref.shape[1] // LANES
    pot = log_target - combine_lse(got_ref[...])
    fast = within(peak_ref[...], pot)

    scales = jnp.exp(pot)
    sums = [jnp.zeros((8, LANES), F32)] * groups
    for t in range(tiles):
        scale = lane_to_sublane(scales[t : t + 1, :])
        for g in range(groups):
            sums[g] = sums[g] + fold(k_ref[t * LANES : (t + 1) * LANES, lane_group(g)] * scale)
    for g in range(groups):
        lse_ref[g : g + 1, :] = jnp.sum(sums[g], axis=0, keepdims=True)
    lse_ref[...] = jnp.log(lse_ref[...])

    @pl.when(jnp.logical_not(fast))
    def _():
        pot_ref[...] = pot
        row_lse_exact(k_ref, within(peak_ref[...]), pot_ref, lse_ref)

    put_copies(out_ref, lse_ref[...])


def col_kernel(got_ref, peak_ref, k_ref, out_ref, lse_ref):
    tiles, groups = k_ref.shape[0] // LANES, k_ref.shape[1] // LANES
    pot = -combine_lse(got_ref[...])
    fast = within(peak_ref[...], pot)

    scale = jnp.exp(pot)
    for t in range(tiles):
        total = jnp.zeros((LANES, LANES), F32)
        for g in range(groups):
            total = total + k_ref[t * LANES : (t + 1) * LANES, lane_group(g)] * scale[g : g + 1, :]
        lse_ref[t : t + 1, :] = jnp.sum(jnp.transpose(total), axis=0, keepdims=True)
    lse_ref[...] = jnp.log(lse_ref[...])

    @pl.when(jnp.logical_not(fast))
    def _():
        col_lse_exact(k_ref, within(peak_ref[...]), pot, lse_ref)

    put_copies(out_ref, lse_ref[...])


def sums_kernel(log_target, flips, *refs):
    first_call = log_target is not None
    cols_ref, rows_ref, peak_ref, k_ref, vec_ref, a_ref, b_ref = refs[:7]
    plan_ref, scale_ref = refs[-2:]
    groups = k_ref.shape[1] // LANES
    if first_call:
        col_pot = log_target - combine_lse(cols_ref[...])
        row_pot = -combine_lse(rows_ref[...])
        for pot_ref in refs[7:9]:
            pot_ref[...] = col_pot
        for pot_ref in refs[9:11]:
            pot_ref[...] = row_pot
    else:
        col_pot, row_pot = cols_ref[...], rows_ref[...]
    fast = within(peak_ref[...], col_pot, row_pot)
    scale_ref[...] = jnp.exp(col_pot)
    row_scale = jnp.exp(row_pot)
    bits = position_bits()
    x1, z1 = bits[XB1], bits[ZB1]
    tiles = []
    for chain, (first, second) in enumerate(((x1, z1), (z1, x1))):
        first = 1 - first if flips[0] else first
        second = 1 - second if flips[1] else second
        tiles.append(chain * 4 + first * 2 + second)

    def plan_tile(chain, out_ref, block):
        total = jnp.zeros((LANES, LANES), F32)
        for g in range(groups):
            plan = block(g)
            total = total + plan
            plan_ref[chain * LANES : (chain + 1) * LANES, lane_group(g)] = plan.astype(jnp.bfloat16)
        mass = jnp.broadcast_to(jnp.sum(total, axis=1, keepdims=True), (LANES, LANES))
        lane = lax.broadcasted_iota(jnp.int32, (8, LANES), 1) // (LANES // PARTS)
        for b in range(LANES // BLOCK):
            unit = mass[b * BLOCK : b * BLOCK + 8, :]
            for k in range(1, PARTS):
                at = b * BLOCK + 8 * k
                unit = jnp.where(lane == k, mass[at : at + 8, :], unit)
            out_ref[b, out_ref.shape[1] - 1] = unit

    def sums():
        block = jnp.dot(plan_ref[...], vec_ref[...], preferred_element_type=F32)
        across = block.shape[1] // LANES
        for chain, out_ref in enumerate((a_ref, b_ref)):
            for b in range(LANES // BLOCK):
                for k in range(PARTS):
                    row = chain * LANES + b * BLOCK + 8 * k
                    for g in range(across):
                        out_ref[b, k * across + g] = block[row : row + 8, lane_group(g)]

    for chain, (tile, out_ref) in enumerate(zip(tiles, (a_ref, b_ref))):
        scale = lane_to_sublane(scale_ref[pl.ds(tile, 1), :])
        plan_tile(
            chain,
            out_ref,
            lambda g: k_ref[row_tile(tile), lane_group(g)] * row_scale[g : g + 1, :] * scale,
        )
    sums()

    @pl.when(jnp.logical_not(fast))
    def _():
        ok = within(peak_ref[...])
        scale_ref[...] = col_pot
        for chain, (tile, out_ref) in enumerate(zip(tiles, (a_ref, b_ref))):
            shift = lane_to_sublane(scale_ref[pl.ds(tile, 1), :])
            plan_tile(
                chain,
                out_ref,
                lambda g: jnp.exp(logit_block(k_ref, ok, tile, g) + row_pot[g : g + 1, :] + shift),
            )
        sums()


def add_kernel(mine_ref, got_ref, out_ref):
    out_ref[...] = mine_ref[...] + got_ref[...]


def spot(flips):
    bits = position_bits()
    x2, z2 = bits[XB2], bits[ZB2]
    return (1 - x2 if flips[0] else x2) * 2 + (1 - z2 if flips[1] else z2)


def pieces_kernel(order, mine_ref, first_ref, second_ref, *out_refs):
    for flips, out_ref in zip(order, out_refs):
        at = spot(flips)
        out_ref[...] = mine_ref[at] + first_ref[at] + second_ref[at]


def own_kernel(mine_ref, first_ref, second_ref, out_ref):
    out_ref[...] = mine_ref[...] + first_ref[...] + second_ref[...]


def mean_kernel(sum_ref, got_ref, out_ref):
    units = sum_ref.shape[0] - 1
    across = out_ref.shape[1] // LANES
    lanes = LANES // PARTS
    mass = sum_ref[units] + got_ref[units]
    for k in range(PARTS):
        part = jnp.broadcast_to(mass[:, k * lanes : k * lanes + 1], (8, LANES))
        for g in range(across):
            u = k * across + g
            out_ref[8 * k : 8 * k + 8, lane_group(g)] = (sum_ref[u] + got_ref[u]) / part


def join_kernel(order, *refs):
    out_ref = refs[-1]
    for flips, part_ref in zip(order, refs):
        at = pl.ds(pl.multiple_of(spot(flips) * BLOCK, BLOCK), BLOCK)
        out_ref[at, :] = part_ref[...]


def place_kernel(spots, *refs):
    out_ref, sems = refs[-2:]
    bits = position_bits()
    x1, z1 = bits[XB1], bits[ZB1]
    copies = []
    for n, ((chain, flips), part_ref) in enumerate(zip(spots, refs)):
        size = part_ref.shape[0]
        first, second = (z1, x1) if chain else (x1, z1)
        first = 1 - first if flips[0] else first
        second = 1 - second if flips[1] else second
        at = pl.ds(pl.multiple_of((chain * 4 + first * 2 + second) * size, size), size)
        copies.append(pltpu.make_async_copy(part_ref, out_ref.at[at, :], sems.at[n]))
    for copy in copies:
        copy.start()
    for copy in copies:
        copy.wait()


def place(row, core):
    return (row // ZS + (XS - 1) * core) % XS, (row % ZS + (ZS - 1) * core) % ZS


def pairs(partner, n_cols):
    out = []
    for row in range(XS * ZS):
        for col in range(n_cols):
            core = col % 2
            x, z = partner(*place(row, core))
            to = (x + core) % XS * ZS + (z + core) % ZS
            out.append((row * n_cols + col, to * n_cols + col))
    return out


def exchange(x, partner):
    return lax.ppermute(x, ("rows", "cols"), pairs(partner, lax.axis_size("cols")))


def x_first(x, z):
    return x ^ 1, z


def x_second(x, z):
    return XS - 1 - x, z


def z_first(x, z):
    return x, z ^ 1


def z_second(x, z):
    return x, (z - 1 + 2 * (z % 2)) % ZS


def z_third(x, z):
    return x, {0: 3, 3: 0, 1: 6, 6: 1, 2: 5, 5: 2, 4: 7, 7: 4}[z]


def position_bits():
    core = lax.axis_index("cols") & 1
    row = lax.axis_index("rows")
    x = ((row >> 3) + (XS - 1) * core) & (XS - 1)
    z = (row + (ZS - 1) * core) & (ZS - 1)
    return (x ^ (x >> 1)) & 1, x >> 1, ((z + 1) >> 1) & 1, (0xB4 >> z) & 1


def add(mine, got):
    return pl.pallas_call(
        add_kernel,
        out_shape=jax.ShapeDtypeStruct(mine.shape, F32),
        in_specs=[vmem(), vmem()],
        out_specs=vmem(),
        compiler_params=params(4),
        name="add",
    )(mine, got)


def put(spots, parts, cents, *before):
    return pl.pallas_call(
        functools.partial(place_kernel, spots),
        out_shape=jax.ShapeDtypeStruct((cents, parts[0].shape[1]), F32),
        in_specs=[vmem()] * len(parts) + [hbm()] * len(before),
        out_specs=hbm(),
        scratch_shapes=[pltpu.SemaphoreType.DMA((len(parts),))],
        input_output_aliases={len(parts): 0} if before else {},
        compiler_params=params(4),
        name="place",
    )(*parts, *before)


A_ORDER = ((True, True), (True, False), (False, True), (False, False))
B_ORDER = ((True, True), (False, True), (True, False), (False, False))


def sum_of_four(order, first, second, *terms):
    piece = jax.ShapeDtypeStruct(terms[0].shape[1:], F32)
    away, stay, hold, own = pl.pallas_call(
        functools.partial(pieces_kernel, order),
        out_shape=(piece,) * 4,
        in_specs=[vmem()] * 3,
        out_specs=(vmem(),) * 4,
        compiler_params=params(4),
        name="pieces",
    )(*terms)
    away, stay = exchange(away, first), exchange(stay, first)
    return pl.pallas_call(
        own_kernel,
        out_shape=piece,
        in_specs=[vmem()] * 3,
        out_specs=vmem(),
        compiler_params=params(4),
        name="own",
    )(own, stay, exchange(add(hold, away), second))


def mean_of_four(order, first, second, mine, got, width):
    mean = pl.pallas_call(
        mean_kernel,
        out_shape=jax.ShapeDtypeStruct((BLOCK, width), F32),
        in_specs=[vmem()] * 2,
        out_specs=vmem(),
        compiler_params=params(4),
        name="mean",
    )(mine, got)
    hold, stay = exchange(mean, second), exchange(mean, first)
    away = exchange(hold, first)
    return pl.pallas_call(
        functools.partial(join_kernel, order),
        out_shape=jax.ShapeDtypeStruct((4 * BLOCK, width), F32),
        in_specs=[vmem()] * 4,
        out_specs=vmem(),
        compiler_params=params(4),
        name="join",
    )(away, stay, hold, mean)


def mean_over_rows(quarter_sums, cents, width):
    pass_a, pass_b = quarter_sums((True, True))
    pass_a, pass_b = exchange(pass_a, x_first), exchange(pass_b, z_first)
    stay_a, stay_b = quarter_sums((True, False))
    stay_a, stay_b = exchange(stay_a, x_first), exchange(stay_b, z_first)
    mine_a, mine_b = quarter_sums((False, True))
    next_a = exchange(add(mine_a, pass_a), z_first)
    next_b = exchange(add(mine_b, pass_b), x_first)
    mine_a, mine_b = quarter_sums((False, False))
    mine_a = sum_of_four(A_ORDER, x_second, z_second, mine_a, stay_a, next_a)
    mine_b = sum_of_four(B_ORDER, z_second, x_second, mine_b, stay_b, next_b)
    got_a, got_b = exchange(mine_a, z_third), exchange(mine_b, z_third)
    mine_a = mean_of_four(A_ORDER, x_second, z_second, mine_a, got_a, width)
    mine_b = mean_of_four(B_ORDER, z_second, x_second, mine_b, got_b, width)
    next_a, next_b = exchange(mine_a, z_first), exchange(mine_b, x_first)
    stay_a, stay_b = exchange(mine_a, x_first), exchange(mine_b, z_first)
    pass_a, pass_b = exchange(next_a, x_first), exchange(next_b, z_first)
    out = put(((0, (False, False)), (1, (False, False))), (mine_a, mine_b), cents)
    out = put(((0, (False, True)), (1, (False, True))), (next_a, next_b), cents, out)
    out = put(((0, (True, False)), (1, (True, False))), (stay_a, stay_b), cents, out)
    return put(((0, (True, True)), (1, (True, True))), (pass_a, pass_b), cents, out)


def vmem():
    return pl.BlockSpec(memory_space=pltpu.VMEM)


def hbm():
    return pl.BlockSpec(memory_space=pltpu.HBM)


def pinned(x):
    return pltpu.with_memory_space_constraint(x, pltpu.VMEM)


def params(mib):
    return pltpu.CompilerParams(vmem_limit_bytes=mib * MIB)


def per_device(vectors, centroids):
    n_rows, n_cols = lax.axis_size("rows"), lax.axis_size("cols")
    rows, width = vectors.shape
    cents = centroids.shape[0]
    log_target = math.log(rows * n_rows / (cents * n_cols))
    groups, tiles = rows // LANES, cents // LANES
    kept = pltpu.VMEM((cents, rows), F32)
    peak_type = jax.ShapeDtypeStruct((8, LANES), F32)
    row_parts = jax.ShapeDtypeStruct((n_cols, groups, LANES), F32)
    col_parts = jax.ShapeDtypeStruct((n_rows, tiles, LANES), F32)
    row_scratch = pltpu.VMEM((groups, LANES), F32)
    col_scratch = pltpu.VMEM((tiles, LANES), F32)

    kernel, peak, part = pl.pallas_call(
        logits_kernel,
        out_shape=(kept, peak_type, row_parts),
        in_specs=[hbm(), hbm()],
        out_specs=(vmem(), vmem(), vmem()),
        scratch_shapes=[
            row_scratch,
            pltpu.VMEM((cents, width), jnp.bfloat16),
            pltpu.VMEM((rows, width), jnp.bfloat16),
            pltpu.SemaphoreType.DMA((2 * CHUNKS,)),
        ],
        compiler_params=params(24),
        name="logits",
    )(*(pltpu.with_memory_space_constraint(x, pltpu.HBM) for x in (centroids, vectors)))

    for step in range(ITERS):
        row_got = lax.all_to_all(part, "cols", 0, 0, tiled=True)
        part = pl.pallas_call(
            col_kernel,
            out_shape=col_parts,
            in_specs=[vmem(), vmem(), vmem()],
            out_specs=vmem(),
            scratch_shapes=[col_scratch],
            compiler_params=params(4),
            name="col_step",
        )(row_got, peak, pinned(kernel))
        col_got = lax.all_to_all(part, "rows", 0, 0, tiled=True)
        part = pl.pallas_call(
            functools.partial(row_kernel, log_target),
            out_shape=row_parts,
            in_specs=[vmem(), vmem(), vmem()],
            out_specs=vmem(),
            scratch_shapes=[col_scratch, row_scratch],
            compiler_params=params(4),
            name="row_step",
        )(col_got, peak, pinned(kernel))
    row_got = lax.all_to_all(part, "cols", 0, 0, tiled=True)

    quarter = jax.ShapeDtypeStruct((LANES // BLOCK, PARTS * (width // LANES) + 1, 8, LANES), F32)
    pots = []

    def quarter_sums(flips):
        first = not pots
        pot_types = tuple(jax.ShapeDtypeStruct((n, LANES), F32) for n in (tiles, tiles, groups, groups))
        a, b, *new = pl.pallas_call(
            functools.partial(sums_kernel, log_target if first else None, flips),
            out_shape=(quarter, quarter) + (pot_types if first else ()),
            in_specs=[vmem()] * 5,
            out_specs=(vmem(),) * (6 if first else 2),
            scratch_shapes=[pltpu.VMEM((2 * LANES, rows), jnp.bfloat16), col_scratch],
            compiler_params=params(8),
            cost_estimate=pl.CostEstimate(
                flops=rows * cents * width // 2, bytes_accessed=4 * MIB, transcendentals=0
            ),
            name="sums",
        )(*(pots[1::2] or (col_got, row_got)), peak, pinned(kernel), vectors)
        pots.extend(new)
        return a, b

    new_centroids = mean_over_rows(quarter_sums, cents, width)
    col_pot, row_pot = pots[0::2]
    return (new_centroids, row_pot.reshape(rows), col_pot.reshape(cents))


def solution(mesh):
    return jax.shard_map(
        per_device,
        mesh=mesh,
        in_specs=(P("rows", None), P("cols", None)),
        out_specs=(P("cols", None), P("rows"), P("cols")),
        check_vma=False,
    )
```

```python
import functools
import math

import jax
import jax.numpy as jnp
from jax import lax
from jax.experimental import pallas as pl
from jax.experimental.pallas import tpu as pltpu
from jax.sharding import PartitionSpec as P

ITERS = 3
LANES = 128
LIM = 40.0
MIB = 1024 * 1024
F32 = jnp.float32
LOG2E = math.log2(math.e)
XS, ZS = 4, 8
BLOCK = 32
PARTS = BLOCK // 8
CHUNKS = 4
XB1, XB2, ZB1, ZB2 = range(4)


def combine_lse(parts):
    top = jnp.max(parts, axis=0)
    return top + jnp.log(jnp.sum(jnp.exp(parts - top[None]), axis=0))


def lane_to_sublane(row):
    return jnp.transpose(jnp.broadcast_to(row, (LANES, LANES)))


def fold(x):
    return jnp.sum(x.reshape(x.shape[0] // 8, 8, x.shape[1]), axis=0)


def lane_group(g):
    return slice(g * LANES, (g + 1) * LANES)


def row_tile(t):
    return pl.ds(pl.multiple_of(t * LANES, LANES), LANES)


def put_copies(out_ref, value):
    for k in range(out_ref.shape[0]):
        out_ref[k] = value


def lane_tile(g):
    return pl.ds(pl.multiple_of(g * LANES, LANES), LANES)


def logit_block(k_ref, ok, t, g):
    block = k_ref[row_tile(t), lane_tile(g)]
    return jnp.where(ok, jnp.log(block), block)


def within(peak, *pots):
    for pot in pots:
        pot = jnp.abs(pot)
        for k in range(pot.shape[0] // 8):
            peak = jnp.maximum(peak, pot[8 * k : 8 * k + 8, :])
    return jnp.max(peak) <= LIM


def row_lse_exact(k_ref, ok, pot_ref, out_ref):
    tiles, groups = k_ref.shape[0] // LANES, k_ref.shape[1] // LANES

    def group(g, carry):
        def shifted(t):
            z = logit_block(k_ref, ok, t, g)
            return z if pot_ref is None else z + lane_to_sublane(pot_ref[pl.ds(t, 1), :])

        def top_of(t, top):
            return jnp.maximum(top, jnp.max(shifted(t), axis=0, keepdims=True))

        top = lax.fori_loop(0, tiles, top_of, jnp.full((1, LANES), -3.0e38, F32))

        def sum_of(t, total):
            return total + jnp.sum(jnp.exp(shifted(t) - top), axis=0, keepdims=True)

        total = lax.fori_loop(0, tiles, sum_of, jnp.zeros((1, LANES), F32))
        out_ref[pl.ds(g, 1), :] = top + jnp.log(total)
        return carry

    lax.fori_loop(0, groups, group, 0)


def col_lse_exact(k_ref, ok, pot_ref, out_ref):
    tiles, groups = k_ref.shape[0] // LANES, k_ref.shape[1] // LANES

    def tile(t, carry):
        def shifted(g):
            return logit_block(k_ref, ok, t, g) + pot_ref[pl.ds(g, 1), :]

        def top_of(g, top):
            return jnp.maximum(top, shifted(g))

        top = lax.fori_loop(0, groups, top_of, jnp.full((LANES, LANES), -3.0e38, F32))
        top = jnp.broadcast_to(jnp.max(top, axis=1, keepdims=True), (LANES, LANES))

        def sum_of(g, total):
            return total + jnp.exp(shifted(g) - top)

        total = lax.fori_loop(0, groups, sum_of, jnp.zeros((LANES, LANES), F32))
        total = jnp.sum(jnp.transpose(total), axis=0, keepdims=True)
        out_ref[pl.ds(t, 1), :] = jnp.transpose(top)[0:1, :] + jnp.log(total)
        return carry

    lax.fori_loop(0, tiles, tile, 0)


def logits_kernel(cent_hbm, vec_hbm, k_ref, peak_ref, out_ref, lse_ref, cent_ref, vec_ref, sems):
    cents, rows = k_ref.shape
    groups = rows // LANES
    step, chunk = cents // CHUNKS, rows // CHUNKS

    def pieces(hbm_ref, vmem_ref, first, size):
        return [
            pltpu.make_async_copy(
                hbm_ref.at[pl.ds(c * size, size), :], vmem_ref.at[pl.ds(c * size, size), :], sems.at[first + c]
            )
            for c in range(CHUNKS)
        ]

    vec_copies = pieces(vec_hbm, vec_ref, 0, chunk)
    cent_copies = pieces(cent_hbm, cent_ref, CHUNKS, step)
    for copy in vec_copies[:1] + cent_copies + vec_copies[1:]:
        copy.start()

    def dots(c):
        vec_copies[c].wait()
        if c == 0:
            for copy in cent_copies:
                copy.wait()
        return lax.dot_general(
            cent_ref[...], vec_ref[c * chunk : (c + 1) * chunk, :],
            (((1,), (1,)), ((), ())), preferred_element_type=F32,
        )

    peak = jnp.zeros((8, LANES), F32)
    ahead = dots(0)
    for c in range(CHUNKS):
        block = ahead
        if c + 1 < CHUNKS:
            ahead = dots(c + 1)
        for g in range(chunk // LANES):
            group = c * (chunk // LANES) + g
            total = jnp.zeros((8, LANES), F32)
            for t in range(cents // LANES):
                part = block[t * LANES : (t + 1) * LANES, lane_group(g)]
                peak = jnp.maximum(peak, jnp.max(jnp.abs(part).reshape(LANES // 8, 8, LANES), axis=0))
                part = jnp.exp2(part * (4.0 * LOG2E))
                k_ref[t * LANES : (t + 1) * LANES, lane_group(group)] = part
                total = total + fold(part)
            lse_ref[group : group + 1, :] = jnp.sum(total, axis=0, keepdims=True)
    peak = 4.0 * peak
    lse_ref[...] = jnp.log(lse_ref[...])
    peak_ref[...] = peak

    @pl.when(jnp.logical_not(within(peak)))
    def _():
        def tile(t, carry):
            def group(g, carry):
                k_ref[row_tile(t), lane_tile(g)] = 4.0 * lax.dot_general(
                    cent_ref[row_tile(t), :], vec_ref[row_tile(g), :],
                    (((1,), (1,)), ((), ())), preferred_element_type=F32,
                )
                return carry

            return lax.fori_loop(0, groups, group, carry)

        lax.fori_loop(0, cents // LANES, tile, 0)
        row_lse_exact(k_ref, False, None, lse_ref)

    put_copies(out_ref, lse_ref[...])


def row_kernel(log_target, got_ref, peak_ref, k_ref, out_ref, pot_ref, lse_ref):
    tiles, groups = k_ref.shape[0] // LANES, k_ref.shape[1] // LANES
    pot = log_target - combine_lse(got_ref[...])
    fast = within(peak_ref[...], pot)

    scales = jnp.exp(pot)
    sums = [jnp.zeros((8, LANES), F32)] * groups
    for t in range(tiles):
        scale = lane_to_sublane(scales[t : t + 1, :])
        for g in range(groups):
            sums[g] = sums[g] + fold(k_ref[t * LANES : (t + 1) * LANES, lane_group(g)] * scale)
    for g in range(groups):
        lse_ref[g : g + 1, :] = jnp.sum(sums[g], axis=0, keepdims=True)
    lse_ref[...] = jnp.log(lse_ref[...])

    @pl.when(jnp.logical_not(fast))
    def _():
        pot_ref[...] = pot
        row_lse_exact(k_ref, within(peak_ref[...]), pot_ref, lse_ref)

    put_copies(out_ref, lse_ref[...])


def col_kernel(got_ref, peak_ref, k_ref, out_ref, lse_ref, pot_ref):
    tiles, groups = k_ref.shape[0] // LANES, k_ref.shape[1] // LANES
    pot = -combine_lse(got_ref[...])
    fast = within(peak_ref[...], pot)

    scale = jnp.exp(pot)
    for t in range(tiles):
        total = jnp.zeros((LANES, LANES), F32)
        for g in range(groups):
            total = total + k_ref[t * LANES : (t + 1) * LANES, lane_group(g)] * scale[g : g + 1, :]
        lse_ref[t : t + 1, :] = jnp.sum(jnp.transpose(total), axis=0, keepdims=True)
    lse_ref[...] = jnp.log(lse_ref[...])

    @pl.when(jnp.logical_not(fast))
    def _():
        pot_ref[...] = pot
        col_lse_exact(k_ref, within(peak_ref[...]), pot_ref, lse_ref)

    put_copies(out_ref, lse_ref[...])


def sums_kernel(log_target, flips, *refs):
    first_call = log_target is not None
    cols_ref, rows_ref, peak_ref, k_ref, vec_ref, a_ref, b_ref = refs[:7]
    plan_ref, col_ref, row_ref = refs[-3:]
    groups = k_ref.shape[1] // LANES
    if first_call:
        col_pot = log_target - combine_lse(cols_ref[...])
        row_pot = -combine_lse(rows_ref[...])
        for pot_ref in refs[7:9]:
            pot_ref[...] = col_pot
        for pot_ref in refs[9:11]:
            pot_ref[...] = row_pot
    else:
        col_pot, row_pot = cols_ref[...], rows_ref[...]
    fast = within(peak_ref[...], col_pot, row_pot)
    col_ref[...] = jnp.exp(col_pot)
    row_scale = jnp.exp(row_pot)
    bits = position_bits()
    x1, z1 = bits[XB1], bits[ZB1]
    tiles = []
    for chain, (first, second) in enumerate(((x1, z1), (z1, x1))):
        first = 1 - first if flips[0] else first
        second = 1 - second if flips[1] else second
        tiles.append(chain * 4 + first * 2 + second)

    def put_mass(total, out_ref):
        mass = jnp.broadcast_to(jnp.sum(total, axis=1, keepdims=True), (LANES, LANES))
        lane = lax.broadcasted_iota(jnp.int32, (8, LANES), 1) // (LANES // PARTS)
        for b in range(LANES // BLOCK):
            unit = mass[b * BLOCK : b * BLOCK + 8, :]
            for k in range(1, PARTS):
                at = b * BLOCK + 8 * k
                unit = jnp.where(lane == k, mass[at : at + 8, :], unit)
            out_ref[b, out_ref.shape[1] - 1] = unit

    for chain, (tile, out_ref) in enumerate(zip(tiles, (a_ref, b_ref))):
        scale = lane_to_sublane(col_ref[pl.ds(tile, 1), :])
        total = jnp.zeros((LANES, LANES), F32)
        for g in range(groups):
            plan = k_ref[row_tile(tile), lane_group(g)] * row_scale[g : g + 1, :] * scale
            total = total + plan
            plan_ref[chain * LANES : (chain + 1) * LANES, lane_group(g)] = plan.astype(jnp.bfloat16)
        put_mass(total, out_ref)

    @pl.when(jnp.logical_not(fast))
    def _():
        ok = within(peak_ref[...])
        col_ref[...] = col_pot
        row_ref[...] = row_pot
        for chain, (tile, out_ref) in enumerate(zip(tiles, (a_ref, b_ref))):
            shift = lane_to_sublane(col_ref[pl.ds(tile, 1), :])

            def group(g, total):
                plan = jnp.exp(logit_block(k_ref, ok, tile, g) + row_ref[pl.ds(g, 1), :] + shift)
                plan_ref[chain * LANES : (chain + 1) * LANES, lane_tile(g)] = plan.astype(jnp.bfloat16)
                return total + plan

            put_mass(lax.fori_loop(0, groups, group, jnp.zeros((LANES, LANES), F32)), out_ref)

    block = jnp.dot(plan_ref[...], vec_ref[...], preferred_element_type=F32)
    across = block.shape[1] // LANES
    for chain, out_ref in enumerate((a_ref, b_ref)):
        for b in range(LANES // BLOCK):
            for k in range(PARTS):
                row = chain * LANES + b * BLOCK + 8 * k
                for g in range(across):
                    out_ref[b, k * across + g] = block[row : row + 8, lane_group(g)]


def add_kernel(mine_ref, got_ref, out_ref):
    out_ref[...] = mine_ref[...] + got_ref[...]


def spot(flips):
    bits = position_bits()
    x2, z2 = bits[XB2], bits[ZB2]
    return (1 - x2 if flips[0] else x2) * 2 + (1 - z2 if flips[1] else z2)


def pieces_kernel(order, mine_ref, first_ref, second_ref, send_ref, keep_ref):
    for n, flips in enumerate(order):
        at = spot(flips)
        out_ref = (send_ref, keep_ref)[n // 2]
        out_ref[n % 2] = mine_ref[at] + first_ref[at] + second_ref[at]


def own_kernel(keep_ref, got_ref, second_ref, out_ref):
    out_ref[...] = keep_ref[1] + got_ref[1] + second_ref[...]


def hold_kernel(keep_ref, got_ref, out_ref):
    out_ref[...] = keep_ref[0] + got_ref[0]


def mean_kernel(sum_ref, got_ref, out_ref):
    units = sum_ref.shape[0] - 1
    across = out_ref.shape[1] // LANES
    lanes = LANES // PARTS
    mass = sum_ref[units] + got_ref[units]
    for k in range(PARTS):
        part = jnp.broadcast_to(mass[:, k * lanes : k * lanes + 1], (8, LANES))
        for g in range(across):
            u = k * across + g
            out_ref[8 * k : 8 * k + 8, lane_group(g)] = (sum_ref[u] + got_ref[u]) / part


def join_kernel(order, *refs):
    out_ref = refs[-1]
    for flips, part_ref in zip(order, refs):
        at = pl.ds(pl.multiple_of(spot(flips) * BLOCK, BLOCK), BLOCK)
        out_ref[at, :] = part_ref[...]


def place_kernel(spots, *refs):
    out_ref, sems = refs[-2:]
    bits = position_bits()
    x1, z1 = bits[XB1], bits[ZB1]
    copies = []
    for n, ((chain, flips), part_ref) in enumerate(zip(spots, refs)):
        size = part_ref.shape[0]
        first, second = (z1, x1) if chain else (x1, z1)
        first = 1 - first if flips[0] else first
        second = 1 - second if flips[1] else second
        at = pl.ds(pl.multiple_of((chain * 4 + first * 2 + second) * size, size), size)
        copies.append(pltpu.make_async_copy(part_ref, out_ref.at[at, :], sems.at[n]))
    for copy in copies:
        copy.start()
    for copy in copies:
        copy.wait()


def place(row, core):
    return (row // ZS + (XS - 1) * core) % XS, (row % ZS + (ZS - 1) * core) % ZS


def pairs(partner, n_cols):
    out = []
    for row in range(XS * ZS):
        for col in range(n_cols):
            core = col % 2
            x, z = partner(*place(row, core))
            to = (x + core) % XS * ZS + (z + core) % ZS
            out.append((row * n_cols + col, to * n_cols + col))
    return out


def exchange(x, partner):
    return lax.ppermute(x, ("rows", "cols"), pairs(partner, lax.axis_size("cols")))


def x_first(x, z):
    return x ^ 1, z


def x_second(x, z):
    return XS - 1 - x, z


def z_first(x, z):
    return x, z ^ 1


def z_second(x, z):
    return x, (z - 1 + 2 * (z % 2)) % ZS


def z_third(x, z):
    return x, {0: 3, 3: 0, 1: 6, 6: 1, 2: 5, 5: 2, 4: 7, 7: 4}[z]


def position_bits():
    core = lax.axis_index("cols") & 1
    row = lax.axis_index("rows")
    x = ((row >> 3) + (XS - 1) * core) & (XS - 1)
    z = (row + (ZS - 1) * core) & (ZS - 1)
    return (x ^ (x >> 1)) & 1, x >> 1, ((z + 1) >> 1) & 1, (0xB4 >> z) & 1


def add(mine, got):
    return pl.pallas_call(
        add_kernel,
        out_shape=jax.ShapeDtypeStruct(mine.shape, F32),
        in_specs=[vmem(), vmem()],
        out_specs=vmem(),
        compiler_params=params(4),
        name="add",
    )(mine, got)


def put(spots, parts, cents, *before):
    return pl.pallas_call(
        functools.partial(place_kernel, spots),
        out_shape=jax.ShapeDtypeStruct((cents, parts[0].shape[1]), F32),
        in_specs=[vmem()] * len(parts) + [hbm()] * len(before),
        out_specs=hbm(),
        scratch_shapes=[pltpu.SemaphoreType.DMA((len(parts),))],
        input_output_aliases={len(parts): 0} if before else {},
        compiler_params=params(4),
        name="place",
    )(*parts, *before)


A_ORDER = ((True, True), (True, False), (False, True), (False, False))
B_ORDER = ((True, True), (False, True), (True, False), (False, False))


def sum_of_four(order, first, second, *terms):
    piece = jax.ShapeDtypeStruct(terms[0].shape[1:], F32)
    pair = jax.ShapeDtypeStruct((2, *terms[0].shape[1:]), F32)
    send, keep = pl.pallas_call(
        functools.partial(pieces_kernel, order),
        out_shape=(pair, pair),
        in_specs=[vmem()] * 3,
        out_specs=(vmem(), vmem()),
        compiler_params=params(4),
        name="pieces",
    )(*terms)
    got = exchange(send, first)
    hold = pl.pallas_call(
        hold_kernel,
        out_shape=piece,
        in_specs=[vmem()] * 2,
        out_specs=vmem(),
        compiler_params=params(4),
        name="hold",
    )(keep, got)
    return pl.pallas_call(
        own_kernel,
        out_shape=piece,
        in_specs=[vmem()] * 3,
        out_specs=vmem(),
        compiler_params=params(4),
        name="own",
    )(keep, got, exchange(hold, second))


def mean_of_four(order, first, second, mine, got, width):
    mean = pl.pallas_call(
        mean_kernel,
        out_shape=jax.ShapeDtypeStruct((BLOCK, width), F32),
        in_specs=[vmem()] * 2,
        out_specs=vmem(),
        compiler_params=params(4),
        name="mean",
    )(mine, got)
    hold, stay = exchange(mean, second), exchange(mean, first)
    away = exchange(hold, first)
    return pl.pallas_call(
        functools.partial(join_kernel, order),
        out_shape=jax.ShapeDtypeStruct((4 * BLOCK, width), F32),
        in_specs=[vmem()] * 4,
        out_specs=vmem(),
        compiler_params=params(4),
        name="join",
    )(away, stay, hold, mean)


def mean_over_rows(quarter_sums, cents, width):
    pass_a, pass_b = quarter_sums((True, True))
    pass_a, pass_b = exchange(pass_a, x_first), exchange(pass_b, z_first)
    stay_a, stay_b = quarter_sums((True, False))
    stay_a, stay_b = exchange(stay_a, x_first), exchange(stay_b, z_first)
    mine_a, mine_b = quarter_sums((False, True))
    next_a = exchange(add(mine_a, pass_a), z_first)
    next_b = exchange(add(mine_b, pass_b), x_first)
    mine_a, mine_b = quarter_sums((False, False))
    mine_a = sum_of_four(A_ORDER, x_second, z_second, mine_a, stay_a, next_a)
    mine_b = sum_of_four(B_ORDER, z_second, x_second, mine_b, stay_b, next_b)
    got_a, got_b = exchange(mine_a, z_third), exchange(mine_b, z_third)
    mine_a = mean_of_four(A_ORDER, x_second, z_second, mine_a, got_a, width)
    mine_b = mean_of_four(B_ORDER, z_second, x_second, mine_b, got_b, width)
    next_a, next_b = exchange(mine_a, z_first), exchange(mine_b, x_first)
    stay_a, stay_b = exchange(mine_a, x_first), exchange(mine_b, z_first)
    pass_a, pass_b = exchange(next_a, x_first), exchange(next_b, z_first)
    near = ((0, (False, False)), (1, (False, False)), (0, (False, True)), (1, (False, True)))
    out = put(near, (mine_a, mine_b, next_a, next_b), cents)
    out = put(((0, (True, False)), (1, (True, False))), (stay_a, stay_b), cents, out)
    return put(((0, (True, True)), (1, (True, True))), (pass_a, pass_b), cents, out)


def vmem():
    return pl.BlockSpec(memory_space=pltpu.VMEM)


def hbm():
    return pl.BlockSpec(memory_space=pltpu.HBM)


def pinned(x):
    return pltpu.with_memory_space_constraint(x, pltpu.VMEM)


def params(mib):
    return pltpu.CompilerParams(vmem_limit_bytes=mib * MIB)


def per_device(vectors, centroids):
    n_rows, n_cols = lax.axis_size("rows"), lax.axis_size("cols")
    rows, width = vectors.shape
    cents = centroids.shape[0]
    log_target = math.log(rows * n_rows / (cents * n_cols))
    groups, tiles = rows // LANES, cents // LANES
    kept = pltpu.VMEM((cents, rows), F32)
    peak_type = jax.ShapeDtypeStruct((8, LANES), F32)
    row_parts = jax.ShapeDtypeStruct((n_cols, groups, LANES), F32)
    col_parts = jax.ShapeDtypeStruct((n_rows, tiles, LANES), F32)
    row_scratch = pltpu.VMEM((groups, LANES), F32)
    col_scratch = pltpu.VMEM((tiles, LANES), F32)

    kernel, peak, part = pl.pallas_call(
        logits_kernel,
        out_shape=(kept, peak_type, row_parts),
        in_specs=[hbm(), hbm()],
        out_specs=(vmem(), vmem(), vmem()),
        scratch_shapes=[
            row_scratch,
            pltpu.VMEM((cents, width), jnp.bfloat16),
            pltpu.VMEM((rows, width), jnp.bfloat16),
            pltpu.SemaphoreType.DMA((2 * CHUNKS,)),
        ],
        compiler_params=params(24),
        name="logits",
    )(*(pltpu.with_memory_space_constraint(x, pltpu.HBM) for x in (centroids, vectors)))

    for step in range(ITERS):
        row_got = lax.all_to_all(part, "cols", 0, 0, tiled=True)
        part = pl.pallas_call(
            col_kernel,
            out_shape=col_parts,
            in_specs=[vmem(), vmem(), vmem()],
            out_specs=vmem(),
            scratch_shapes=[col_scratch, row_scratch],
            compiler_params=params(4),
            name="col_step",
        )(row_got, peak, pinned(kernel))
        col_got = lax.all_to_all(part, "rows", 0, 0, tiled=True)
        part = pl.pallas_call(
            functools.partial(row_kernel, log_target),
            out_shape=row_parts,
            in_specs=[vmem(), vmem(), vmem()],
            out_specs=vmem(),
            scratch_shapes=[col_scratch, row_scratch],
            compiler_params=params(4),
            name="row_step",
        )(col_got, peak, pinned(kernel))
    row_got = lax.all_to_all(part, "cols", 0, 0, tiled=True)

    quarter = jax.ShapeDtypeStruct((LANES // BLOCK, PARTS * (width // LANES) + 1, 8, LANES), F32)
    pots = []

    def quarter_sums(flips):
        first = not pots
        pot_types = tuple(jax.ShapeDtypeStruct((n, LANES), F32) for n in (tiles, tiles, groups, groups))
        a, b, *new = pl.pallas_call(
            functools.partial(sums_kernel, log_target if first else None, flips),
            out_shape=(quarter, quarter) + (pot_types if first else ()),
            in_specs=[vmem()] * 5,
            out_specs=(vmem(),) * (6 if first else 2),
            scratch_shapes=[pltpu.VMEM((2 * LANES, rows), jnp.bfloat16), col_scratch, row_scratch],
            compiler_params=params(8),
            cost_estimate=pl.CostEstimate(
                flops=rows * cents * width // 2, bytes_accessed=4 * MIB, transcendentals=0
            ),
            name="sums",
        )(*(pots[1::2] or (col_got, row_got)), peak, pinned(kernel), vectors)
        pots.extend(new)
        return a, b

    new_centroids = mean_over_rows(quarter_sums, cents, width)
    col_pot, row_pot = pots[0::2]
    return (new_centroids, row_pot.reshape(rows), col_pot.reshape(cents))


def solution(mesh):
    return jax.shard_map(
        per_device,
        mesh=mesh,
        in_specs=(P("rows", None), P("cols", None)),
        out_specs=(P("cols", None), P("rows"), P("cols")),
        check_vma=False,
    )
```

```python
import functools
import math

import jax
import jax.numpy as jnp
from jax import lax
from jax.experimental import pallas as pl
from jax.experimental.pallas import tpu as pltpu
from jax.sharding import PartitionSpec as P

ITERS = 3
LANES = 128
LIM = 40.0
MIB = 1024 * 1024
F32 = jnp.float32
LOG2E = math.log2(math.e)
XS, ZS = 4, 8
BLOCK = 32
PARTS = BLOCK // 8
CHUNKS = 4
XB1, XB2, ZB1, ZB2 = range(4)


def combine_lse(parts):
    top = jnp.max(parts, axis=0)
    return top + jnp.log(jnp.sum(jnp.exp(parts - top[None]), axis=0))


def lane_to_sublane(row):
    return jnp.transpose(jnp.broadcast_to(row, (LANES, LANES)))


def fold(x):
    return jnp.sum(x.reshape(x.shape[0] // 8, 8, x.shape[1]), axis=0)


def lane_group(g):
    return slice(g * LANES, (g + 1) * LANES)


def row_tile(t):
    return pl.ds(pl.multiple_of(t * LANES, LANES), LANES)


def put_copies(out_ref, value):
    for k in range(out_ref.shape[0]):
        out_ref[k] = value


def lane_tile(g):
    return pl.ds(pl.multiple_of(g * LANES, LANES), LANES)


def logit_block(k_ref, ok, t, g):
    block = k_ref[row_tile(t), lane_tile(g)]
    return jnp.where(ok, jnp.log(block), block)


def within(peak, *pots):
    for pot in pots:
        pot = jnp.abs(pot)
        for k in range(pot.shape[0] // 8):
            peak = jnp.maximum(peak, pot[8 * k : 8 * k + 8, :])
    return jnp.max(peak) <= LIM


def row_lse_exact(k_ref, ok, pot_ref, out_ref):
    tiles, groups = k_ref.shape[0] // LANES, k_ref.shape[1] // LANES

    def group(g, carry):
        def shifted(t):
            z = logit_block(k_ref, ok, t, g)
            return z if pot_ref is None else z + lane_to_sublane(pot_ref[pl.ds(t, 1), :])

        def top_of(t, top):
            return jnp.maximum(top, jnp.max(shifted(t), axis=0, keepdims=True))

        top = lax.fori_loop(0, tiles, top_of, jnp.full((1, LANES), -3.0e38, F32))

        def sum_of(t, total):
            return total + jnp.sum(jnp.exp(shifted(t) - top), axis=0, keepdims=True)

        total = lax.fori_loop(0, tiles, sum_of, jnp.zeros((1, LANES), F32))
        out_ref[pl.ds(g, 1), :] = top + jnp.log(total)
        return carry

    lax.fori_loop(0, groups, group, 0)


def col_lse_exact(k_ref, ok, pot_ref, out_ref):
    tiles, groups = k_ref.shape[0] // LANES, k_ref.shape[1] // LANES

    def tile(t, carry):
        def shifted(g):
            return logit_block(k_ref, ok, t, g) + pot_ref[pl.ds(g, 1), :]

        def top_of(g, top):
            return jnp.maximum(top, shifted(g))

        top = lax.fori_loop(0, groups, top_of, jnp.full((LANES, LANES), -3.0e38, F32))
        top = jnp.broadcast_to(jnp.max(top, axis=1, keepdims=True), (LANES, LANES))

        def sum_of(g, total):
            return total + jnp.exp(shifted(g) - top)

        total = lax.fori_loop(0, groups, sum_of, jnp.zeros((LANES, LANES), F32))
        total = jnp.sum(jnp.transpose(total), axis=0, keepdims=True)
        out_ref[pl.ds(t, 1), :] = jnp.transpose(top)[0:1, :] + jnp.log(total)
        return carry

    lax.fori_loop(0, tiles, tile, 0)


def logits_kernel(cent_hbm, vec_hbm, k_ref, peak_ref, out_ref, lse_ref, cent_ref, vec_ref, sems):
    cents, rows = k_ref.shape
    groups = rows // LANES
    step, chunk = cents // CHUNKS, rows // CHUNKS

    def pieces(hbm_ref, vmem_ref, first, size):
        return [
            pltpu.make_async_copy(
                hbm_ref.at[pl.ds(c * size, size), :], vmem_ref.at[pl.ds(c * size, size), :], sems.at[first + c]
            )
            for c in range(CHUNKS)
        ]

    vec_copies = pieces(vec_hbm, vec_ref, 0, chunk)
    cent_copies = pieces(cent_hbm, cent_ref, CHUNKS, step)
    for copy in vec_copies[:1] + cent_copies + vec_copies[1:]:
        copy.start()

    def dots(c):
        vec_copies[c].wait()
        if c == 0:
            for copy in cent_copies:
                copy.wait()
        return lax.dot_general(
            cent_ref[...], vec_ref[c * chunk : (c + 1) * chunk, :],
            (((1,), (1,)), ((), ())), preferred_element_type=F32,
        )

    peak = jnp.zeros((8, LANES), F32)
    ahead = dots(0)
    for c in range(CHUNKS):
        block = ahead
        if c + 1 < CHUNKS:
            ahead = dots(c + 1)
        for g in range(chunk // LANES):
            group = c * (chunk // LANES) + g
            total = jnp.zeros((8, LANES), F32)
            for t in range(cents // LANES):
                part = block[t * LANES : (t + 1) * LANES, lane_group(g)]
                peak = jnp.maximum(peak, jnp.max(jnp.abs(part).reshape(LANES // 8, 8, LANES), axis=0))
                part = jnp.exp2(part * (4.0 * LOG2E))
                k_ref[t * LANES : (t + 1) * LANES, lane_group(group)] = part
                total = total + fold(part)
            lse_ref[group : group + 1, :] = jnp.sum(total, axis=0, keepdims=True)
    peak = 4.0 * peak
    lse_ref[...] = jnp.log(lse_ref[...])
    peak_ref[...] = peak

    @pl.when(jnp.logical_not(within(peak)))
    def _():
        def tile(t, carry):
            def group(g, carry):
                k_ref[row_tile(t), lane_tile(g)] = 4.0 * lax.dot_general(
                    cent_ref[row_tile(t), :], vec_ref[row_tile(g), :],
                    (((1,), (1,)), ((), ())), preferred_element_type=F32,
                )
                return carry

            return lax.fori_loop(0, groups, group, carry)

        lax.fori_loop(0, cents // LANES, tile, 0)
        row_lse_exact(k_ref, False, None, lse_ref)

    put_copies(out_ref, lse_ref[...])


def row_kernel(log_target, got_ref, peak_ref, k_ref, out_ref, pot_ref, lse_ref):
    tiles, groups = k_ref.shape[0] // LANES, k_ref.shape[1] // LANES
    pot = log_target - combine_lse(got_ref[...])
    fast = within(peak_ref[...], pot)

    scales = jnp.exp(pot)
    sums = [jnp.zeros((8, LANES), F32)] * groups
    for t in range(tiles):
        scale = lane_to_sublane(scales[t : t + 1, :])
        for g in range(groups):
            sums[g] = sums[g] + fold(k_ref[t * LANES : (t + 1) * LANES, lane_group(g)] * scale)
    for g in range(groups):
        lse_ref[g : g + 1, :] = jnp.sum(sums[g], axis=0, keepdims=True)
    lse_ref[...] = jnp.log(lse_ref[...])

    @pl.when(jnp.logical_not(fast))
    def _():
        pot_ref[...] = pot
        row_lse_exact(k_ref, within(peak_ref[...]), pot_ref, lse_ref)

    put_copies(out_ref, lse_ref[...])


def col_kernel(got_ref, peak_ref, k_ref, out_ref, lse_ref, pot_ref):
    tiles, groups = k_ref.shape[0] // LANES, k_ref.shape[1] // LANES
    pot = -combine_lse(got_ref[...])
    fast = within(peak_ref[...], pot)

    scale = jnp.exp(pot)
    for t in range(tiles):
        total = jnp.zeros((LANES, LANES), F32)
        for g in range(groups):
            total = total + k_ref[t * LANES : (t + 1) * LANES, lane_group(g)] * scale[g : g + 1, :]
        lse_ref[t : t + 1, :] = jnp.sum(jnp.transpose(total), axis=0, keepdims=True)
    lse_ref[...] = jnp.log(lse_ref[...])

    @pl.when(jnp.logical_not(fast))
    def _():
        pot_ref[...] = pot
        col_lse_exact(k_ref, within(peak_ref[...]), pot_ref, lse_ref)

    put_copies(out_ref, lse_ref[...])


def sums_kernel(log_target, flips, *refs):
    first_call = log_target is not None
    cols_ref, rows_ref, peak_ref, k_ref, vec_ref, a_ref, b_ref = refs[:7]
    plan_ref, col_ref, row_ref = refs[-3:]
    groups = k_ref.shape[1] // LANES
    if first_call:
        col_pot = log_target - combine_lse(cols_ref[...])
        row_pot = -combine_lse(rows_ref[...])
        for pot_ref in refs[7:9]:
            pot_ref[...] = col_pot
        for pot_ref in refs[9:11]:
            pot_ref[...] = row_pot
    else:
        col_pot, row_pot = cols_ref[...], rows_ref[...]
    fast = within(peak_ref[...], col_pot, row_pot)
    col_ref[...] = jnp.exp(col_pot)
    row_scale = jnp.exp(row_pot)
    bits = position_bits()
    x1, z1 = bits[XB1], bits[ZB1]
    tiles = []
    for chain, (first, second) in enumerate(((x1, z1), (z1, x1))):
        first = 1 - first if flips[0] else first
        second = 1 - second if flips[1] else second
        tiles.append(chain * 4 + first * 2 + second)

    def put_mass(total, out_ref):
        mass = jnp.broadcast_to(jnp.sum(total, axis=1, keepdims=True), (LANES, LANES))
        lane = lax.broadcasted_iota(jnp.int32, (8, LANES), 1) // (LANES // PARTS)
        for b in range(LANES // BLOCK):
            unit = mass[b * BLOCK : b * BLOCK + 8, :]
            for k in range(1, PARTS):
                at = b * BLOCK + 8 * k
                unit = jnp.where(lane == k, mass[at : at + 8, :], unit)
            out_ref[b, out_ref.shape[1] - 1] = unit

    for chain, (tile, out_ref) in enumerate(zip(tiles, (a_ref, b_ref))):
        scale = lane_to_sublane(col_ref[pl.ds(tile, 1), :])
        total = jnp.zeros((LANES, LANES), F32)
        for g in range(groups):
            plan = k_ref[row_tile(tile), lane_group(g)] * row_scale[g : g + 1, :] * scale
            total = total + plan
            plan_ref[chain * LANES : (chain + 1) * LANES, lane_group(g)] = plan.astype(jnp.bfloat16)
        put_mass(total, out_ref)

    @pl.when(jnp.logical_not(fast))
    def _():
        ok = within(peak_ref[...])
        col_ref[...] = col_pot
        row_ref[...] = row_pot
        for chain, (tile, out_ref) in enumerate(zip(tiles, (a_ref, b_ref))):
            shift = lane_to_sublane(col_ref[pl.ds(tile, 1), :])

            def group(g, total):
                plan = jnp.exp(logit_block(k_ref, ok, tile, g) + row_ref[pl.ds(g, 1), :] + shift)
                plan_ref[chain * LANES : (chain + 1) * LANES, lane_tile(g)] = plan.astype(jnp.bfloat16)
                return total + plan

            put_mass(lax.fori_loop(0, groups, group, jnp.zeros((LANES, LANES), F32)), out_ref)

    block = jnp.dot(plan_ref[...], vec_ref[...], preferred_element_type=F32)
    across = block.shape[1] // LANES
    for chain, out_ref in enumerate((a_ref, b_ref)):
        for b in range(LANES // BLOCK):
            for k in range(PARTS):
                row = chain * LANES + b * BLOCK + 8 * k
                for g in range(across):
                    out_ref[b, k * across + g] = block[row : row + 8, lane_group(g)]


def add_kernel(mine_ref, got_ref, out_ref):
    out_ref[...] = mine_ref[...] + got_ref[...]


def spot(flips):
    bits = position_bits()
    x2, z2 = bits[XB2], bits[ZB2]
    return (1 - x2 if flips[0] else x2) * 2 + (1 - z2 if flips[1] else z2)


def pieces_kernel(order, mine_ref, first_ref, second_ref, send_ref, keep_ref):
    for n, flips in enumerate(order):
        at = spot(flips)
        out_ref = (send_ref, keep_ref)[n // 2]
        out_ref[n % 2] = mine_ref[at] + first_ref[at] + second_ref[at]


def own_kernel(keep_ref, got_ref, second_ref, out_ref):
    out_ref[...] = keep_ref[1] + got_ref[1] + second_ref[...]


def hold_kernel(keep_ref, got_ref, out_ref):
    out_ref[...] = keep_ref[0] + got_ref[0]


def mean_kernel(sum_ref, got_ref, out_ref):
    units = sum_ref.shape[0] - 1
    across = out_ref.shape[1] // LANES
    lanes = LANES // PARTS
    mass = sum_ref[units] + got_ref[units]
    for k in range(PARTS):
        part = jnp.broadcast_to(mass[:, k * lanes : k * lanes + 1], (8, LANES))
        for g in range(across):
            u = k * across + g
            out_ref[8 * k : 8 * k + 8, lane_group(g)] = (sum_ref[u] + got_ref[u]) / part


def join_kernel(order, *refs):
    out_ref = refs[-1]
    for flips, part_ref in zip(order, refs):
        at = pl.ds(pl.multiple_of(spot(flips) * BLOCK, BLOCK), BLOCK)
        out_ref[at, :] = part_ref[...]


def place_kernel(spots, *refs):
    out_ref, sems = refs[-2:]
    bits = position_bits()
    x1, z1 = bits[XB1], bits[ZB1]
    copies = []
    for n, ((chain, flips), part_ref) in enumerate(zip(spots, refs)):
        size = part_ref.shape[0]
        first, second = (z1, x1) if chain else (x1, z1)
        first = 1 - first if flips[0] else first
        second = 1 - second if flips[1] else second
        at = pl.ds(pl.multiple_of((chain * 4 + first * 2 + second) * size, size), size)
        copies.append(pltpu.make_async_copy(part_ref, out_ref.at[at, :], sems.at[n]))
    for copy in copies:
        copy.start()
    for copy in copies:
        copy.wait()


def place(row, core):
    return (row // ZS + (XS - 1) * core) % XS, (row % ZS + (ZS - 1) * core) % ZS


def pairs(partner, n_cols):
    out = []
    for row in range(XS * ZS):
        for col in range(n_cols):
            core = col % 2
            x, z = partner(*place(row, core))
            to = (x + core) % XS * ZS + (z + core) % ZS
            out.append((row * n_cols + col, to * n_cols + col))
    return out


def exchange(x, partner):
    return lax.ppermute(x, ("rows", "cols"), pairs(partner, lax.axis_size("cols")))


def x_first(x, z):
    return x ^ 1, z


def x_second(x, z):
    return XS - 1 - x, z


def z_first(x, z):
    return x, z ^ 1


def z_second(x, z):
    return x, (z - 1 + 2 * (z % 2)) % ZS


def z_third(x, z):
    return x, {0: 3, 3: 0, 1: 6, 6: 1, 2: 5, 5: 2, 4: 7, 7: 4}[z]


def position_bits():
    core = lax.axis_index("cols") & 1
    row = lax.axis_index("rows")
    x = ((row >> 3) + (XS - 1) * core) & (XS - 1)
    z = (row + (ZS - 1) * core) & (ZS - 1)
    return (x ^ (x >> 1)) & 1, x >> 1, ((z + 1) >> 1) & 1, (0xB4 >> z) & 1


def add(mine, got):
    return pl.pallas_call(
        add_kernel,
        out_shape=jax.ShapeDtypeStruct(mine.shape, F32),
        in_specs=[vmem(), vmem()],
        out_specs=vmem(),
        compiler_params=params(4),
        name="add",
    )(mine, got)


def put(spots, parts, cents, *before):
    return pl.pallas_call(
        functools.partial(place_kernel, spots),
        out_shape=jax.ShapeDtypeStruct((cents, parts[0].shape[1]), F32),
        in_specs=[vmem()] * len(parts) + [hbm()] * len(before),
        out_specs=hbm(),
        scratch_shapes=[pltpu.SemaphoreType.DMA((len(parts),))],
        input_output_aliases={len(parts): 0} if before else {},
        compiler_params=params(4),
        name="place",
    )(*parts, *before)


A_ORDER = ((True, True), (True, False), (False, True), (False, False))
B_ORDER = ((True, True), (False, True), (True, False), (False, False))


def sum_of_four(order, first, second, *terms):
    piece = jax.ShapeDtypeStruct(terms[0].shape[1:], F32)
    pair = jax.ShapeDtypeStruct((2, *terms[0].shape[1:]), F32)
    send, keep = pl.pallas_call(
        functools.partial(pieces_kernel, order),
        out_shape=(pair, pair),
        in_specs=[vmem()] * 3,
        out_specs=(vmem(), vmem()),
        compiler_params=params(4),
        name="pieces",
    )(*terms)
    got = exchange(send, first)
    hold = pl.pallas_call(
        hold_kernel,
        out_shape=piece,
        in_specs=[vmem()] * 2,
        out_specs=vmem(),
        compiler_params=params(4),
        name="hold",
    )(keep, got)
    return pl.pallas_call(
        own_kernel,
        out_shape=piece,
        in_specs=[vmem()] * 3,
        out_specs=vmem(),
        compiler_params=params(4),
        name="own",
    )(keep, got, exchange(hold, second))


def mean_of_four(order, first, second, mine, got, width):
    mean = pl.pallas_call(
        mean_kernel,
        out_shape=jax.ShapeDtypeStruct((BLOCK, width), F32),
        in_specs=[vmem()] * 2,
        out_specs=vmem(),
        compiler_params=params(4),
        name="mean",
    )(mine, got)
    hold, stay = exchange(mean, second), exchange(mean, first)
    away = exchange(hold, first)
    return pl.pallas_call(
        functools.partial(join_kernel, order),
        out_shape=jax.ShapeDtypeStruct((4 * BLOCK, width), F32),
        in_specs=[vmem()] * 4,
        out_specs=vmem(),
        compiler_params=params(4),
        name="join",
    )(away, stay, hold, mean)


def mean_over_rows(quarter_sums, cents, width):
    pass_a, pass_b = quarter_sums((True, True))
    pass_a, pass_b = exchange(pass_a, x_first), exchange(pass_b, z_first)
    stay_a, stay_b = quarter_sums((True, False))
    stay_a, stay_b = exchange(stay_a, x_first), exchange(stay_b, z_first)
    mine_a, mine_b = quarter_sums((False, True))
    next_a = exchange(add(mine_a, pass_a), z_first)
    next_b = exchange(add(mine_b, pass_b), x_first)
    mine_a, mine_b = quarter_sums((False, False))
    mine_a = sum_of_four(A_ORDER, x_second, z_second, mine_a, stay_a, next_a)
    mine_b = sum_of_four(B_ORDER, z_second, x_second, mine_b, stay_b, next_b)
    got_a, got_b = exchange(mine_a, z_third), exchange(mine_b, z_third)
    mine_a = mean_of_four(A_ORDER, x_second, z_second, mine_a, got_a, width)
    mine_b = mean_of_four(B_ORDER, z_second, x_second, mine_b, got_b, width)
    next_a, next_b = exchange(mine_a, z_first), exchange(mine_b, x_first)
    stay_a, stay_b = exchange(mine_a, x_first), exchange(mine_b, z_first)
    pass_a, pass_b = exchange(next_a, x_first), exchange(next_b, z_first)
    near = ((0, (False, False)), (1, (False, False)), (0, (False, True)), (1, (False, True)))
    out = put(near, (mine_a, mine_b, next_a, next_b), cents)
    out = put(((0, (True, False)), (1, (True, False))), (stay_a, stay_b), cents, out)
    out = put(((0, (True, True)),), (pass_a,), cents, out)
    return put(((1, (True, True)),), (pass_b,), cents, out)


def vmem():
    return pl.BlockSpec(memory_space=pltpu.VMEM)


def hbm():
    return pl.BlockSpec(memory_space=pltpu.HBM)


def pinned(x):
    return pltpu.with_memory_space_constraint(x, pltpu.VMEM)


def params(mib):
    return pltpu.CompilerParams(vmem_limit_bytes=mib * MIB)


def per_device(vectors, centroids):
    n_rows, n_cols = lax.axis_size("rows"), lax.axis_size("cols")
    rows, width = vectors.shape
    cents = centroids.shape[0]
    log_target = math.log(rows * n_rows / (cents * n_cols))
    groups, tiles = rows // LANES, cents // LANES
    kept = pltpu.VMEM((cents, rows), F32)
    peak_type = jax.ShapeDtypeStruct((8, LANES), F32)
    row_parts = jax.ShapeDtypeStruct((n_cols, groups, LANES), F32)
    col_parts = jax.ShapeDtypeStruct((n_rows, tiles, LANES), F32)
    row_scratch = pltpu.VMEM((groups, LANES), F32)
    col_scratch = pltpu.VMEM((tiles, LANES), F32)

    kernel, peak, part = pl.pallas_call(
        logits_kernel,
        out_shape=(kept, peak_type, row_parts),
        in_specs=[hbm(), hbm()],
        out_specs=(vmem(), vmem(), vmem()),
        scratch_shapes=[
            row_scratch,
            pltpu.VMEM((cents, width), jnp.bfloat16),
            pltpu.VMEM((rows, width), jnp.bfloat16),
            pltpu.SemaphoreType.DMA((2 * CHUNKS,)),
        ],
        compiler_params=params(24),
        name="logits",
    )(*(pltpu.with_memory_space_constraint(x, pltpu.HBM) for x in (centroids, vectors)))

    for step in range(ITERS):
        row_got = lax.all_to_all(part, "cols", 0, 0, tiled=True)
        part = pl.pallas_call(
            col_kernel,
            out_shape=col_parts,
            in_specs=[vmem(), vmem(), vmem()],
            out_specs=vmem(),
            scratch_shapes=[col_scratch, row_scratch],
            compiler_params=params(4),
            name="col_step",
        )(row_got, peak, pinned(kernel))
        col_got = lax.all_to_all(part, "rows", 0, 0, tiled=True)
        part = pl.pallas_call(
            functools.partial(row_kernel, log_target),
            out_shape=row_parts,
            in_specs=[vmem(), vmem(), vmem()],
            out_specs=vmem(),
            scratch_shapes=[col_scratch, row_scratch],
            compiler_params=params(4),
            name="row_step",
        )(col_got, peak, pinned(kernel))
    row_got = lax.all_to_all(part, "cols", 0, 0, tiled=True)

    quarter = jax.ShapeDtypeStruct((LANES // BLOCK, PARTS * (width // LANES) + 1, 8, LANES), F32)
    pots = []

    def quarter_sums(flips):
        first = not pots
        pot_types = tuple(jax.ShapeDtypeStruct((n, LANES), F32) for n in (tiles, tiles, groups, groups))
        a, b, *new = pl.pallas_call(
            functools.partial(sums_kernel, log_target if first else None, flips),
            out_shape=(quarter, quarter) + (pot_types if first else ()),
            in_specs=[vmem()] * 5,
            out_specs=(vmem(),) * (6 if first else 2),
            scratch_shapes=[pltpu.VMEM((2 * LANES, rows), jnp.bfloat16), col_scratch, row_scratch],
            compiler_params=params(8),
            cost_estimate=pl.CostEstimate(
                flops=rows * cents * width // 2, bytes_accessed=4 * MIB, transcendentals=0
            ),
            name="sums",
        )(*(pots[1::2] or (col_got, row_got)), peak, pinned(kernel), vectors)
        pots.extend(new)
        return a, b

    new_centroids = mean_over_rows(quarter_sums, cents, width)
    col_pot, row_pot = pots[0::2]
    return (new_centroids, row_pot.reshape(rows), col_pot.reshape(cents))


def solution(mesh):
    return jax.shard_map(
        per_device,
        mesh=mesh,
        in_specs=(P("rows", None), P("cols", None)),
        out_specs=(P("cols", None), P("rows"), P("cols")),
        check_vma=False,
    )
```

```python
import functools
import math

import jax
import jax.numpy as jnp
from jax import lax
from jax.experimental import pallas as pl
from jax.experimental.pallas import tpu as pltpu
from jax.sharding import PartitionSpec as P

ITERS = 3
LANES = 128
LIM = 40.0
MIB = 1024 * 1024
F32 = jnp.float32
LOG2E = math.log2(math.e)
XS, ZS = 4, 8
BLOCK = 32
PARTS = BLOCK // 8
CHUNKS = 2
XB1, XB2, ZB1, ZB2 = range(4)


def combine_lse(parts):
    top = jnp.max(parts, axis=0)
    return top + jnp.log(jnp.sum(jnp.exp(parts - top[None]), axis=0))


def lane_to_sublane(row):
    return jnp.transpose(jnp.broadcast_to(row, (LANES, LANES)))


def fold(x):
    return jnp.sum(x.reshape(x.shape[0] // 8, 8, x.shape[1]), axis=0)


def lane_group(g):
    return slice(g * LANES, (g + 1) * LANES)


def row_tile(t):
    return pl.ds(pl.multiple_of(t * LANES, LANES), LANES)


def put_copies(out_ref, value):
    for k in range(out_ref.shape[0]):
        out_ref[k] = value


def lane_tile(g):
    return pl.ds(pl.multiple_of(g * LANES, LANES), LANES)


def logit_block(k_ref, ok, t, g):
    block = k_ref[row_tile(t), lane_tile(g)]
    return jnp.where(ok, jnp.log(block), block)


def within(peak, *pots):
    for pot in pots:
        pot = jnp.abs(pot)
        for k in range(pot.shape[0] // 8):
            peak = jnp.maximum(peak, pot[8 * k : 8 * k + 8, :])
    return jnp.max(peak) <= LIM


def row_lse_exact(k_ref, ok, pot_ref, out_ref):
    tiles, groups = k_ref.shape[0] // LANES, k_ref.shape[1] // LANES

    def group(g, carry):
        def shifted(t):
            z = logit_block(k_ref, ok, t, g)
            return z if pot_ref is None else z + lane_to_sublane(pot_ref[pl.ds(t, 1), :])

        def top_of(t, top):
            return jnp.maximum(top, jnp.max(shifted(t), axis=0, keepdims=True))

        top = lax.fori_loop(0, tiles, top_of, jnp.full((1, LANES), -3.0e38, F32))

        def sum_of(t, total):
            return total + jnp.sum(jnp.exp(shifted(t) - top), axis=0, keepdims=True)

        total = lax.fori_loop(0, tiles, sum_of, jnp.zeros((1, LANES), F32))
        out_ref[pl.ds(g, 1), :] = top + jnp.log(total)
        return carry

    lax.fori_loop(0, groups, group, 0)


def col_lse_exact(k_ref, ok, pot_ref, out_ref):
    tiles, groups = k_ref.shape[0] // LANES, k_ref.shape[1] // LANES

    def tile(t, carry):
        def shifted(g):
            return logit_block(k_ref, ok, t, g) + pot_ref[pl.ds(g, 1), :]

        def top_of(g, top):
            return jnp.maximum(top, shifted(g))

        top = lax.fori_loop(0, groups, top_of, jnp.full((LANES, LANES), -3.0e38, F32))
        top = jnp.broadcast_to(jnp.max(top, axis=1, keepdims=True), (LANES, LANES))

        def sum_of(g, total):
            return total + jnp.exp(shifted(g) - top)

        total = lax.fori_loop(0, groups, sum_of, jnp.zeros((LANES, LANES), F32))
        total = jnp.sum(jnp.transpose(total), axis=0, keepdims=True)
        out_ref[pl.ds(t, 1), :] = jnp.transpose(top)[0:1, :] + jnp.log(total)
        return carry

    lax.fori_loop(0, tiles, tile, 0)


def logits_kernel(cent_hbm, vec_hbm, k_ref, peak_ref, out_ref, lse_ref, cent_ref, vec_ref, sems):
    cents, rows = k_ref.shape
    groups = rows // LANES
    step, chunk = cents // CHUNKS, rows // CHUNKS

    def pieces(hbm_ref, vmem_ref, first, size):
        return [
            pltpu.make_async_copy(
                hbm_ref.at[pl.ds(c * size, size), :], vmem_ref.at[pl.ds(c * size, size), :], sems.at[first + c]
            )
            for c in range(CHUNKS)
        ]

    vec_copies = pieces(vec_hbm, vec_ref, 0, chunk)
    cent_copies = pieces(cent_hbm, cent_ref, CHUNKS, step)
    for copy in vec_copies[:1] + cent_copies + vec_copies[1:]:
        copy.start()

    def dots(c):
        vec_copies[c].wait()
        if c == 0:
            for copy in cent_copies:
                copy.wait()
        return lax.dot_general(
            cent_ref[...], vec_ref[c * chunk : (c + 1) * chunk, :],
            (((1,), (1,)), ((), ())), preferred_element_type=F32,
        )

    peak = jnp.zeros((8, LANES), F32)
    ahead = dots(0)
    for c in range(CHUNKS):
        block = ahead
        if c + 1 < CHUNKS:
            ahead = dots(c + 1)
        for g in range(chunk // LANES):
            group = c * (chunk // LANES) + g
            total = jnp.zeros((8, LANES), F32)
            for t in range(cents // LANES):
                part = block[t * LANES : (t + 1) * LANES, lane_group(g)]
                peak = jnp.maximum(peak, jnp.max(jnp.abs(part).reshape(LANES // 8, 8, LANES), axis=0))
                part = jnp.exp2(part * (4.0 * LOG2E))
                k_ref[t * LANES : (t + 1) * LANES, lane_group(group)] = part
                total = total + fold(part)
            lse_ref[group : group + 1, :] = jnp.sum(total, axis=0, keepdims=True)
    peak = 4.0 * peak
    lse_ref[...] = jnp.log(lse_ref[...])
    peak_ref[...] = peak

    @pl.when(jnp.logical_not(within(peak)))
    def _():
        def tile(t, carry):
            def group(g, carry):
                k_ref[row_tile(t), lane_tile(g)] = 4.0 * lax.dot_general(
                    cent_ref[row_tile(t), :], vec_ref[row_tile(g), :],
                    (((1,), (1,)), ((), ())), preferred_element_type=F32,
                )
                return carry

            return lax.fori_loop(0, groups, group, carry)

        lax.fori_loop(0, cents // LANES, tile, 0)
        row_lse_exact(k_ref, False, None, lse_ref)

    put_copies(out_ref, lse_ref[...])


def row_kernel(log_target, got_ref, peak_ref, k_ref, out_ref, pot_ref, lse_ref):
    tiles, groups = k_ref.shape[0] // LANES, k_ref.shape[1] // LANES
    pot = log_target - combine_lse(got_ref[...])
    fast = within(peak_ref[...], pot)

    scales = jnp.exp(pot)
    sums = [jnp.zeros((8, LANES), F32)] * groups
    for t in range(tiles):
        scale = lane_to_sublane(scales[t : t + 1, :])
        for g in range(groups):
            sums[g] = sums[g] + fold(k_ref[t * LANES : (t + 1) * LANES, lane_group(g)] * scale)
    for g in range(groups):
        lse_ref[g : g + 1, :] = jnp.sum(sums[g], axis=0, keepdims=True)
    lse_ref[...] = jnp.log(lse_ref[...])

    @pl.when(jnp.logical_not(fast))
    def _():
        pot_ref[...] = pot
        row_lse_exact(k_ref, within(peak_ref[...]), pot_ref, lse_ref)

    put_copies(out_ref, lse_ref[...])


def col_kernel(got_ref, peak_ref, k_ref, out_ref, lse_ref, pot_ref):
    tiles, groups = k_ref.shape[0] // LANES, k_ref.shape[1] // LANES
    pot = -combine_lse(got_ref[...])
    fast = within(peak_ref[...], pot)

    scale = jnp.exp(pot)
    for t in range(tiles):
        total = jnp.zeros((LANES, LANES), F32)
        for g in range(groups):
            total = total + k_ref[t * LANES : (t + 1) * LANES, lane_group(g)] * scale[g : g + 1, :]
        lse_ref[t : t + 1, :] = jnp.sum(jnp.transpose(total), axis=0, keepdims=True)
    lse_ref[...] = jnp.log(lse_ref[...])

    @pl.when(jnp.logical_not(fast))
    def _():
        pot_ref[...] = pot
        col_lse_exact(k_ref, within(peak_ref[...]), pot_ref, lse_ref)

    put_copies(out_ref, lse_ref[...])


def sums_kernel(log_target, flips, *refs):
    first_call = log_target is not None
    cols_ref, rows_ref, peak_ref, k_ref, vec_ref, a_ref, b_ref = refs[:7]
    plan_ref, col_ref, row_ref = refs[-3:]
    groups = k_ref.shape[1] // LANES
    if first_call:
        col_pot = log_target - combine_lse(cols_ref[...])
        row_pot = -combine_lse(rows_ref[...])
        for pot_ref in refs[7:9]:
            pot_ref[...] = col_pot
        for pot_ref in refs[9:11]:
            pot_ref[...] = row_pot
    else:
        col_pot, row_pot = cols_ref[...], rows_ref[...]
    fast = within(peak_ref[...], col_pot, row_pot)
    col_ref[...] = jnp.exp(col_pot)
    row_scale = jnp.exp(row_pot)
    bits = position_bits()
    x1, z1 = bits[XB1], bits[ZB1]
    tiles = []
    for chain, (first, second) in enumerate(((x1, z1), (z1, x1))):
        first = 1 - first if flips[0] else first
        second = 1 - second if flips[1] else second
        tiles.append(chain * 4 + first * 2 + second)

    def put_mass(total, out_ref):
        mass = jnp.broadcast_to(jnp.sum(total, axis=1, keepdims=True), (LANES, LANES))
        lane = lax.broadcasted_iota(jnp.int32, (8, LANES), 1) // (LANES // PARTS)
        for b in range(LANES // BLOCK):
            unit = mass[b * BLOCK : b * BLOCK + 8, :]
            for k in range(1, PARTS):
                at = b * BLOCK + 8 * k
                unit = jnp.where(lane == k, mass[at : at + 8, :], unit)
            out_ref[b, out_ref.shape[1] - 1] = unit

    for chain, (tile, out_ref) in enumerate(zip(tiles, (a_ref, b_ref))):
        scale = lane_to_sublane(col_ref[pl.ds(tile, 1), :])
        total = jnp.zeros((LANES, LANES), F32)
        for g in range(groups):
            plan = k_ref[row_tile(tile), lane_group(g)] * row_scale[g : g + 1, :] * scale
            total = total + plan
            plan_ref[chain * LANES : (chain + 1) * LANES, lane_group(g)] = plan.astype(jnp.bfloat16)
        put_mass(total, out_ref)

    @pl.when(jnp.logical_not(fast))
    def _():
        ok = within(peak_ref[...])
        col_ref[...] = col_pot
        row_ref[...] = row_pot
        for chain, (tile, out_ref) in enumerate(zip(tiles, (a_ref, b_ref))):
            shift = lane_to_sublane(col_ref[pl.ds(tile, 1), :])

            def group(g, total):
                plan = jnp.exp(logit_block(k_ref, ok, tile, g) + row_ref[pl.ds(g, 1), :] + shift)
                plan_ref[chain * LANES : (chain + 1) * LANES, lane_tile(g)] = plan.astype(jnp.bfloat16)
                return total + plan

            put_mass(lax.fori_loop(0, groups, group, jnp.zeros((LANES, LANES), F32)), out_ref)

    block = jnp.dot(plan_ref[...], vec_ref[...], preferred_element_type=F32)
    across = block.shape[1] // LANES
    for chain, out_ref in enumerate((a_ref, b_ref)):
        for b in range(LANES // BLOCK):
            for k in range(PARTS):
                row = chain * LANES + b * BLOCK + 8 * k
                for g in range(across):
                    out_ref[b, k * across + g] = block[row : row + 8, lane_group(g)]


def add_kernel(mine_ref, got_ref, out_ref):
    out_ref[...] = mine_ref[...] + got_ref[...]


def spot(flips):
    bits = position_bits()
    x2, z2 = bits[XB2], bits[ZB2]
    return (1 - x2 if flips[0] else x2) * 2 + (1 - z2 if flips[1] else z2)


def pieces_kernel(order, mine_ref, first_ref, second_ref, send_ref, keep_ref):
    for n, flips in enumerate(order):
        at = spot(flips)
        out_ref = (send_ref, keep_ref)[n // 2]
        out_ref[n % 2] = mine_ref[at] + first_ref[at] + second_ref[at]


def own_kernel(keep_ref, got_ref, second_ref, out_ref):
    out_ref[...] = keep_ref[1] + got_ref[1] + second_ref[...]


def hold_kernel(keep_ref, got_ref, out_ref):
    out_ref[...] = keep_ref[0] + got_ref[0]


def mean_kernel(sum_ref, got_ref, out_ref):
    units = sum_ref.shape[0] - 1
    across = out_ref.shape[1] // LANES
    lanes = LANES // PARTS
    mass = sum_ref[units] + got_ref[units]
    for k in range(PARTS):
        part = jnp.broadcast_to(mass[:, k * lanes : k * lanes + 1], (8, LANES))
        for g in range(across):
            u = k * across + g
            out_ref[8 * k : 8 * k + 8, lane_group(g)] = (sum_ref[u] + got_ref[u]) / part


def join_kernel(order, *refs):
    out_ref = refs[-1]
    for flips, part_ref in zip(order, refs):
        at = pl.ds(pl.multiple_of(spot(flips) * BLOCK, BLOCK), BLOCK)
        out_ref[at, :] = part_ref[...]


def place_kernel(spots, *refs):
    out_ref, sems = refs[-2:]
    bits = position_bits()
    x1, z1 = bits[XB1], bits[ZB1]
    copies = []
    for n, ((chain, flips), part_ref) in enumerate(zip(spots, refs)):
        size = part_ref.shape[0]
        first, second = (z1, x1) if chain else (x1, z1)
        first = 1 - first if flips[0] else first
        second = 1 - second if flips[1] else second
        at = pl.ds(pl.multiple_of((chain * 4 + first * 2 + second) * size, size), size)
        copies.append(pltpu.make_async_copy(part_ref, out_ref.at[at, :], sems.at[n]))
    for copy in copies:
        copy.start()
    for copy in copies:
        copy.wait()


def place(row, core):
    return (row // ZS + (XS - 1) * core) % XS, (row % ZS + (ZS - 1) * core) % ZS


def pairs(partner, n_cols):
    out = []
    for row in range(XS * ZS):
        for col in range(n_cols):
            core = col % 2
            x, z = partner(*place(row, core))
            to = (x + core) % XS * ZS + (z + core) % ZS
            out.append((row * n_cols + col, to * n_cols + col))
    return out


def exchange(x, partner):
    return lax.ppermute(x, ("rows", "cols"), pairs(partner, lax.axis_size("cols")))


def x_first(x, z):
    return x ^ 1, z


def x_second(x, z):
    return XS - 1 - x, z


def z_first(x, z):
    return x, z ^ 1


def z_second(x, z):
    return x, (z - 1 + 2 * (z % 2)) % ZS


def z_third(x, z):
    return x, {0: 3, 3: 0, 1: 6, 6: 1, 2: 5, 5: 2, 4: 7, 7: 4}[z]


def position_bits():
    core = lax.axis_index("cols") & 1
    row = lax.axis_index("rows")
    x = ((row >> 3) + (XS - 1) * core) & (XS - 1)
    z = (row + (ZS - 1) * core) & (ZS - 1)
    return (x ^ (x >> 1)) & 1, x >> 1, ((z + 1) >> 1) & 1, (0xB4 >> z) & 1


def add(mine, got):
    return pl.pallas_call(
        add_kernel,
        out_shape=jax.ShapeDtypeStruct(mine.shape, F32),
        in_specs=[vmem(), vmem()],
        out_specs=vmem(),
        compiler_params=params(4),
        name="add",
    )(mine, got)


def put(spots, parts, cents, *before):
    return pl.pallas_call(
        functools.partial(place_kernel, spots),
        out_shape=jax.ShapeDtypeStruct((cents, parts[0].shape[1]), F32),
        in_specs=[vmem()] * len(parts) + [hbm()] * len(before),
        out_specs=hbm(),
        scratch_shapes=[pltpu.SemaphoreType.DMA((len(parts),))],
        input_output_aliases={len(parts): 0} if before else {},
        compiler_params=params(4),
        name="place",
    )(*parts, *before)


A_ORDER = ((True, True), (True, False), (False, True), (False, False))
B_ORDER = ((True, True), (False, True), (True, False), (False, False))


def sum_of_four(order, first, second, *terms):
    piece = jax.ShapeDtypeStruct(terms[0].shape[1:], F32)
    pair = jax.ShapeDtypeStruct((2, *terms[0].shape[1:]), F32)
    send, keep = pl.pallas_call(
        functools.partial(pieces_kernel, order),
        out_shape=(pair, pair),
        in_specs=[vmem()] * 3,
        out_specs=(vmem(), vmem()),
        compiler_params=params(4),
        name="pieces",
    )(*terms)
    got = exchange(send, first)
    hold = pl.pallas_call(
        hold_kernel,
        out_shape=piece,
        in_specs=[vmem()] * 2,
        out_specs=vmem(),
        compiler_params=params(4),
        name="hold",
    )(keep, got)
    return pl.pallas_call(
        own_kernel,
        out_shape=piece,
        in_specs=[vmem()] * 3,
        out_specs=vmem(),
        compiler_params=params(4),
        name="own",
    )(keep, got, exchange(hold, second))


def mean_of_four(order, first, second, mine, got, width):
    mean = pl.pallas_call(
        mean_kernel,
        out_shape=jax.ShapeDtypeStruct((BLOCK, width), F32),
        in_specs=[vmem()] * 2,
        out_specs=vmem(),
        compiler_params=params(4),
        name="mean",
    )(mine, got)
    hold, stay = exchange(mean, second), exchange(mean, first)
    away = exchange(hold, first)
    return pl.pallas_call(
        functools.partial(join_kernel, order),
        out_shape=jax.ShapeDtypeStruct((4 * BLOCK, width), F32),
        in_specs=[vmem()] * 4,
        out_specs=vmem(),
        compiler_params=params(4),
        name="join",
    )(away, stay, hold, mean)


def mean_over_rows(quarter_sums, cents, width):
    pass_a, pass_b = quarter_sums((True, True))
    pass_a, pass_b = exchange(pass_a, x_first), exchange(pass_b, z_first)
    stay_a, stay_b = quarter_sums((True, False))
    stay_a, stay_b = exchange(stay_a, x_first), exchange(stay_b, z_first)
    mine_a, mine_b = quarter_sums((False, True))
    next_a = exchange(add(mine_a, pass_a), z_first)
    next_b = exchange(add(mine_b, pass_b), x_first)
    mine_a, mine_b = quarter_sums((False, False))
    mine_a = sum_of_four(A_ORDER, x_second, z_second, mine_a, stay_a, next_a)
    mine_b = sum_of_four(B_ORDER, z_second, x_second, mine_b, stay_b, next_b)
    got_a, got_b = exchange(mine_a, z_third), exchange(mine_b, z_third)
    mine_a = mean_of_four(A_ORDER, x_second, z_second, mine_a, got_a, width)
    mine_b = mean_of_four(B_ORDER, z_second, x_second, mine_b, got_b, width)
    next_a, next_b = exchange(mine_a, z_first), exchange(mine_b, x_first)
    stay_a, stay_b = exchange(mine_a, x_first), exchange(mine_b, z_first)
    pass_a, pass_b = exchange(next_a, x_first), exchange(next_b, z_first)
    near = ((0, (False, False)), (1, (False, False)), (0, (False, True)), (1, (False, True)))
    out = put(near, (mine_a, mine_b, next_a, next_b), cents)
    out = put(((0, (True, False)), (1, (True, False))), (stay_a, stay_b), cents, out)
    return put(((0, (True, True)), (1, (True, True))), (pass_a, pass_b), cents, out)


def vmem():
    return pl.BlockSpec(memory_space=pltpu.VMEM)


def hbm():
    return pl.BlockSpec(memory_space=pltpu.HBM)


def pinned(x):
    return pltpu.with_memory_space_constraint(x, pltpu.VMEM)


def params(mib):
    return pltpu.CompilerParams(vmem_limit_bytes=mib * MIB)


def per_device(vectors, centroids):
    n_rows, n_cols = lax.axis_size("rows"), lax.axis_size("cols")
    rows, width = vectors.shape
    cents = centroids.shape[0]
    log_target = math.log(rows * n_rows / (cents * n_cols))
    groups, tiles = rows // LANES, cents // LANES
    kept = pltpu.VMEM((cents, rows), F32)
    peak_type = jax.ShapeDtypeStruct((8, LANES), F32)
    row_parts = jax.ShapeDtypeStruct((n_cols, groups, LANES), F32)
    col_parts = jax.ShapeDtypeStruct((n_rows, tiles, LANES), F32)
    row_scratch = pltpu.VMEM((groups, LANES), F32)
    col_scratch = pltpu.VMEM((tiles, LANES), F32)

    kernel, peak, part = pl.pallas_call(
        logits_kernel,
        out_shape=(kept, peak_type, row_parts),
        in_specs=[hbm(), hbm()],
        out_specs=(vmem(), vmem(), vmem()),
        scratch_shapes=[
            row_scratch,
            pltpu.VMEM((cents, width), jnp.bfloat16),
            pltpu.VMEM((rows, width), jnp.bfloat16),
            pltpu.SemaphoreType.DMA((2 * CHUNKS,)),
        ],
        compiler_params=params(24),
        name="logits",
    )(*(pltpu.with_memory_space_constraint(x, pltpu.HBM) for x in (centroids, vectors)))

    for step in range(ITERS):
        row_got = lax.all_to_all(part, "cols", 0, 0, tiled=True)
        part = pl.pallas_call(
            col_kernel,
            out_shape=col_parts,
            in_specs=[vmem(), vmem(), vmem()],
            out_specs=vmem(),
            scratch_shapes=[col_scratch, row_scratch],
            compiler_params=params(4),
            name="col_step",
        )(row_got, peak, pinned(kernel))
        col_got = lax.all_to_all(part, "rows", 0, 0, tiled=True)
        part = pl.pallas_call(
            functools.partial(row_kernel, log_target),
            out_shape=row_parts,
            in_specs=[vmem(), vmem(), vmem()],
            out_specs=vmem(),
            scratch_shapes=[col_scratch, row_scratch],
            compiler_params=params(4),
            name="row_step",
        )(col_got, peak, pinned(kernel))
    row_got = lax.all_to_all(part, "cols", 0, 0, tiled=True)

    quarter = jax.ShapeDtypeStruct((LANES // BLOCK, PARTS * (width // LANES) + 1, 8, LANES), F32)
    pots = []

    def quarter_sums(flips):
        first = not pots
        pot_types = tuple(jax.ShapeDtypeStruct((n, LANES), F32) for n in (tiles, tiles, groups, groups))
        a, b, *new = pl.pallas_call(
            functools.partial(sums_kernel, log_target if first else None, flips),
            out_shape=(quarter, quarter) + (pot_types if first else ()),
            in_specs=[vmem()] * 5,
            out_specs=(vmem(),) * (6 if first else 2),
            scratch_shapes=[pltpu.VMEM((2 * LANES, rows), jnp.bfloat16), col_scratch, row_scratch],
            compiler_params=params(8),
            cost_estimate=pl.CostEstimate(
                flops=rows * cents * width // 2, bytes_accessed=4 * MIB, transcendentals=0
            ),
            name="sums",
        )(*(pots[1::2] or (col_got, row_got)), peak, pinned(kernel), vectors)
        pots.extend(new)
        return a, b

    new_centroids = mean_over_rows(quarter_sums, cents, width)
    col_pot, row_pot = pots[0::2]
    return (new_centroids, row_pot.reshape(rows), col_pot.reshape(cents))


def solution(mesh):
    return jax.shard_map(
        per_device,
        mesh=mesh,
        in_specs=(P("rows", None), P("cols", None)),
        out_specs=(P("cols", None), P("rows"), P("cols")),
        check_vma=False,
    )
```
